512 devices in a mesh: leaf: 32 (over x, z), task: 16 (over y, core).
Axes of the slice: x: 4, y: 8, z: 8, core: 2. Of those that a mesh axis runs over, the one named last changes fastest.
Arguments:
- points: bfloat16 [2097152, 64], P(('leaf', 'task')), may hold values from -6 to 6
- weights: bfloat16 [2097152, 64], P(('leaf', 'task')), may hold values from -4 to 4
- point_order: int32 [32, 16, 4096], P('leaf', 'task'), may hold values from 0 to 4095, each once within a row
- node_order: int32 [32, 16, 4096], P('leaf', 'task'), may hold values from 0 to 4095, each once within a row
- merge_order: int32 [32, 16, 2, 1024], P('leaf', 'task'), may hold values from 0 to 1023, as said below
- far_list: int32 [32, 16, 4, 3], P('leaf', 'task'), may hold values 0 or 1
- task_target: int32 [32, 16, 16, 1], P('leaf', 'task'), may hold values from -1 to 3, as said below
- task_source: int32 [32, 16, 16, 1], P('leaf', 'task'), may hold values from 0 to 3
Outputs:
- potentials: float32 [2097152, 64], P(('leaf', 'task'))
The draws below stay inside these ranges and needn't reach their ends.
Inputs may be any that keep to these rules, and one draw needn't show every extreme that they name: `merge_order`: each row is a permutation of 0 to 1023; rows [i, j, b] are equal for all i with the same i // 2 ** (b + 1). `task_target`: -1 marks an empty slot; every device of every draw has a slab toward which all 1 slots are used.
All inputs are finite; a program needn't handle non-finite values. No bound on the sum of `far_list` on one device may be relied on, other than what follows from the above.
Results may differ from the reference program's by a relative error of at most 0.002.
Values may be sent and summed in bfloat16 or wider, within the bound.
No kernel may reach another device: no remote copies, remote signals or barrier semaphores. Data moves between devices by JAX's collectives and lax.ppermute only.
A program may use at most 64 MiB of HBM per device.

```python
import jax
import jax.numpy as jnp
from jax import lax

F = 64
C = 64
LEAF_PTS = 1024
SKEL = 512
LEVELS = 3
LEAF_DEV = 4
CAP = 1
PTS_DEV = 4096
MERGES = 2
REGIONS = 32
SLABS = 16
POINTS = 2097152


def draw_merge_order(key, part):
    base_key = jax.random.fold_in(key, 7)
    key_list = jax.random.split(base_key, REGIONS * SLABS * MERGES)
    shuffles = jax.vmap(lambda one_key: jax.random.permutation(one_key, 2 * SKEL))(key_list)
    shuffles = shuffles.reshape(REGIONS, SLABS, MERGES, 2 * SKEL)
    per_tier = []
    for tier_index in range(MERGES):
        stride_len = 2 ** (tier_index + 1)
        leaders = jnp.arange(REGIONS) // stride_len * stride_len
        per_tier.append(shuffles[leaders, :, tier_index, :])
    return jnp.stack(per_tier, axis=2).astype(jnp.int32)


def draw_task_target(key, part):
    busy_key, roll_key, leaf_key = jax.random.split(jax.random.fold_in(key, 11), 3)
    busyness = jax.random.randint(busy_key, (REGIONS, 1, SLABS, 1), 1, 5)
    rolled = jax.random.randint(roll_key, (REGIONS, SLABS, SLABS, CAP), 0, 4)
    chosen = jax.random.randint(leaf_key, (REGIONS, SLABS, SLABS, CAP), 0, LEAF_DEV)
    sender = jnp.arange(SLABS)[None, :, None, None]
    receiver = jnp.arange(SLABS)[None, None, :, None]
    forced = receiver == (sender + 1) % SLABS
    return jnp.where((rolled < busyness) | forced, chosen, -1).astype(jnp.int32)


def with_ends(array, rng, smallest, top_value):
    index_at = [jax.random.randint(jax.random.fold_in(rng, axis), (), 0, length) for axis, length in enumerate(array.shape)]
    main_axis = array.shape.index(max(array.shape))
    neighbour = index_at[:main_axis] + [(index_at[main_axis] + 1) % array.shape[main_axis]] + index_at[main_axis + 1:]
    return array.at[tuple(index_at)].set(smallest).at[tuple(neighbour)].set(top_value)


def steps_of(own_key, shape, cuts, low, top_value):
    def one(position, parts):
        draws = jax.random.uniform(jax.random.fold_in(jax.random.fold_in(own_key, 6), position), (parts,), jnp.float32, low / len(cuts), top_value / len(cuts))
        return jnp.repeat(jnp.exp(draws), shape[position] // parts).reshape((-1,) + (1,) * (len(shape) - position - 1))

    factor_of = one(*cuts[0])
    for cut in cuts[1:]:
        factor_of = factor_of * one(*cut)
    return factor_of


def noise(stream_key, extent, width, most, cuts=(), held_as=jnp.bfloat16):
    values = jax.random.normal(stream_key, extent, jnp.float32) * width
    if len(cuts) > 0:
        values = steps_of(stream_key, extent, cuts, -0.22, 0.18) * values
    return jnp.clip(values, min=-most, max=most).astype(held_as)


def setup_inputs(seed: int = 0) -> dict:
    key_of = jax.random.split(jax.random.key(seed), 9)
    return {
        "points": noise(key_of[0], (POINTS, F), 1.0, 6.0, ((0, 512),)),
        "weights": noise(key_of[1], (POINTS, C), 0.5, 4.0, ((0, 512),)),
        "point_order": jax.vmap(lambda own: jax.random.permutation(own, PTS_DEV))(jax.random.split(key_of[2], REGIONS * SLABS)).reshape((REGIONS, SLABS, PTS_DEV)).astype(jnp.int32),
        "node_order": jax.vmap(lambda own: jax.random.permutation(own, PTS_DEV))(jax.random.split(key_of[3], REGIONS * SLABS)).reshape((REGIONS, SLABS, PTS_DEV)).astype(jnp.int32),
        "merge_order": draw_merge_order(jax.random.fold_in(key_of[8], 71), 0),
        "far_list": with_ends((jax.random.randint(key_of[5], (REGIONS, SLABS, LEAF_DEV, LEVELS), 0, 4) < 3).astype(jnp.int32), jax.random.fold_in(key_of[5], 1), 0, 1),
        "task_target": draw_task_target(jax.random.fold_in(key_of[8], 71), 0),
        "task_source": with_ends(jax.random.randint(key_of[7], (REGIONS, SLABS, SLABS, CAP), 0, LEAF_DEV), jax.random.fold_in(key_of[7], 1), 0, LEAF_DEV - 1).astype(jnp.int32),
    }


KERNEL_SCALE = 1.5


def kernel(left_pts, right_pts):
    cross_term = jnp.dot(left_pts, right_pts.T, preferred_element_type=jnp.float32)
    left_norm = jnp.sum(jnp.square(left_pts.astype(jnp.float32)), axis=1)
    right_norm = jnp.sum(jnp.square(right_pts.astype(jnp.float32)), axis=1)
    distance = left_norm[:, None] + right_norm[None, :] - 2.0 * cross_term
    return jnp.exp((-KERNEL_SCALE / left_pts.shape[1]) * distance)


def anterpolate(skel_x, rest_x, skel_w, rest_w):
    dense = kernel(skel_x, rest_x)
    spread = (dense / jnp.sum(dense, axis=0, keepdims=True)).astype(jnp.bfloat16)
    summed = skel_w.astype(jnp.float32) + jnp.dot(spread, rest_w, preferred_element_type=jnp.float32)
    return summed.astype(jnp.bfloat16)


def merge_node(payload):
    picked_x, picked_w = payload
    return picked_x[:SKEL], anterpolate(picked_x[:SKEL], picked_x[SKEL:], picked_w[:SKEL], picked_w[SKEL:])


def level_zero(payload):
    tree_x, tree_w, node_pick = payload
    return merge_node((tree_x[node_pick], tree_w[node_pick]))


def reference(points, weights, point_order, node_order, merge_order, far_list, task_target, task_source):
    features = points.shape[1]
    columns = weights.shape[1]
    devices = REGIONS * SLABS
    block_x = points.reshape(devices, PTS_DEV, features)
    block_w = weights.reshape(devices, PTS_DEV, columns)
    tree_order = point_order.reshape(devices, PTS_DEV)
    tree_x = jax.vmap(lambda rows_x, picks: rows_x[picks])(block_x, tree_order)
    tree_w = jax.vmap(lambda rows_w, picks: rows_w[picks])(block_w, tree_order)
    node_x, node_w = lax.map(level_zero, (tree_x, tree_w, node_order.reshape(devices, PTS_DEV)))
    node_x = node_x.reshape(REGIONS, SLABS, SKEL, features)
    node_w = node_w.reshape(REGIONS, SLABS, SKEL, columns)
    region = jnp.arange(REGIONS)
    sibling_x = []
    sibling_w = []
    for level_index in range(LEVELS):
        partner = region ^ (1 << level_index)
        other_x = node_x[partner]
        other_w = node_w[partner]
        sibling_x.append(other_x)
        sibling_w.append(other_w)
        if level_index < LEVELS - 1:
            upper = (((region >> level_index) & 1) == 1)[:, None, None, None]
            cat_x = jnp.concatenate([jnp.where(upper, other_x, node_x), jnp.where(upper, node_x, other_x)], axis=2)
            cat_w = jnp.concatenate([jnp.where(upper, other_w, node_w), jnp.where(upper, node_w, other_w)], axis=2)
            merge_rows = merge_order[:, :, level_index, :]
            picked_x = jnp.take_along_axis(cat_x, merge_rows[..., None], axis=2)
            picked_w = jnp.take_along_axis(cat_w, merge_rows[..., None], axis=2)
            new_x, new_w = lax.map(merge_node, (picked_x.reshape(devices, 2 * SKEL, features), picked_w.reshape(devices, 2 * SKEL, columns)))
            node_x = new_x.reshape(REGIONS, SLABS, SKEL, features)
            node_w = new_w.reshape(REGIONS, SLABS, SKEL, columns)
    stack_x = jnp.stack(sibling_x, axis=2).reshape(devices, LEVELS, SKEL, features)
    stack_w = jnp.stack(sibling_w, axis=2).reshape(devices, LEVELS, SKEL, columns)
    leaves_x = tree_x.reshape(REGIONS, SLABS, LEAF_DEV, LEAF_PTS, features)
    leaves_w = tree_w.reshape(REGIONS, SLABS, LEAF_DEV, LEAF_PTS, columns)
    far_flags = far_list.reshape(devices, LEAF_DEV, LEVELS)
    targets_all = task_target.reshape(devices, SLABS, CAP)
    sources_all = task_source.reshape(devices, SLABS, CAP)

    def pair_terms(payload):
        target_x, source_x, source_w = payload

        def single(one_t, one_s, one_w):
            return jnp.dot(kernel(one_t, one_s).astype(jnp.bfloat16), one_w, preferred_element_type=jnp.float32)

        return jax.vmap(single)(target_x, source_x, source_w)

    def device_sum(device):
        region_index = device // SLABS
        slab_index = device % SLABS
        own_x = tree_x[device]
        far_field = jnp.zeros((LEAF_DEV, LEAF_PTS, columns), jnp.float32)
        for level_index in range(LEVELS):
            dense = kernel(own_x, stack_x[device, level_index]).astype(jnp.bfloat16)
            far_part = jnp.dot(dense, stack_w[device, level_index], preferred_element_type=jnp.float32)
            flags = far_flags[device, :, level_index].astype(jnp.float32)
            far_field = far_field + far_part.reshape(LEAF_DEV, LEAF_PTS, columns) * flags[:, None, None]
        target = targets_all[device]
        source = sources_all[device]
        is_live = target >= 0
        slot_leaf = jnp.maximum(target, 0)
        own_leaves = leaves_x[region_index, slab_index]
        peer_rows = jnp.arange(SLABS)[:, None]
        chosen_x = leaves_x[region_index][peer_rows, source]
        chosen_w = leaves_w[region_index][peer_rows, source]
        slot_terms = lax.map(pair_terms, (own_leaves[slot_leaf], chosen_x, chosen_w))
        onehot = ((slot_leaf[..., None] == jnp.arange(LEAF_DEV)[None, None, :]) & is_live[..., None]).astype(jnp.float32)
        near_field = jnp.einsum('pcl,pcte->lte', onehot, slot_terms, precision=lax.Precision.HIGHEST)
        return (far_field + near_field).reshape(PTS_DEV, columns)

    result = lax.map(device_sum, jnp.arange(devices))
    return result.reshape(POINTS, columns)
```

```python
import functools
import math

import jax
import jax.numpy as jnp
from jax import lax
from jax.experimental import pallas as pl
from jax.experimental.pallas import tpu as pltpu
from jax.sharding import PartitionSpec as P

LEAF_PTS = 1024
SKEL = 512
LEVELS = 3
LEAF_DEV = 4
F = 64
PTS = LEAF_PTS * LEAF_DEV
RATE = 1.5 / 64 * math.log2(math.e)
VMEM = pl.BlockSpec(memory_space=pltpu.VMEM)
SMEM = pl.BlockSpec(memory_space=pltpu.SMEM)
PARAMS = pltpu.CompilerParams(vmem_limit_bytes=40 * 2**20)


def split3(value):
    one = value.astype(jnp.bfloat16).astype(jnp.float32)
    rest = value - one
    two = rest.astype(jnp.bfloat16).astype(jnp.float32)
    return one, two, rest - two


def gather_rows(src_ref, index_ref, dst_ref, count, unroll=16):
    def step(i, _):
        for k in range(unroll):
            at = i * unroll + k
            dst_ref[pl.ds(at, 1), :] = src_ref[pl.ds(index_ref[at], 1), :]
        return 0

    lax.fori_loop(0, count // unroll, step, 0)


def sort_kernel(order_ref, points_ref, weights_ref, out_ref, raw, tree):
    for c in range(8):
        cols = pl.ds(c * 512, 512)
        block = jnp.concatenate([points_ref[:, cols], weights_ref[:, cols]], axis=0)
        raw[pl.ds(c * 512, 512), :] = block.astype(jnp.float32).T
    gather_rows(raw, order_ref, tree, PTS)
    for leaf in range(LEAF_DEV):
        rows = tree[pl.ds(leaf * LEAF_PTS, LEAF_PTS), :]
        out_ref[leaf] = rows.T.astype(jnp.bfloat16)


def sort_leaves(order, points_t, weights_t):
    return pl.pallas_call(
        sort_kernel,
        out_shape=jax.ShapeDtypeStruct((LEAF_DEV, 2 * F, LEAF_PTS), jnp.bfloat16),
        in_specs=[SMEM, VMEM, VMEM],
        out_specs=VMEM,
        scratch_shapes=[pltpu.VMEM((PTS, 2 * F), jnp.float32), pltpu.VMEM((PTS, 2 * F), jnp.float32)],
        compiler_params=PARAMS,
        name="sort_leaves",
        cost_estimate=pl.CostEstimate(flops=0, bytes_accessed=25 * 10**6, transcendentals=0),
    )(order, points_t, weights_t)


def left_factor(rows, with_ones):
    lane = lax.broadcasted_iota(jnp.int32, rows.shape, 1)
    is_point = lane < F
    scaled = jnp.where(is_point, rows * (2 * RATE), 0.0)
    high = scaled.astype(jnp.bfloat16)
    low = scaled - high.astype(jnp.float32)
    norm = -RATE * jnp.sum(jnp.where(is_point, rows * rows, 0.0), axis=1, keepdims=True)
    one, two, three = split3(norm)
    tail = jnp.where(lane == F, one, 0.0)
    tail = jnp.where(lane == F + 1, two, tail)
    tail = jnp.where(lane == F + 2, three, tail)
    if with_ones:
        tail = jnp.where((lane > F + 2) & (lane < F + 6), 1.0, tail)
    second = jnp.where(is_point, low, tail).astype(jnp.bfloat16)
    return jnp.concatenate([high, second], axis=1)


def fill_right(right, block):
    size = block.shape[1]
    points = block[:F]
    wide = points.astype(jnp.float32)
    norm = -RATE * jnp.sum(wide * wide, axis=0, keepdims=True)
    one, two, three = split3(norm)
    row = lax.broadcasted_iota(jnp.int32, (16, size), 0)
    tail = jnp.where(row < 3, 1.0, 0.0)
    tail = jnp.where(row == 3, one, tail)
    tail = jnp.where(row == 4, two, tail)
    tail = jnp.where(row == 5, three, tail)
    right[pl.ds(0, 2 * F), :] = block
    right[pl.ds(2 * F, F), :] = points
    right[pl.ds(3 * F, 16), :] = tail.astype(jnp.bfloat16)
    right[pl.ds(3 * F + 16, F - 16), :] = jnp.zeros((F - 16, size), jnp.bfloat16)


def targets_kernel(leaves_ref, out_ref):
    for leaf in range(LEAF_DEV):
        for half in range(2):
            rows = leaves_ref[leaf, :, pl.ds(half * 512, 512)].astype(jnp.float32).T
            out_ref[pl.ds(leaf * LEAF_PTS + half * 512, 512), :] = left_factor(rows, True)


def target_factors(leaves):
    return pl.pallas_call(
        targets_kernel,
        out_shape=jax.ShapeDtypeStruct((PTS, 4 * F), jnp.bfloat16),
        in_specs=[VMEM],
        out_specs=VMEM,
        compiler_params=PARAMS,
        name="target_factors",
        cost_estimate=pl.CostEstimate(flops=0, bytes_accessed=8 * 10**6, transcendentals=0),
    )(leaves)


def skeleton(index_ref, rows, blocks, chosen, zero, right, total):
    gather_rows(rows, index_ref, chosen, SKEL)
    blank = jnp.zeros((1, 2 * F), jnp.float32)

    def wipe(i, _):
        for k in range(16):
            rows[pl.ds(index_ref[i * 16 + k], 1), :] = blank
        return 0

    lax.fori_loop(0, SKEL // 16, wipe, 0)
    left = left_factor(chosen[...], False)
    total[...] = chosen[...]
    lane = lax.broadcasted_iota(jnp.int32, (SKEL, 2 * F), 1)
    at = 0
    for block in blocks:
        block = block()
        size = block.shape[1]
        fill_right(right, block)
        exponent = jnp.dot(left, right[...], preferred_element_type=jnp.float32)
        dense = jnp.exp2(exponent)
        spread = (dense * (1.0 / jnp.sum(dense, axis=0, keepdims=True))).astype(jnp.bfloat16)
        rest = rows[pl.ds(at, size), :].astype(jnp.bfloat16)
        part = jnp.dot(spread, rest, preferred_element_type=jnp.float32)
        total[...] += jnp.where(lane < F, 0.0, part)
        at += size


def node_kernel(index_ref, leaves_ref, out_ref, rows, chosen, right, total):
    for leaf in range(LEAF_DEV):
        for half in range(2):
            part = leaves_ref[leaf, :, pl.ds(half * 512, 512)].astype(jnp.float32).T
            rows[pl.ds(leaf * LEAF_PTS + half * 512, 512), :] = part
    blocks = [
        functools.partial(lambda leaf, half: leaves_ref[leaf, :, pl.ds(half * 512, 512)], leaf, half)
        for leaf in range(LEAF_DEV)
        for half in range(2)
    ]
    skeleton(index_ref, rows, blocks, chosen, None, right, total)
    out_ref[...] = total[...].T.astype(jnp.bfloat16)


def first_node(index, leaves):
    return pl.pallas_call(
        node_kernel,
        out_shape=jax.ShapeDtypeStruct((2 * F, SKEL), jnp.bfloat16),
        in_specs=[SMEM, VMEM],
        out_specs=VMEM,
        scratch_shapes=[
            pltpu.VMEM((PTS, 2 * F), jnp.float32),
            pltpu.VMEM((SKEL, 2 * F), jnp.float32),
            pltpu.VMEM((4 * F, 512), jnp.bfloat16),
            pltpu.VMEM((SKEL, 2 * F), jnp.float32),
        ],
        compiler_params=PARAMS,
        name="first_node",
        cost_estimate=pl.CostEstimate(flops=0, bytes_accessed=20 * 10**6, transcendentals=0),
    )(index, leaves)


def merge_kernel(upper_ref, index_ref, node_ref, other_ref, out_ref, rows, chosen, right, total):
    upper = upper_ref[0]
    mine = pl.multiple_of(upper * SKEL, SKEL)
    others = pl.multiple_of((1 - upper) * SKEL, SKEL)
    rows[pl.ds(mine, SKEL), :] = node_ref[...].astype(jnp.float32).T
    rows[pl.ds(others, SKEL), :] = other_ref[...].astype(jnp.float32).T
    first = lambda: jnp.where(upper == 1, other_ref[...].astype(jnp.float32), node_ref[...].astype(jnp.float32)).astype(jnp.bfloat16)
    second = lambda: jnp.where(upper == 1, node_ref[...].astype(jnp.float32), other_ref[...].astype(jnp.float32)).astype(jnp.bfloat16)
    skeleton(index_ref, rows, [first, second], chosen, None, right, total)
    out_ref[...] = total[...].T.astype(jnp.bfloat16)


def merge_nodes(upper, index, node, other):
    return pl.pallas_call(
        merge_kernel,
        out_shape=jax.ShapeDtypeStruct((2 * F, SKEL), jnp.bfloat16),
        in_specs=[SMEM, SMEM, VMEM, VMEM],
        out_specs=VMEM,
        scratch_shapes=[
            pltpu.VMEM((2 * SKEL, 2 * F), jnp.float32),
            pltpu.VMEM((SKEL, 2 * F), jnp.float32),
            pltpu.VMEM((4 * F, 512), jnp.bfloat16),
            pltpu.VMEM((SKEL, 2 * F), jnp.float32),
        ],
        compiler_params=PARAMS,
        name="merge_nodes",
        cost_estimate=pl.CostEstimate(flops=0, bytes_accessed=8 * 10**6, transcendentals=0),
    )(upper, index, node, other)


def add_terms(target, block, left_ref, total, right):
    fill_right(right, block)
    weights = block
    base = pl.multiple_of(target * LEAF_PTS, LEAF_PTS)
    for step in range(LEAF_PTS // 256):
        rows = pl.ds(base + step * 256, 256)
        exponent = jnp.dot(left_ref[rows, :], right[...], preferred_element_type=jnp.float32)
        dense = jnp.exp2(exponent).astype(jnp.bfloat16)
        total[rows, :] += lax.dot_general(
            dense, weights, (((1,), (1,)), ((), ())), preferred_element_type=jnp.float32
        )


def near_kernel(target_ref, left_ref, before_ref, block_ref, out_ref, total, right):
    slot = pl.program_id(0)

    @pl.when(slot == 0)
    def _():
        total[...] = before_ref[...]

    target = target_ref[slot]

    @pl.when(target >= 0)
    def _():
        add_terms(target, block_ref[0], left_ref, total, right)

    @pl.when(slot == pl.num_programs(0) - 1)
    def _():
        out_ref[...] = total[...]


def near_terms(target, left, before, blocks):
    count = blocks.shape[0]
    return pl.pallas_call(
        near_kernel,
        out_shape=jax.ShapeDtypeStruct((PTS, 2 * F), jnp.float32),
        grid=(count,),
        in_specs=[SMEM, VMEM, VMEM, pl.BlockSpec((1, 2 * F, LEAF_PTS), lambda i: (i, 0, 0))],
        out_specs=VMEM,
        scratch_shapes=[pltpu.VMEM((PTS, 2 * F), jnp.float32), pltpu.VMEM((4 * F, LEAF_PTS), jnp.bfloat16)],
        compiler_params=PARAMS,
        name="near_terms",
        cost_estimate=pl.CostEstimate(flops=count * 10**9, bytes_accessed=8 * 10**6, transcendentals=0),
    )(target, left, before, blocks)


def far_kernel(flags_ref, left_ref, *refs):
    *siblings, out_ref, right = refs
    out_ref[...] = jnp.zeros_like(out_ref)
    for level, sibling in enumerate(siblings):
        block = sibling[...]
        fill_right(right, block)

        def leaf_step(leaf, _):
            @pl.when(flags_ref[leaf * LEVELS + level] != 0)
            def _():
                base = pl.multiple_of(leaf * LEAF_PTS, LEAF_PTS)
                for step in range(2):
                    rows = pl.ds(base + step * 512, 512)
                    exponent = jnp.dot(left_ref[rows, :], right[...], preferred_element_type=jnp.float32)
                    dense = jnp.exp2(exponent).astype(jnp.bfloat16)
                    out_ref[rows, :] += lax.dot_general(
                        dense, block, (((1,), (1,)), ((), ())), preferred_element_type=jnp.float32
                    )
            return 0

        lax.fori_loop(0, LEAF_DEV, leaf_step, 0)


def far_terms(flags, left, siblings):
    return pl.pallas_call(
        far_kernel,
        out_shape=jax.ShapeDtypeStruct((PTS, 2 * F), jnp.float32),
        in_specs=[SMEM, VMEM] + [VMEM] * LEVELS,
        out_specs=VMEM,
        scratch_shapes=[pltpu.VMEM((4 * F, SKEL), jnp.bfloat16)],
        compiler_params=PARAMS,
        name="far_terms",
        cost_estimate=pl.CostEstimate(flops=6 * 10**9, bytes_accessed=8 * 10**6, transcendentals=0),
    )(flags, left, *siblings)


def pick_kernel(pick_ref, leaf_ref, out_ref):
    out_ref[...] = leaf_ref[...]


def pick_leaves(pick, leaves):
    return pl.pallas_call(
        pick_kernel,
        out_shape=jax.ShapeDtypeStruct((pick.shape[0],) + leaves.shape[1:], leaves.dtype),
        grid_spec=pltpu.PrefetchScalarGridSpec(
            num_scalar_prefetch=1,
            grid=(pick.shape[0],),
            in_specs=[pl.BlockSpec((1, 2 * F, LEAF_PTS), lambda i, pick: (pick[i], 0, 0))],
            out_specs=pl.BlockSpec((1, 2 * F, LEAF_PTS), lambda i, pick: (i, 0, 0)),
        ),
        name="pick_leaves",
    )(pick, leaves)


def partner(value, axis, stride):
    pairs = [(source, source ^ 2**stride) for source in range(lax.axis_size(axis))]
    return lax.ppermute(value, axis, pairs)


def body(points, weights, point_order, node_order, merge_order, far_list, task_target, task_source):
    leaves = sort_leaves(point_order.reshape(-1), points.T, weights.T)
    requested = lax.all_to_all(task_source[0, 0], "task", split_axis=0, concat_axis=0, tiled=True)
    picked = pick_leaves(requested.reshape(-1), leaves)
    arrived = lax.all_to_all(picked, "task", split_axis=0, concat_axis=0, tiled=True)
    position = lax.axis_index("leaf")
    node = first_node(node_order.reshape(-1)[:SKEL], leaves)
    left = target_factors(leaves)
    siblings = []
    for level in range(LEVELS):
        other = partner(node, "leaf", level)
        siblings.append(other)
        if level < LEVELS - 1:
            upper = ((position >> level) & 1).astype(jnp.int32).reshape(1)
            node = merge_nodes(upper, merge_order[0, 0, level], node, other)
    far = far_terms(far_list.reshape(-1), left, siblings)
    total = near_terms(task_target.reshape(-1), left, far, arrived)
    return total[:, F:]


def solution(mesh):
    return jax.shard_map(
        body,
        mesh=mesh,
        in_specs=(
            P(("leaf", "task"), None),
            P(("leaf", "task"), None),
            P("leaf", "task", None),
            P("leaf", "task", None),
            P("leaf", "task", None, None),
            P("leaf", "task", None, None),
            P("leaf", "task", None, None),
            P("leaf", "task", None, None),
        ),
        out_specs=P(("leaf", "task"), None),
        check_vma=False,
    )
```

```python
import functools
import math

import jax
import jax.numpy as jnp
from jax import lax
from jax.experimental import pallas as pl
from jax.experimental.pallas import tpu as pltpu
from jax.sharding import PartitionSpec as P

LEAF_PTS = 1024
SKEL = 512
LEVELS = 3
LEAF_DEV = 4
F = 64
PTS = LEAF_PTS * LEAF_DEV
RATE = 1.5 / 64 * math.log2(math.e)
VMEM = pl.BlockSpec(memory_space=pltpu.VMEM)
SMEM = pl.BlockSpec(memory_space=pltpu.SMEM)
PARAMS = pltpu.CompilerParams(vmem_limit_bytes=40 * 2**20)


def split3(value):
    one = value.astype(jnp.bfloat16).astype(jnp.float32)
    rest = value - one
    two = rest.astype(jnp.bfloat16).astype(jnp.float32)
    return one, two, rest - two


def gather_rows(src_ref, index_ref, dst_ref, count, unroll=16):
    def step(i, _):
        for k in range(unroll):
            at = i * unroll + k
            dst_ref[pl.ds(at, 1), :] = src_ref[pl.ds(index_ref[at], 1), :]
        return 0

    lax.fori_loop(0, count // unroll, step, 0)


def sort_kernel(order_ref, points_ref, weights_ref, out_ref, raw, tree):
    for c in range(8):
        cols = pl.ds(c * 512, 512)
        block = jnp.concatenate([points_ref[:, cols], weights_ref[:, cols]], axis=0)
        raw[pl.ds(c * 512, 512), :] = block.astype(jnp.float32).T
    gather_rows(raw, order_ref, tree, PTS)
    for leaf in range(LEAF_DEV):
        rows = tree[pl.ds(leaf * LEAF_PTS, LEAF_PTS), :]
        out_ref[leaf] = rows.T.astype(jnp.bfloat16)


def sort_leaves(order, points_t, weights_t):
    return pl.pallas_call(
        sort_kernel,
        out_shape=jax.ShapeDtypeStruct((LEAF_DEV, 2 * F, LEAF_PTS), jnp.bfloat16),
        in_specs=[SMEM, VMEM, VMEM],
        out_specs=VMEM,
        scratch_shapes=[pltpu.VMEM((PTS, 2 * F), jnp.float32), pltpu.VMEM((PTS, 2 * F), jnp.float32)],
        compiler_params=PARAMS,
        name="sort_leaves",
        cost_estimate=pl.CostEstimate(flops=0, bytes_accessed=25 * 10**6, transcendentals=0),
    )(order, points_t, weights_t)


def left_factor(rows, with_ones):
    lane = lax.broadcasted_iota(jnp.int32, rows.shape, 1)
    is_point = lane < F
    scaled = jnp.where(is_point, rows * (2 * RATE), 0.0)
    high = scaled.astype(jnp.bfloat16)
    low = scaled - high.astype(jnp.float32)
    norm = -RATE * jnp.sum(jnp.where(is_point, rows * rows, 0.0), axis=1, keepdims=True)
    one, two, three = split3(norm)
    tail = jnp.where(lane == F, one, 0.0)
    tail = jnp.where(lane == F + 1, two, tail)
    tail = jnp.where(lane == F + 2, three, tail)
    if with_ones:
        tail = jnp.where((lane > F + 2) & (lane < F + 6), 1.0, tail)
    second = jnp.where(is_point, low, tail).astype(jnp.bfloat16)
    return jnp.concatenate([high, second], axis=1)


def fill_right(right, block):
    size = block.shape[1]
    points = block[:F]
    wide = points.astype(jnp.float32)
    norm = -RATE * jnp.sum(wide * wide, axis=0, keepdims=True)
    one, two, three = split3(norm)
    row = lax.broadcasted_iota(jnp.int32, (16, size), 0)
    tail = jnp.where(row < 3, 1.0, 0.0)
    tail = jnp.where(row == 3, one, tail)
    tail = jnp.where(row == 4, two, tail)
    tail = jnp.where(row == 5, three, tail)
    right[pl.ds(0, 2 * F), :] = block
    right[pl.ds(2 * F, F), :] = points
    right[pl.ds(3 * F, 16), :] = tail.astype(jnp.bfloat16)
    right[pl.ds(3 * F + 16, F - 16), :] = jnp.zeros((F - 16, size), jnp.bfloat16)


def targets_kernel(leaves_ref, out_ref):
    for leaf in range(LEAF_DEV):
        for half in range(2):
            rows = leaves_ref[leaf, :, pl.ds(half * 512, 512)].astype(jnp.float32).T
            out_ref[pl.ds(leaf * LEAF_PTS + half * 512, 512), :] = left_factor(rows, True)


def target_factors(leaves):
    return pl.pallas_call(
        targets_kernel,
        out_shape=jax.ShapeDtypeStruct((PTS, 4 * F), jnp.bfloat16),
        in_specs=[VMEM],
        out_specs=VMEM,
        compiler_params=PARAMS,
        name="target_factors",
        cost_estimate=pl.CostEstimate(flops=0, bytes_accessed=8 * 10**6, transcendentals=0),
    )(leaves)


def skeleton(index_ref, rows, blocks, chosen, zero, right, total):
    gather_rows(rows, index_ref, chosen, SKEL)
    blank = jnp.zeros((1, 2 * F), jnp.float32)

    def wipe(i, _):
        for k in range(16):
            rows[pl.ds(index_ref[i * 16 + k], 1), :] = blank
        return 0

    lax.fori_loop(0, SKEL // 16, wipe, 0)
    left = left_factor(chosen[...], False)
    total[...] = chosen[...]
    lane = lax.broadcasted_iota(jnp.int32, (SKEL, 2 * F), 1)
    at = 0
    for block in blocks:
        block = block()
        size = block.shape[1]
        fill_right(right, block)
        exponent = jnp.dot(left, right[...], preferred_element_type=jnp.float32)
        dense = jnp.exp2(exponent)
        spread = (dense * (1.0 / jnp.sum(dense, axis=0, keepdims=True))).astype(jnp.bfloat16)
        rest = rows[pl.ds(at, size), :].astype(jnp.bfloat16)
        part = jnp.dot(spread, rest, preferred_element_type=jnp.float32)
        total[...] += jnp.where(lane < F, 0.0, part)
        at += size


def node_kernel(index_ref, leaves_ref, out_ref, rows, chosen, right, total):
    for leaf in range(LEAF_DEV):
        for half in range(2):
            part = leaves_ref[leaf, :, pl.ds(half * 512, 512)].astype(jnp.float32).T
            rows[pl.ds(leaf * LEAF_PTS + half * 512, 512), :] = part
    blocks = [
        functools.partial(lambda leaf, half: leaves_ref[leaf, :, pl.ds(half * 512, 512)], leaf, half)
        for leaf in range(LEAF_DEV)
        for half in range(2)
    ]
    skeleton(index_ref, rows, blocks, chosen, None, right, total)
    out_ref[...] = total[...].T.astype(jnp.bfloat16)


def first_node(index, leaves):
    return pl.pallas_call(
        node_kernel,
        out_shape=jax.ShapeDtypeStruct((2 * F, SKEL), jnp.bfloat16),
        in_specs=[SMEM, VMEM],
        out_specs=VMEM,
        scratch_shapes=[
            pltpu.VMEM((PTS, 2 * F), jnp.float32),
            pltpu.VMEM((SKEL, 2 * F), jnp.float32),
            pltpu.VMEM((4 * F, 512), jnp.bfloat16),
            pltpu.VMEM((SKEL, 2 * F), jnp.float32),
        ],
        compiler_params=PARAMS,
        name="first_node",
        cost_estimate=pl.CostEstimate(flops=0, bytes_accessed=20 * 10**6, transcendentals=0),
    )(index, leaves)


def merge_kernel(upper_ref, index_ref, node_ref, other_ref, out_ref, rows, chosen, right, total):
    upper = upper_ref[0]
    mine = pl.multiple_of(upper * SKEL, SKEL)
    others = pl.multiple_of((1 - upper) * SKEL, SKEL)
    rows[pl.ds(mine, SKEL), :] = node_ref[...].astype(jnp.float32).T
    rows[pl.ds(others, SKEL), :] = other_ref[...].astype(jnp.float32).T
    first = lambda: jnp.where(upper == 1, other_ref[...].astype(jnp.float32), node_ref[...].astype(jnp.float32)).astype(jnp.bfloat16)
    second = lambda: jnp.where(upper == 1, node_ref[...].astype(jnp.float32), other_ref[...].astype(jnp.float32)).astype(jnp.bfloat16)
    skeleton(index_ref, rows, [first, second], chosen, None, right, total)
    out_ref[...] = total[...].T.astype(jnp.bfloat16)


def merge_nodes(upper, index, node, other):
    return pl.pallas_call(
        merge_kernel,
        out_shape=jax.ShapeDtypeStruct((2 * F, SKEL), jnp.bfloat16),
        in_specs=[SMEM, SMEM, VMEM, VMEM],
        out_specs=VMEM,
        scratch_shapes=[
            pltpu.VMEM((2 * SKEL, 2 * F), jnp.float32),
            pltpu.VMEM((SKEL, 2 * F), jnp.float32),
            pltpu.VMEM((4 * F, 512), jnp.bfloat16),
            pltpu.VMEM((SKEL, 2 * F), jnp.float32),
        ],
        compiler_params=PARAMS,
        name="merge_nodes",
        cost_estimate=pl.CostEstimate(flops=0, bytes_accessed=8 * 10**6, transcendentals=0),
    )(upper, index, node, other)


def add_terms(target, block, left_ref, total, right):
    fill_right(right, block)
    weights = block
    base = pl.multiple_of(target * LEAF_PTS, LEAF_PTS)
    for step in range(LEAF_PTS // 256):
        rows = pl.ds(base + step * 256, 256)
        exponent = jnp.dot(left_ref[rows, :], right[...], preferred_element_type=jnp.float32)
        dense = jnp.exp2(exponent).astype(jnp.bfloat16)
        total[rows, :] += lax.dot_general(
            dense, weights, (((1,), (1,)), ((), ())), preferred_element_type=jnp.float32
        )


def far_kernel(flags_ref, left_ref, before_ref, *refs):
    *siblings, out_ref, right = refs
    out_ref[...] = before_ref[...]
    for level, sibling in enumerate(siblings):
        block = sibling[...]
        fill_right(right, block)

        def leaf_step(leaf, _):
            @pl.when(flags_ref[leaf * LEVELS + level] != 0)
            def _():
                base = pl.multiple_of(leaf * LEAF_PTS, LEAF_PTS)
                for step in range(2):
                    rows = pl.ds(base + step * 512, 512)
                    exponent = jnp.dot(left_ref[rows, :], right[...], preferred_element_type=jnp.float32)
                    dense = jnp.exp2(exponent).astype(jnp.bfloat16)
                    out_ref[rows, :] += lax.dot_general(
                        dense, block, (((1,), (1,)), ((), ())), preferred_element_type=jnp.float32
                    )
            return 0

        lax.fori_loop(0, LEAF_DEV, leaf_step, 0)


def far_terms(flags, left, before, siblings):
    return pl.pallas_call(
        far_kernel,
        out_shape=jax.ShapeDtypeStruct((PTS, 2 * F), jnp.float32),
        in_specs=[SMEM, VMEM, VMEM] + [VMEM] * LEVELS,
        out_specs=VMEM,
        scratch_shapes=[pltpu.VMEM((4 * F, SKEL), jnp.bfloat16)],
        compiler_params=PARAMS,
        name="far_terms",
        cost_estimate=pl.CostEstimate(flops=6 * 10**9, bytes_accessed=8 * 10**6, transcendentals=0),
    )(flags, left, before, *siblings)


def source_of(me, distance, other):
    core = me % 2
    chip = (me // 2 - (1 - 2 * core) * distance + 8) % 8
    return 2 * chip + (core + other) % 2


def copy_kernel(picks, me_ref, table_ref, *refs):
    n_inputs = 1 + max(source for out in picks for source, _ in out)
    inputs, outputs, sems = refs[:n_inputs], refs[n_inputs:-1], refs[-1]
    me = me_ref[0]
    copies = []
    for out_ref, out in zip(outputs, picks):
        for k, (source, leaf_of) in enumerate(out):
            copies.append(
                pltpu.make_async_copy(inputs[source].at[leaf_of(me, table_ref)], out_ref.at[k], sems.at[len(copies)])
            )
    for copy in copies:
        copy.start()
    for copy in copies:
        copy.wait()


def copy_leaves(me, table, inputs, picks):
    size = (2 * F, LEAF_PTS)
    return pl.pallas_call(
        functools.partial(copy_kernel, picks),
        out_shape=[jax.ShapeDtypeStruct((len(out),) + size, jnp.bfloat16) for out in picks],
        in_specs=[SMEM, SMEM] + [pl.BlockSpec(memory_space=pl.ANY)] * len(inputs),
        out_specs=[pl.BlockSpec(memory_space=pl.ANY)] * len(picks),
        scratch_shapes=[pltpu.SemaphoreType.DMA((sum(len(out) for out in picks),))],
        name="copy_leaves",
        cost_estimate=pl.CostEstimate(flops=0, bytes_accessed=3 * 10**6, transcendentals=0),
    )(me, table, *inputs)


def asked(distance, other, to_chip, to_other):
    def leaf_of(me, table_ref):
        core = me % 2
        chip = (me // 2 + (1 - 2 * core) * to_chip + 8) % 8
        return table_ref[(2 * chip + (core + to_other) % 2) * 16 + source_of(me, distance, other)]

    return leaf_of


def at_slot(slot):
    return lambda me, table_ref: slot


def near_kernel(items, first, last, me_ref, source_ref, target_ref, left_ref, *refs):
    refs = list(refs)
    before_ref = None if first else refs.pop(0)
    blocks, out_ref, right = refs[: len(items)], refs[len(items)], refs[-1]
    total = refs[-2] if last else out_ref
    total[...] = jnp.zeros_like(total) if first else before_ref[...]
    for (distance, other, _), block_ref in zip(items, blocks):
        target = target_ref[source_of(me_ref[0], distance, other)]

        @pl.when(target >= 0)
        def _():
            add_terms(target, block_ref[0], left_ref, total, right)

    if last:
        for part in range(8):
            rows = pl.ds(part * 512, 512)
            out_ref[:, rows] = total[rows, :].T[F:]


def near_terms(me, source, target, left, before, items, last=False):
    def index_of(distance, other, slot):
        if slot is not None:
            return lambda i, me_ref, source_ref, target_ref: (slot, 0, 0)
        return lambda i, me_ref, source_ref, target_ref: (source_ref[source_of(me_ref[0], distance, other)], 0, 0)

    first = before is None
    plan = [item[1:] for item in items]
    scratch = [pltpu.VMEM((4 * F, LEAF_PTS), jnp.bfloat16)]
    if last:
        scratch = [pltpu.VMEM((PTS, 2 * F), jnp.float32)] + scratch
    return pl.pallas_call(
        functools.partial(near_kernel, plan, first, last),
        out_shape=jax.ShapeDtypeStruct((F, PTS) if last else (PTS, 2 * F), jnp.float32),
        grid_spec=pltpu.PrefetchScalarGridSpec(
            num_scalar_prefetch=3,
            grid=(1,),
            in_specs=[VMEM] * (1 if first else 2)
            + [pl.BlockSpec((1, 2 * F, LEAF_PTS), index_of(*item)) for item in plan],
            out_specs=VMEM,
            scratch_shapes=scratch,
        ),
        compiler_params=PARAMS,
        name="near_terms",
        cost_estimate=pl.CostEstimate(flops=len(items) * 10**9, bytes_accessed=4 * 10**6, transcendentals=0),
    )(me, source, target, left, *([] if first else [before]), *[item[0] for item in items])


def partner(value, axis, stride):
    pairs = [(source, source ^ 2**stride) for source in range(lax.axis_size(axis))]
    return lax.ppermute(value, axis, pairs)


def hop(value):
    pairs = [(j, (j + 2 - 4 * (j % 2)) % 16) for j in range(16)]
    return lax.ppermute(value, "task", pairs)


def after(value, *others):
    return lax.optimization_barrier((value, *others))[0]


def body(points, weights, point_order, node_order, merge_order, far_list, task_target, task_source):
    me = lax.axis_index("task").astype(jnp.int32).reshape(1)
    source = task_source.reshape(-1)
    target = task_target.reshape(-1)
    near = functools.partial(near_terms, me, source, target)
    position = lax.axis_index("leaf")

    def merged(level, node, other):
        upper = ((position >> level) & 1).astype(jnp.int32).reshape(1)
        return merge_nodes(upper, merge_order[0, 0, level], node, other)

    leaves = sort_leaves(point_order.reshape(-1), points.T, weights.T)
    one_a = hop(leaves)
    beside = partner(leaves, "task", 0)
    node = first_node(node_order.reshape(-1)[:SKEL], leaves)
    beside = after(beside, node)
    one_b = hop(beside)

    sibling_0 = partner(node, "leaf", 0)
    left = target_factors(leaves)
    row = after(jnp.broadcast_to(source, (16, 16)), node)
    table = lax.all_to_all(row, "task", split_axis=0, concat_axis=0, tiled=True).reshape(-1)
    sibling_0 = after(sibling_0, left)
    node = merged(0, node, sibling_0)
    sibling_1 = partner(node, "leaf", 1)
    total = near(left, None, [(leaves, 0, 0, None), (after(beside, node), 0, 1, None)])
    sibling_1 = after(sibling_1, total)
    node = merged(1, node, sibling_1)
    one_a = after(one_a, total)
    two_a = hop(one_a)
    sibling_2 = partner(node, "leaf", 2)
    total = near(left, total, [(one_a, 1, 0, None)])

    one_b = after(one_b, total)
    two_b = hop(one_b)
    [side_one] = copy_leaves(me, table, [one_a, one_b], [[(0, asked(1, 0, 0, 1)), (1, asked(1, 1, 0, 1))]])
    side_one = partner(side_one, "task", 0)
    total = near(left, total, [(one_b, 1, 1, None)])
    total = far_terms(far_list.reshape(-1), left, total, [sibling_0, sibling_1, sibling_2])

    two_a = after(two_a, total)
    [send_a] = copy_leaves(me, table, [two_a], [[(0, asked(2, 0, 1, 0)), (0, asked(2, 0, 1, 1)), (0, asked(2, 0, 2, 0))]])
    three_a = hop(send_a)
    total = near(left, total, [(side_one, -1, 1, 0), (side_one, -1, 0, 1), (two_a, 2, 0, None)])
    two_b = after(two_b, total)
    side_two, send_b = copy_leaves(
        me,
        table,
        [two_a, two_b],
        [
            [(0, asked(2, 0, 0, 1)), (1, asked(2, 1, 0, 1))],
            [(1, asked(2, 1, 1, 0)), (1, asked(2, 1, 1, 1)), (1, asked(2, 1, 2, 0))],
        ],
    )
    three_b = hop(send_b)
    side_two = partner(side_two, "task", 0)
    total = near(left, total, [(two_b, 2, 1, None)])
    three_a = after(three_a, total)
    total = near(left, total, [(three_a, 3, 0, 0)])
    three_b = after(three_b, total)
    send_c, side_three = copy_leaves(
        me, table, [three_a, three_b], [[(0, at_slot(2)), (1, at_slot(2))], [(0, at_slot(1)), (1, at_slot(1))]]
    )
    four = hop(send_c)
    side_three = partner(side_three, "task", 0)
    total = near(left, total, [(side_two, -2, 1, 0), (side_two, -2, 0, 1), (three_b, 3, 1, 0)])
    side_three = after(side_three, total)
    total = near(left, total, [(side_three, -3, 1, 0), (side_three, -3, 0, 1)])
    four = after(four, total)
    total = near(left, total, [(four, 4, 0, 0), (four, 4, 1, 1)], last=True)
    return total.T


def solution(mesh):
    return jax.shard_map(
        body,
        mesh=mesh,
        in_specs=(
            P(("leaf", "task"), None),
            P(("leaf", "task"), None),
            P("leaf", "task", None),
            P("leaf", "task", None),
            P("leaf", "task", None, None),
            P("leaf", "task", None, None),
            P("leaf", "task", None, None),
            P("leaf", "task", None, None),
        ),
        out_specs=P(("leaf", "task"), None),
        check_vma=False,
    )
```

```python
import functools
import math

import jax
import jax.numpy as jnp
from jax import lax
from jax.experimental import pallas as pl
from jax.experimental.pallas import tpu as pltpu
from jax.sharding import PartitionSpec as P

LEAF_PTS = 1024
SKEL = 512
LEVELS = 3
LEAF_DEV = 4
F = 64
PTS = LEAF_PTS * LEAF_DEV
RATE = 1.5 / 64 * math.log2(math.e)
VMEM = pl.BlockSpec(memory_space=pltpu.VMEM)
SMEM = pl.BlockSpec(memory_space=pltpu.SMEM)
HBM = pl.BlockSpec(memory_space=pltpu.HBM)
COST = pl.CostEstimate(flops=0, bytes_accessed=1000, transcendentals=0)
PARAMS = pltpu.CompilerParams(vmem_limit_bytes=40 * 2**20)


def split3(value):
    one = value.astype(jnp.bfloat16).astype(jnp.float32)
    rest = value - one
    two = rest.astype(jnp.bfloat16).astype(jnp.float32)
    return one, two, rest - two


def gather_rows(src_ref, index_ref, dst_ref, count, unroll=16):
    def step(i, _):
        for k in range(unroll):
            at = i * unroll + k
            dst_ref[pl.ds(at, 1), :] = src_ref[pl.ds(index_ref[at], 1), :]
        return 0

    lax.fori_loop(0, count // unroll, step, 0)


def sort_kernel(order_ref, points_ref, weights_ref, out_ref, raw, tree):
    for c in range(8):
        cols = pl.ds(c * 512, 512)
        block = jnp.concatenate([points_ref[:, cols], weights_ref[:, cols]], axis=0)
        raw[pl.ds(c * 512, 512), :] = block.astype(jnp.float32).T
    gather_rows(raw, order_ref, tree, PTS)
    for leaf in range(LEAF_DEV):
        rows = tree[pl.ds(leaf * LEAF_PTS, LEAF_PTS), :]
        out_ref[leaf] = rows.T.astype(jnp.bfloat16)


def sort_leaves(order, points_t, weights_t):
    return pl.pallas_call(
        sort_kernel,
        out_shape=jax.ShapeDtypeStruct((LEAF_DEV, 2 * F, LEAF_PTS), jnp.bfloat16),
        in_specs=[SMEM, VMEM, VMEM],
        out_specs=VMEM,
        scratch_shapes=[pltpu.VMEM((PTS, 2 * F), jnp.float32), pltpu.VMEM((PTS, 2 * F), jnp.float32)],
        compiler_params=PARAMS,
        name="sort_leaves",
        cost_estimate=COST,
    )(order, points_t, weights_t)


def left_factor(rows, with_ones):
    lane = lax.broadcasted_iota(jnp.int32, rows.shape, 1)
    is_point = lane < F
    scaled = jnp.where(is_point, rows * (2 * RATE), 0.0)
    high = scaled.astype(jnp.bfloat16)
    low = scaled - high.astype(jnp.float32)
    norm = -RATE * jnp.sum(jnp.where(is_point, rows * rows, 0.0), axis=1, keepdims=True)
    one, two, three = split3(norm)
    tail = jnp.where(lane == F, one, 0.0)
    tail = jnp.where(lane == F + 1, two, tail)
    tail = jnp.where(lane == F + 2, three, tail)
    if with_ones:
        tail = jnp.where((lane > F + 2) & (lane < F + 6), 1.0, tail)
    second = jnp.where(is_point, low, tail).astype(jnp.bfloat16)
    return jnp.concatenate([high, second], axis=1)


def fill_right(right, block):
    size = block.shape[1]
    points = block[:F]
    wide = points.astype(jnp.float32)
    norm = -RATE * jnp.sum(wide * wide, axis=0, keepdims=True)
    one, two, three = split3(norm)
    row = lax.broadcasted_iota(jnp.int32, (16, size), 0)
    tail = jnp.where(row < 3, 1.0, 0.0)
    tail = jnp.where(row == 3, one, tail)
    tail = jnp.where(row == 4, two, tail)
    tail = jnp.where(row == 5, three, tail)
    right[pl.ds(0, 2 * F), :] = block
    right[pl.ds(2 * F, F), :] = points
    right[pl.ds(3 * F, 16), :] = tail.astype(jnp.bfloat16)
    right[pl.ds(3 * F + 16, F - 16), :] = jnp.zeros((F - 16, size), jnp.bfloat16)


def targets_kernel(leaves_ref, out_ref):
    for leaf in range(LEAF_DEV):
        for half in range(2):
            rows = leaves_ref[leaf, :, pl.ds(half * 512, 512)].astype(jnp.float32).T
            out_ref[pl.ds(leaf * LEAF_PTS + half * 512, 512), :] = left_factor(rows, True)


def target_factors(leaves):
    return pl.pallas_call(
        targets_kernel,
        out_shape=jax.ShapeDtypeStruct((PTS, 4 * F), jnp.bfloat16),
        in_specs=[VMEM],
        out_specs=VMEM,
        compiler_params=PARAMS,
        name="target_factors",
        cost_estimate=COST,
    )(leaves)


def skeleton(index, blocks, right, chosen, total):
    spots = lax.broadcasted_iota(jnp.int32, (SKEL, SKEL), 0).astype(jnp.float32)

    def picks(k):
        return jnp.where(spots == index - k * SKEL, 1.0, 0.0).astype(jnp.bfloat16)

    for k, block in enumerate(blocks):
        part = jnp.dot(block(), picks(k), preferred_element_type=jnp.float32)
        chosen[...] = part if k == 0 else chosen[...] + part
    left = left_factor(chosen[...].T, False)
    ones = jnp.ones((16, SKEL), jnp.bfloat16)
    nt = (((1,), (1,)), ((), ()))
    for k, block in enumerate(blocks):
        taken = lax.dot_general(ones, picks(k), nt, preferred_element_type=jnp.float32)[:1]
        rows = block()
        fill_right(right, rows)
        dense = jnp.exp2(jnp.dot(left, right[...], preferred_element_type=jnp.float32))
        factor = jnp.where(taken > 0.5, 0.0, 1.0 / jnp.sum(dense, axis=0, keepdims=True))
        spread = (dense * factor).astype(jnp.bfloat16)
        part = lax.dot_general(rows, spread, nt, preferred_element_type=jnp.float32)
        total[...] = part if k == 0 else total[...] + part
    row = lax.broadcasted_iota(jnp.int32, (2 * F, SKEL), 0)
    return (chosen[...] + jnp.where(row < F, 0.0, total[...])).astype(jnp.bfloat16)


SKELETON_SCRATCH = [
    pltpu.VMEM((4 * F, SKEL), jnp.bfloat16),
    pltpu.VMEM((2 * F, SKEL), jnp.float32),
    pltpu.VMEM((2 * F, SKEL), jnp.float32),
]


def node_kernel(index_ref, merge_ref, leaves_ref, out_ref, right, chosen, total):
    def block_at(k):
        return lambda: leaves_ref[k // 2, :, pl.ds(k % 2 * SKEL, SKEL)]

    index = index_ref[...].astype(jnp.float32)
    out_ref[pl.ds(0, 2 * F), :] = skeleton(index, [block_at(k) for k in range(2 * LEAF_DEV)], right, chosen, total)
    entry = merge_ref[...]
    high = entry // 32
    row = lax.broadcasted_iota(jnp.int32, (16, SKEL), 0)
    packed = jnp.zeros((16, SKEL), jnp.float32)
    for k, line in enumerate((high[:1], entry[:1] - 32 * high[:1], high[1:2], entry[1:2] - 32 * high[1:2])):
        packed = jnp.where(row == k, line.astype(jnp.float32), packed)
    out_ref[pl.ds(2 * F, 16), :] = packed.astype(jnp.bfloat16)


def first_node(index, merge_index, leaves):
    return pl.pallas_call(
        node_kernel,
        out_shape=jax.ShapeDtypeStruct((2 * F + 16, SKEL), jnp.bfloat16),
        in_specs=[VMEM, VMEM, VMEM],
        out_specs=VMEM,
        scratch_shapes=SKELETON_SCRATCH,
        compiler_params=PARAMS,
        name="first_node",
        cost_estimate=COST,
    )(index, merge_index, leaves)


def siblings_kernel(place_ref, nodes_ref, out_ref, pairs, right, chosen, total):
    place = place_ref[0]
    pair = place // 2
    quad = place // 4
    other_pair = pair + 1 - 2 * (pair % 2)
    other_quad = quad + 1 - 2 * (quad % 2)
    out_ref[0] = nodes_ref[place + 1 - 2 * (place % 2), pl.ds(0, 2 * F), :]

    def entries(base, level):
        lines = nodes_ref[base, pl.ds(2 * F, 16), :].astype(jnp.float32)
        return lines[2 * level : 2 * level + 1] * 32.0 + lines[2 * level + 1 : 2 * level + 2]

    def merge_pair(k, _):
        base = 2 * jnp.where(k == 0, other_pair, 2 * other_quad + k - 1)
        blocks = [lambda: nodes_ref[base, pl.ds(0, 2 * F), :], lambda: nodes_ref[base + 1, pl.ds(0, 2 * F), :]]
        pairs[k] = skeleton(entries(base, 0), blocks, right, chosen, total)
        return 0

    lax.fori_loop(0, 3, merge_pair, 0)
    out_ref[1] = pairs[0]
    out_ref[2] = skeleton(entries(4 * other_quad, 1), [lambda: pairs[1], lambda: pairs[2]], right, chosen, total)


def sibling_nodes(place, nodes):
    return pl.pallas_call(
        siblings_kernel,
        out_shape=jax.ShapeDtypeStruct((LEVELS, 2 * F, SKEL), jnp.bfloat16),
        in_specs=[SMEM, VMEM],
        out_specs=VMEM,
        scratch_shapes=[pltpu.VMEM((3, 2 * F, SKEL), jnp.bfloat16)] + SKELETON_SCRATCH,
        compiler_params=PARAMS,
        name="sibling_nodes",
        cost_estimate=COST,
    )(place, nodes)


def add_terms(target, block, left_ref, total, right):
    fill_right(right, block)
    weights = block
    base = pl.multiple_of(target * LEAF_PTS, LEAF_PTS)
    for step in range(LEAF_PTS // 256):
        rows = pl.ds(base + step * 256, 256)
        exponent = jnp.dot(left_ref[rows, :], right[...], preferred_element_type=jnp.float32)
        dense = jnp.exp2(exponent).astype(jnp.bfloat16)
        total[rows, :] += lax.dot_general(
            dense, weights, (((1,), (1,)), ((), ())), preferred_element_type=jnp.float32
        )


def far_kernel(flags_ref, left_ref, before_ref, siblings_ref, out_ref, right):
    out_ref[...] = before_ref[...]
    for level in range(LEVELS):
        block = siblings_ref[level]
        fill_right(right, block)

        def leaf_step(leaf, _):
            @pl.when(flags_ref[leaf * LEVELS + level] != 0)
            def _():
                base = pl.multiple_of(leaf * LEAF_PTS, LEAF_PTS)
                for step in range(2):
                    rows = pl.ds(base + step * 512, 512)
                    exponent = jnp.dot(left_ref[rows, :], right[...], preferred_element_type=jnp.float32)
                    dense = jnp.exp2(exponent).astype(jnp.bfloat16)
                    out_ref[rows, :] += lax.dot_general(
                        dense, block, (((1,), (1,)), ((), ())), preferred_element_type=jnp.float32
                    )
            return 0

        lax.fori_loop(0, LEAF_DEV, leaf_step, 0)


def far_terms(flags, left, before, siblings):
    return pl.pallas_call(
        far_kernel,
        out_shape=jax.ShapeDtypeStruct((PTS, 2 * F), jnp.float32),
        in_specs=[SMEM, VMEM, VMEM, VMEM],
        out_specs=VMEM,
        scratch_shapes=[pltpu.VMEM((4 * F, SKEL), jnp.bfloat16)],
        compiler_params=PARAMS,
        name="far_terms",
        cost_estimate=COST,
    )(flags, left, before, siblings)


def source_of(me, distance, other):
    core = me % 2
    chip = (me // 2 - (1 - 2 * core) * distance + 8) % 8
    return 2 * chip + (core + other) % 2


def copy_kernel(picks, me_ref, table_ref, *refs):
    inputs, out_ref, held, arrive, leave = refs[:-4], refs[-4], refs[-3], refs[-2], refs[-1]
    me = me_ref[0]
    incoming = [
        pltpu.make_async_copy(inputs[source].at[leaf_of(me, table_ref)], held.at[k], arrive.at[k])
        for k, (source, leaf_of) in enumerate(picks)
    ]
    outgoing = [pltpu.make_async_copy(held.at[k], out_ref.at[k], leave.at[k]) for k in range(len(picks))]
    for copy in incoming:
        copy.start()
    for one, two in zip(incoming, outgoing):
        one.wait()
        two.start()
    for copy in outgoing:
        copy.wait()


def copy_leaves(me, table, inputs, picks):
    size = (len(picks), 2 * F, LEAF_PTS)
    return pl.pallas_call(
        functools.partial(copy_kernel, picks),
        out_shape=jax.ShapeDtypeStruct(size, jnp.bfloat16),
        in_specs=[SMEM, SMEM] + [HBM] * len(inputs),
        out_specs=HBM,
        scratch_shapes=[
            pltpu.VMEM(size, jnp.bfloat16),
            pltpu.SemaphoreType.DMA((len(picks),)),
            pltpu.SemaphoreType.DMA((len(picks),)),
        ],
        compiler_params=PARAMS,
        name="copy_leaves",
        cost_estimate=COST,
    )(me, table, *inputs)


def asked(distance, other, to_chip, to_other):
    def leaf_of(me, table_ref):
        core = me % 2
        chip = (me // 2 + (1 - 2 * core) * to_chip + 8) % 8
        return table_ref[2 * chip + (core + to_other) % 2, 0, source_of(me, distance, other)]

    return leaf_of


def at_slot(slot):
    return lambda me, table_ref: slot


def near_kernel(items, first, last, me_ref, source_ref, target_ref, left_ref, *refs):
    refs = list(refs)
    before_ref = None if first else refs.pop(0)
    count = len(items)
    arrays, out_ref, held, arrive, right = refs[:count], refs[count], refs[count + 1], refs[count + 2], refs[count + 3]
    total = refs[count + 4] if last else out_ref
    plan = []
    for k, ((distance, other, slot), array_ref) in enumerate(zip(items, arrays)):
        peer = source_of(me_ref[0], distance, other)
        leaf = source_ref[peer] if slot is None else slot
        plan.append((target_ref[peer], pltpu.make_async_copy(array_ref.at[leaf], held.at[k], arrive.at[k])))
    for target, copy in plan:
        pl.when(target >= 0)(copy.start)
    total[...] = jnp.zeros_like(total) if first else before_ref[...]
    for k, (target, copy) in enumerate(plan):

        @pl.when(target >= 0)
        def _():
            copy.wait()
            add_terms(target, held[k], left_ref, total, right)

    if last:
        for part in range(8):
            rows = pl.ds(part * 512, 512)
            out_ref[:, rows] = total[rows, :].T[F:]


def near_terms(me, source, target, left, before, items, last=False):
    first = before is None
    plan = [item[1:] for item in items]
    count = len(items)
    scratch = [
        pltpu.VMEM((count, 2 * F, LEAF_PTS), jnp.bfloat16),
        pltpu.SemaphoreType.DMA((count,)),
        pltpu.VMEM((4 * F, LEAF_PTS), jnp.bfloat16),
    ]
    if last:
        scratch.append(pltpu.VMEM((PTS, 2 * F), jnp.float32))
    return pl.pallas_call(
        functools.partial(near_kernel, plan, first, last),
        out_shape=jax.ShapeDtypeStruct((F, PTS) if last else (PTS, 2 * F), jnp.float32),
        in_specs=[SMEM] * 3 + [VMEM] * (1 if first else 2) + [HBM] * count,
        out_specs=VMEM,
        scratch_shapes=scratch,
        compiler_params=PARAMS,
        name="near_terms",
        cost_estimate=COST,
    )(me, source, target, left, *([] if first else [before]), *[item[0] for item in items])


def partner(value, axis, stride):
    pairs = [(source, source ^ 2**stride) for source in range(lax.axis_size(axis))]
    return lax.ppermute(value, axis, pairs)


def hop(value):
    pairs = [(j, (j + 2 - 4 * (j % 2)) % 16) for j in range(16)]
    return lax.ppermute(value, "task", pairs)


def after(value, *others):
    return lax.optimization_barrier((value, *others))[0]


def body(points, weights, point_order, node_order, merge_order, far_list, task_target, task_source):
    me = lax.axis_index("task").astype(jnp.int32).reshape(1)
    source = task_source.reshape(-1)
    target = task_target.reshape(-1)
    near = functools.partial(near_terms, me, source, target)
    place = (lax.axis_index("leaf") % 8).astype(jnp.int32).reshape(1)

    leaves = sort_leaves(point_order.reshape(-1), points.T, weights.T)
    one_a = hop(leaves)
    beside = partner(leaves, "task", 0)
    row = after(jnp.broadcast_to(source, (16, 1, 16)), leaves)
    table = lax.all_to_all(row, "task", split_axis=0, concat_axis=0, tiled=True)
    left = target_factors(leaves)
    beside = after(beside, left)
    one_b = hop(beside)
    node = first_node(node_order.reshape(1, -1)[:, :SKEL], merge_order[0, 0, :, :SKEL], after(leaves, beside))
    groups = [list(range(8 * x, 8 * x + 8)) for x in range(lax.axis_size("leaf") // 8)]
    nodes = lax.all_gather(node, "leaf", axis_index_groups=groups)
    beside = after(beside, node)
    total = near(left, None, [(leaves, 0, 0, None), (beside, 0, 1, None)])

    one_a = after(one_a, total)
    two_a = hop(one_a)
    total = near(left, total, [(one_a, 1, 0, None)])
    one_b = after(one_b, total)
    two_b = hop(one_b)
    total = near(left, total, [(one_b, 1, 1, None)])
    nodes = after(nodes, total)
    siblings = sibling_nodes(place, nodes)
    total = far_terms(far_list.reshape(-1), left, total, siblings)

    two_a = after(two_a, total)
    two_b = after(two_b, two_a)
    send = copy_leaves(
        me,
        table,
        [two_a, two_b],
        [(0, asked(2, 0, 2, 0)), (1, asked(2, 1, 2, 0)), (0, asked(2, 0, 1, 0)), (1, asked(2, 1, 1, 0))],
    )
    three = hop(send)
    send = copy_leaves(me, table, [after(two_a, send), two_b], [(0, asked(2, 0, 1, 1)), (1, asked(2, 1, 1, 1))])
    three_side = hop(send)
    send = copy_leaves(
        me,
        table,
        [after(one_a, send), one_b, two_a, two_b],
        [(0, asked(1, 0, 0, 1)), (1, asked(1, 1, 0, 1)), (2, asked(2, 0, 0, 1)), (3, asked(2, 1, 0, 1))],
    )
    side = partner(send, "task", 0)
    total = near(left, total, [(after(two_a, send), 2, 0, None), (two_b, 2, 1, None)])
    side = after(side, total)
    total = near(left, total, [(side, -1, 1, 0), (side, -1, 0, 1), (side, -2, 1, 2), (side, -2, 0, 3)])
    three = after(three, total)
    send = copy_leaves(me, table, [three], [(0, at_slot(0)), (0, at_slot(1))])
    four = hop(send)
    total = near(left, total, [(after(three, send), 3, 0, 2), (three, 3, 1, 3)])
    three_side = partner(after(three_side, total), "task", 0)
    four = after(four, total)
    total = near(left, total, [(four, 4, 0, 0), (four, 4, 1, 1)])
    three_side = after(three_side, total)
    total = near(left, total, [(three_side, -3, 1, 0), (three_side, -3, 0, 1)], last=True)
    return total.T


def solution(mesh):
    return jax.shard_map(
        body,
        mesh=mesh,
        in_specs=(
            P(("leaf", "task"), None),
            P(("leaf", "task"), None),
            P("leaf", "task", None),
            P("leaf", "task", None),
            P("leaf", "task", None, None),
            P("leaf", "task", None, None),
            P("leaf", "task", None, None),
            P("leaf", "task", None, None),
        ),
        out_specs=P(("leaf", "task"), None),
        check_vma=False,
    )
```

```python
import functools
import math

import jax
import jax.numpy as jnp
from jax import lax
from jax.experimental import pallas as pl
from jax.experimental.pallas import tpu as pltpu
from jax.sharding import PartitionSpec as P

LEAF_PTS = 1024
SKEL = 512
LEVELS = 3
LEAF_DEV = 4
F = 64
PTS = LEAF_PTS * LEAF_DEV
RATE = 1.5 / 64 * math.log2(math.e)
VMEM = pl.BlockSpec(memory_space=pltpu.VMEM)
SMEM = pl.BlockSpec(memory_space=pltpu.SMEM)
HBM = pl.BlockSpec(memory_space=pltpu.HBM)
COST = pl.CostEstimate(flops=0, bytes_accessed=1000, transcendentals=0)
PARAMS = pltpu.CompilerParams(vmem_limit_bytes=20 * 2**20)


def split3(value):
    one = value.astype(jnp.bfloat16).astype(jnp.float32)
    rest = value - one
    two = rest.astype(jnp.bfloat16).astype(jnp.float32)
    return one, two, rest - two


def gather_rows(src_ref, index_ref, dst_ref, count, unroll=16):
    def step(i, _):
        for k in range(unroll):
            at = i * unroll + k
            dst_ref[pl.ds(at, 1), :] = src_ref[pl.ds(index_ref[at], 1), :]
        return 0

    lax.fori_loop(0, count // unroll, step, 0)


def sort_kernel(order_ref, points_ref, weights_ref, out_ref, raw, tree):
    for c in range(8):
        cols = pl.ds(c * 512, 512)
        block = jnp.concatenate([points_ref[:, cols], weights_ref[:, cols]], axis=0)
        raw[pl.ds(c * 512, 512), :] = block.astype(jnp.float32).T
    gather_rows(raw, order_ref, tree, PTS)
    for leaf in range(LEAF_DEV):
        rows = tree[pl.ds(leaf * LEAF_PTS, LEAF_PTS), :]
        out_ref[leaf] = rows.T.astype(jnp.bfloat16)


def sort_leaves(order, points_t, weights_t):
    return pl.pallas_call(
        sort_kernel,
        out_shape=jax.ShapeDtypeStruct((LEAF_DEV, 2 * F, LEAF_PTS), jnp.bfloat16),
        in_specs=[SMEM, VMEM, VMEM],
        out_specs=VMEM,
        scratch_shapes=[pltpu.VMEM((PTS, 2 * F), jnp.float32), pltpu.VMEM((PTS, 2 * F), jnp.float32)],
        compiler_params=PARAMS,
        name="sort_leaves",
        cost_estimate=COST,
    )(order, points_t, weights_t)


def left_factor(rows, with_ones):
    lane = lax.broadcasted_iota(jnp.int32, rows.shape, 1)
    is_point = lane < F
    scaled = jnp.where(is_point, rows * (2 * RATE), 0.0)
    high = scaled.astype(jnp.bfloat16)
    low = scaled - high.astype(jnp.float32)
    norm = -RATE * jnp.sum(jnp.where(is_point, rows * rows, 0.0), axis=1, keepdims=True)
    one, two, three = split3(norm)
    tail = jnp.where(lane == F, one, 0.0)
    tail = jnp.where(lane == F + 1, two, tail)
    tail = jnp.where(lane == F + 2, three, tail)
    if with_ones:
        tail = jnp.where((lane > F + 2) & (lane < F + 6), 1.0, tail)
    second = jnp.where(is_point, low, tail).astype(jnp.bfloat16)
    return jnp.concatenate([high, second], axis=1)


def fill_right(right, block):
    size = block.shape[1]
    points = block[:F]
    wide = points.astype(jnp.float32)
    norm = -RATE * jnp.sum(wide * wide, axis=0, keepdims=True)
    one, two, three = split3(norm)
    row = lax.broadcasted_iota(jnp.int32, (16, size), 0)
    tail = jnp.where(row < 3, 1.0, 0.0)
    tail = jnp.where(row == 3, one, tail)
    tail = jnp.where(row == 4, two, tail)
    tail = jnp.where(row == 5, three, tail)
    right[pl.ds(0, 2 * F), :] = block
    right[pl.ds(2 * F, F), :] = points
    right[pl.ds(3 * F, 16), :] = tail.astype(jnp.bfloat16)
    right[pl.ds(3 * F + 16, F - 16), :] = jnp.zeros((F - 16, size), jnp.bfloat16)


def targets_kernel(leaves_ref, out_ref):
    for leaf in range(LEAF_DEV):
        for half in range(2):
            rows = leaves_ref[leaf, :, pl.ds(half * 512, 512)].astype(jnp.float32).T
            out_ref[pl.ds(leaf * LEAF_PTS + half * 512, 512), :] = left_factor(rows, True)


def target_factors(leaves):
    return pl.pallas_call(
        targets_kernel,
        out_shape=jax.ShapeDtypeStruct((PTS, 4 * F), jnp.bfloat16),
        in_specs=[VMEM],
        out_specs=VMEM,
        compiler_params=PARAMS,
        name="target_factors",
        cost_estimate=COST,
    )(leaves)


def skeleton(index, blocks, right, chosen, total):
    spots = lax.broadcasted_iota(jnp.int32, (SKEL, SKEL), 0).astype(jnp.float32)

    def picks(k):
        return jnp.where(spots == index - k * SKEL, 1.0, 0.0).astype(jnp.bfloat16)

    for k, block in enumerate(blocks):
        part = jnp.dot(block(), picks(k), preferred_element_type=jnp.float32)
        chosen[...] = part if k == 0 else chosen[...] + part
    left = left_factor(chosen[...].T, False)
    ones = jnp.ones((16, SKEL), jnp.bfloat16)
    nt = (((1,), (1,)), ((), ()))
    for k, block in enumerate(blocks):
        taken = lax.dot_general(ones, picks(k), nt, preferred_element_type=jnp.float32)[:1]
        rows = block()
        fill_right(right, rows)
        dense = jnp.exp2(jnp.dot(left, right[...], preferred_element_type=jnp.float32))
        factor = jnp.where(taken > 0.5, 0.0, 1.0 / jnp.sum(dense, axis=0, keepdims=True))
        spread = (dense * factor).astype(jnp.bfloat16)
        part = lax.dot_general(rows, spread, nt, preferred_element_type=jnp.float32)
        total[...] = part if k == 0 else total[...] + part
    row = lax.broadcasted_iota(jnp.int32, (2 * F, SKEL), 0)
    return (chosen[...] + jnp.where(row < F, 0.0, total[...])).astype(jnp.bfloat16)


SKELETON_SCRATCH = [
    pltpu.VMEM((4 * F, SKEL), jnp.bfloat16),
    pltpu.VMEM((2 * F, SKEL), jnp.float32),
    pltpu.VMEM((2 * F, SKEL), jnp.float32),
]


def node_kernel(index_ref, merge_ref, leaves_ref, out_ref, right, chosen, total):
    def block_at(k):
        return lambda: leaves_ref[k // 2, :, pl.ds(k % 2 * SKEL, SKEL)]

    index = index_ref[...].astype(jnp.float32)
    out_ref[pl.ds(0, 2 * F), :] = skeleton(index, [block_at(k) for k in range(2 * LEAF_DEV)], right, chosen, total)
    entry = merge_ref[...]
    high = entry // 32
    row = lax.broadcasted_iota(jnp.int32, (16, SKEL), 0)
    packed = jnp.zeros((16, SKEL), jnp.float32)
    for k, line in enumerate((high[:1], entry[:1] - 32 * high[:1], high[1:2], entry[1:2] - 32 * high[1:2])):
        packed = jnp.where(row == k, line.astype(jnp.float32), packed)
    out_ref[pl.ds(2 * F, 16), :] = packed.astype(jnp.bfloat16)


def first_node(index, merge_index, leaves):
    return pl.pallas_call(
        node_kernel,
        out_shape=jax.ShapeDtypeStruct((2 * F + 16, SKEL), jnp.bfloat16),
        in_specs=[VMEM, VMEM, VMEM],
        out_specs=VMEM,
        scratch_shapes=SKELETON_SCRATCH,
        compiler_params=PARAMS,
        name="first_node",
        cost_estimate=COST,
    )(index, merge_index, leaves)


def siblings_kernel(place_ref, nodes_ref, out_ref, pairs, right, chosen, total):
    place = place_ref[0]
    pair = place // 2
    quad = place // 4
    other_pair = pair + 1 - 2 * (pair % 2)
    other_quad = quad + 1 - 2 * (quad % 2)
    out_ref[0] = nodes_ref[place + 1 - 2 * (place % 2), pl.ds(0, 2 * F), :]

    def entries(base, level):
        lines = nodes_ref[base, pl.ds(2 * F, 16), :].astype(jnp.float32)
        return lines[2 * level : 2 * level + 1] * 32.0 + lines[2 * level + 1 : 2 * level + 2]

    def merge_pair(k, _):
        base = 2 * jnp.where(k == 0, other_pair, 2 * other_quad + k - 1)
        blocks = [lambda: nodes_ref[base, pl.ds(0, 2 * F), :], lambda: nodes_ref[base + 1, pl.ds(0, 2 * F), :]]
        pairs[k] = skeleton(entries(base, 0), blocks, right, chosen, total)
        return 0

    lax.fori_loop(0, 3, merge_pair, 0)
    out_ref[1] = pairs[0]
    out_ref[2] = skeleton(entries(4 * other_quad, 1), [lambda: pairs[1], lambda: pairs[2]], right, chosen, total)


def sibling_nodes(place, nodes):
    return pl.pallas_call(
        siblings_kernel,
        out_shape=jax.ShapeDtypeStruct((LEVELS, 2 * F, SKEL), jnp.bfloat16),
        in_specs=[SMEM, VMEM],
        out_specs=VMEM,
        scratch_shapes=[pltpu.VMEM((3, 2 * F, SKEL), jnp.bfloat16)] + SKELETON_SCRATCH,
        compiler_params=PARAMS,
        name="sibling_nodes",
        cost_estimate=COST,
    )(place, nodes)


def add_terms(target, block, left_ref, total, right):
    fill_right(right, block)
    weights = block
    base = pl.multiple_of(target * LEAF_PTS, LEAF_PTS)
    for step in range(LEAF_PTS // 256):
        rows = pl.ds(base + step * 256, 256)
        exponent = jnp.dot(left_ref[rows, :], right[...], preferred_element_type=jnp.float32)
        dense = jnp.exp2(exponent).astype(jnp.bfloat16)
        total[rows, :] += lax.dot_general(
            dense, weights, (((1,), (1,)), ((), ())), preferred_element_type=jnp.float32
        )


def far_kernel(flags_ref, left_ref, before_ref, siblings_ref, out_ref, right):
    out_ref[...] = before_ref[...]
    for level in range(LEVELS):
        block = siblings_ref[level]
        fill_right(right, block)

        def leaf_step(leaf, _):
            @pl.when(flags_ref[leaf * LEVELS + level] != 0)
            def _():
                base = pl.multiple_of(leaf * LEAF_PTS, LEAF_PTS)
                for step in range(2):
                    rows = pl.ds(base + step * 512, 512)
                    exponent = jnp.dot(left_ref[rows, :], right[...], preferred_element_type=jnp.float32)
                    dense = jnp.exp2(exponent).astype(jnp.bfloat16)
                    out_ref[rows, :] += lax.dot_general(
                        dense, block, (((1,), (1,)), ((), ())), preferred_element_type=jnp.float32
                    )
            return 0

        lax.fori_loop(0, LEAF_DEV, leaf_step, 0)


def far_terms(flags, left, before, siblings):
    return pl.pallas_call(
        far_kernel,
        out_shape=jax.ShapeDtypeStruct((PTS, 2 * F), jnp.float32),
        in_specs=[SMEM, VMEM, VMEM, VMEM],
        out_specs=VMEM,
        scratch_shapes=[pltpu.VMEM((4 * F, SKEL), jnp.bfloat16)],
        compiler_params=PARAMS,
        name="far_terms",
        cost_estimate=COST,
    )(flags, left, before, siblings)


def source_of(me, distance, other):
    core = me % 2
    chip = (me // 2 - (1 - 2 * core) * distance + 8) % 8
    return 2 * chip + (core + other) % 2


def copy_kernel(picks, me_ref, table_ref, *refs):
    inputs, outputs = refs[: -3 - len(picks)], refs[-3 - len(picks) : -3]
    held, arrive, leave = refs[-3:]
    me = me_ref[0]
    rows = [(out_ref, k, *pick) for out_ref, out in zip(outputs, picks) for k, pick in enumerate(out)]
    incoming, outgoing = [], []
    for at, (out_ref, k, source, leaf_of) in enumerate(rows):
        incoming.append(pltpu.make_async_copy(inputs[source].at[leaf_of(me, table_ref)], held.at[at], arrive.at[at]))
        outgoing.append(pltpu.make_async_copy(held.at[at], out_ref.at[k], leave.at[at]))
    for copy in incoming:
        copy.start()
    for one, two in zip(incoming, outgoing):
        one.wait()
        two.start()
    for copy in outgoing:
        copy.wait()


def copy_leaves(me, table, inputs, picks):
    size = (2 * F, LEAF_PTS)
    count = sum(len(rows) for rows in picks)
    return pl.pallas_call(
        functools.partial(copy_kernel, picks),
        out_shape=[jax.ShapeDtypeStruct((len(rows),) + size, jnp.bfloat16) for rows in picks],
        in_specs=[SMEM, SMEM] + [HBM] * len(inputs),
        out_specs=[HBM] * len(picks),
        scratch_shapes=[
            pltpu.VMEM((count,) + size, jnp.bfloat16),
            pltpu.SemaphoreType.DMA((count,)),
            pltpu.SemaphoreType.DMA((count,)),
        ],
        compiler_params=PARAMS,
        name="copy_leaves",
        cost_estimate=COST,
    )(me, table, *inputs)


def asked(distance, other, to_chip, to_other):
    def leaf_of(me, table_ref):
        core = me % 2
        chip = (me // 2 + (1 - 2 * core) * to_chip + 8) % 8
        return table_ref[2 * chip + (core + to_other) % 2, 0, source_of(me, distance, other)]

    return leaf_of


def at_slot(slot):
    return lambda me, table_ref: slot


def near_kernel(items, first, last, me_ref, source_ref, target_ref, left_ref, *refs):
    refs = list(refs)
    before_ref = None if first else refs.pop(0)
    count = len(items)
    arrays, out_ref, held, arrive, right = refs[:count], refs[count], refs[count + 1], refs[count + 2], refs[count + 3]
    total = refs[count + 4] if last else out_ref
    plan = []
    for k, ((distance, other, slot), array_ref) in enumerate(zip(items, arrays)):
        peer = source_of(me_ref[0], distance, other)
        leaf = source_ref[peer] if slot is None else slot
        plan.append((target_ref[peer], pltpu.make_async_copy(array_ref.at[leaf], held.at[k], arrive.at[k])))
    for target, copy in plan:
        pl.when(target >= 0)(copy.start)
    total[...] = jnp.zeros_like(total) if first else before_ref[...]
    for k, (target, copy) in enumerate(plan):

        @pl.when(target >= 0)
        def _():
            copy.wait()
            add_terms(target, held[k], left_ref, total, right)

    if last:
        for part in range(8):
            rows = pl.ds(part * 512, 512)
            out_ref[:, rows] = total[rows, :].T[F:]


def near_terms(me, source, target, left, before, items, last=False):
    first = before is None
    plan = [item[1:] for item in items]
    count = len(items)
    scratch = [
        pltpu.VMEM((count, 2 * F, LEAF_PTS), jnp.bfloat16),
        pltpu.SemaphoreType.DMA((count,)),
        pltpu.VMEM((4 * F, LEAF_PTS), jnp.bfloat16),
    ]
    if last:
        scratch.append(pltpu.VMEM((PTS, 2 * F), jnp.float32))
    return pl.pallas_call(
        functools.partial(near_kernel, plan, first, last),
        out_shape=jax.ShapeDtypeStruct((F, PTS) if last else (PTS, 2 * F), jnp.float32),
        in_specs=[SMEM] * 3 + [VMEM] * (1 if first else 2) + [HBM] * count,
        out_specs=VMEM,
        scratch_shapes=scratch,
        compiler_params=PARAMS,
        name="near_terms",
        cost_estimate=COST,
    )(me, source, target, left, *([] if first else [before]), *[item[0] for item in items])


def partner(value, axis, stride):
    pairs = [(source, source ^ 2**stride) for source in range(lax.axis_size(axis))]
    return lax.ppermute(value, axis, pairs)


def hop(value):
    pairs = [(j, (j + 2 - 4 * (j % 2)) % 16) for j in range(16)]
    return lax.ppermute(value, "task", pairs)


def after(value, *others):
    return lax.optimization_barrier((value, *others))[0]


def body(points, weights, point_order, node_order, merge_order, far_list, task_target, task_source):
    me = lax.axis_index("task").astype(jnp.int32).reshape(1)
    source = task_source.reshape(-1)
    target = task_target.reshape(-1)
    near = functools.partial(near_terms, me, source, target)
    place = (lax.axis_index("leaf") % 8).astype(jnp.int32).reshape(1)

    leaves = sort_leaves(point_order.reshape(-1), points.T, weights.T)
    one_a = hop(leaves)
    beside = partner(leaves, "task", 0)
    row = after(jnp.broadcast_to(source, (16, 1, 16)), leaves)
    table = lax.all_to_all(row, "task", split_axis=0, concat_axis=0, tiled=True)
    left = target_factors(leaves)
    beside = after(beside, left)
    one_b = hop(beside)
    node = first_node(node_order.reshape(1, -1)[:, :SKEL], merge_order[0, 0, :, :SKEL], after(leaves, beside))
    groups = [list(range(8 * x, 8 * x + 8)) for x in range(lax.axis_size("leaf") // 8)]
    nodes = lax.all_gather(node, "leaf", axis_index_groups=groups)
    beside = after(beside, node)
    total = near(left, None, [(leaves, 0, 0, None), (beside, 0, 1, None)])

    one_a = after(one_a, total)
    two_a = hop(one_a)
    one_b = after(one_b, one_a)
    two_b = hop(one_b)
    total = near(left, total, [(one_a, 1, 0, None), (one_b, 1, 1, None)])
    two_a = after(two_a, total)
    send, send_side = copy_leaves(
        me,
        table,
        [one_a, one_b, two_a],
        [
            [(2, asked(2, 0, 1, 0)), (2, asked(2, 0, 1, 1)), (2, asked(2, 0, 2, 0))],
            [(0, asked(1, 0, 0, 1)), (1, asked(1, 1, 0, 1)), (2, asked(2, 0, 0, 1))],
        ],
    )
    three_a = hop(send)
    side = partner(send_side, "task", 0)
    two_b = after(two_b, send)
    [send] = copy_leaves(
        me, table, [two_b], [[(0, asked(2, 1, 1, 0)), (0, asked(2, 1, 1, 1)), (0, asked(2, 1, 2, 0))]]
    )
    three_b = hop(send)
    total = near(left, total, [(two_a, 2, 0, None), (after(two_b, send), 2, 1, None)])
    nodes = after(nodes, total)
    siblings = sibling_nodes(place, nodes)
    total = after(total, siblings)
    side = after(side, siblings)
    total = near(left, total, [(side, -1, 1, 0), (side, -1, 0, 1), (side, -2, 1, 2)])
    three_a = after(three_a, total)
    send, send_side = copy_leaves(
        me,
        table,
        [two_b, three_a, three_b],
        [[(1, at_slot(2)), (2, at_slot(2))], [(0, asked(2, 1, 0, 1)), (1, at_slot(1)), (2, at_slot(1))]],
    )
    four = hop(send)
    side = partner(send_side, "task", 0)
    total = far_terms(far_list.reshape(-1), left, after(total, send), siblings)
    side = after(side, total)
    total = near(
        left,
        total,
        [
            (three_a, 3, 0, 0),
            (three_b, 3, 1, 0),
            (side, -2, 0, 0),
            (side, -3, 1, 1),
            (side, -3, 0, 2),
            (after(four, side), 4, 0, 0),
            (four, 4, 1, 1),
        ],
        last=True,
    )
    return total.T


def solution(mesh):
    return jax.shard_map(
        body,
        mesh=mesh,
        in_specs=(
            P(("leaf", "task"), None),
            P(("leaf", "task"), None),
            P("leaf", "task", None),
            P("leaf", "task", None),
            P("leaf", "task", None, None),
            P("leaf", "task", None, None),
            P("leaf", "task", None, None),
            P("leaf", "task", None, None),
        ),
        out_specs=P(("leaf", "task"), None),
        check_vma=False,
    )
```

```python
import functools
import math

import jax
import jax.numpy as jnp
from jax import lax
from jax.experimental import pallas as pl
from jax.experimental.pallas import tpu as pltpu
from jax.sharding import PartitionSpec as P

LEAF_PTS = 1024
SKEL = 512
LEVELS = 3
LEAF_DEV = 4
F = 64
PTS = LEAF_PTS * LEAF_DEV
RATE = 1.5 / 64 * math.log2(math.e)
VMEM = pl.BlockSpec(memory_space=pltpu.VMEM)
SMEM = pl.BlockSpec(memory_space=pltpu.SMEM)
HBM = pl.BlockSpec(memory_space=pltpu.HBM)
COST = pl.CostEstimate(flops=0, bytes_accessed=1000, transcendentals=0)
PARAMS = pltpu.CompilerParams(vmem_limit_bytes=20 * 2**20)


def split3(value):
    one = value.astype(jnp.bfloat16).astype(jnp.float32)
    rest = value - one
    two = rest.astype(jnp.bfloat16).astype(jnp.float32)
    return one, two, rest - two


def gather_rows(src_ref, index_ref, dst_ref, count, unroll=16):
    def step(i, _):
        for k in range(unroll):
            at = i * unroll + k
            dst_ref[pl.ds(at, 1), :] = src_ref[pl.ds(index_ref[at], 1), :]
        return 0

    lax.fori_loop(0, count // unroll, step, 0)


def sort_kernel(order_ref, points_ref, weights_ref, out_ref, raw, tree):
    for c in range(8):
        cols = pl.ds(c * 512, 512)
        block = jnp.concatenate([points_ref[:, cols], weights_ref[:, cols]], axis=0)
        raw[pl.ds(c * 512, 512), :] = block.astype(jnp.float32).T
    gather_rows(raw, order_ref, tree, PTS)
    for leaf in range(LEAF_DEV):
        rows = tree[pl.ds(leaf * LEAF_PTS, LEAF_PTS), :]
        out_ref[leaf] = rows.T.astype(jnp.bfloat16)


def sort_leaves(order, points_t, weights_t):
    return pl.pallas_call(
        sort_kernel,
        out_shape=jax.ShapeDtypeStruct((LEAF_DEV, 2 * F, LEAF_PTS), jnp.bfloat16),
        in_specs=[SMEM, VMEM, VMEM],
        out_specs=VMEM,
        scratch_shapes=[pltpu.VMEM((PTS, 2 * F), jnp.float32), pltpu.VMEM((PTS, 2 * F), jnp.float32)],
        compiler_params=PARAMS,
        name="sort_leaves",
        cost_estimate=COST,
    )(order, points_t, weights_t)


def left_factor(rows, with_ones):
    lane = lax.broadcasted_iota(jnp.int32, rows.shape, 1)
    is_point = lane < F
    scaled = jnp.where(is_point, rows * (2 * RATE), 0.0)
    high = scaled.astype(jnp.bfloat16)
    low = scaled - high.astype(jnp.float32)
    norm = -RATE * jnp.sum(jnp.where(is_point, rows * rows, 0.0), axis=1, keepdims=True)
    one, two, three = split3(norm)
    tail = jnp.where(lane == F, one, 0.0)
    tail = jnp.where(lane == F + 1, two, tail)
    tail = jnp.where(lane == F + 2, three, tail)
    if with_ones:
        tail = jnp.where((lane > F + 2) & (lane < F + 6), 1.0, tail)
    second = jnp.where(is_point, low, tail).astype(jnp.bfloat16)
    return jnp.concatenate([high, second], axis=1)


def fill_right(right, block):
    size = block.shape[1]
    points = block[:F]
    wide = points.astype(jnp.float32)
    norm = -RATE * jnp.sum(wide * wide, axis=0, keepdims=True)
    one, two, three = split3(norm)
    row = lax.broadcasted_iota(jnp.int32, (16, size), 0)
    tail = jnp.where(row < 3, 1.0, 0.0)
    tail = jnp.where(row == 3, one, tail)
    tail = jnp.where(row == 4, two, tail)
    tail = jnp.where(row == 5, three, tail)
    right[pl.ds(0, 2 * F), :] = block
    right[pl.ds(2 * F, F), :] = points
    right[pl.ds(3 * F, 16), :] = tail.astype(jnp.bfloat16)
    right[pl.ds(3 * F + 16, F - 16), :] = jnp.zeros((F - 16, size), jnp.bfloat16)


def targets_kernel(leaves_ref, out_ref):
    for leaf in range(LEAF_DEV):
        for half in range(2):
            rows = leaves_ref[leaf, :, pl.ds(half * 512, 512)].astype(jnp.float32).T
            out_ref[pl.ds(leaf * LEAF_PTS + half * 512, 512), :] = left_factor(rows, True)


def target_factors(leaves):
    return pl.pallas_call(
        targets_kernel,
        out_shape=jax.ShapeDtypeStruct((PTS, 4 * F), jnp.bfloat16),
        in_specs=[VMEM],
        out_specs=VMEM,
        compiler_params=PARAMS,
        name="target_factors",
        cost_estimate=COST,
    )(leaves)


def skeleton(index, blocks, right, chosen, total):
    spots = lax.broadcasted_iota(jnp.int32, (SKEL, SKEL), 0).astype(jnp.float32)

    def picks(k):
        return jnp.where(spots == index - k * SKEL, 1.0, 0.0).astype(jnp.bfloat16)

    for k, block in enumerate(blocks):
        part = jnp.dot(block(), picks(k), preferred_element_type=jnp.float32)
        chosen[...] = part if k == 0 else chosen[...] + part
    left = left_factor(chosen[...].T, False)
    ones = jnp.ones((16, SKEL), jnp.bfloat16)
    nt = (((1,), (1,)), ((), ()))
    for k, block in enumerate(blocks):
        taken = lax.dot_general(ones, picks(k), nt, preferred_element_type=jnp.float32)[:1]
        rows = block()
        fill_right(right, rows)
        dense = jnp.exp2(jnp.dot(left, right[...], preferred_element_type=jnp.float32))
        factor = jnp.where(taken > 0.5, 0.0, 1.0 / jnp.sum(dense, axis=0, keepdims=True))
        spread = (dense * factor).astype(jnp.bfloat16)
        part = lax.dot_general(rows, spread, nt, preferred_element_type=jnp.float32)
        total[...] = part if k == 0 else total[...] + part
    row = lax.broadcasted_iota(jnp.int32, (2 * F, SKEL), 0)
    return (chosen[...] + jnp.where(row < F, 0.0, total[...])).astype(jnp.bfloat16)


SKELETON_SCRATCH = [
    pltpu.VMEM((4 * F, SKEL), jnp.bfloat16),
    pltpu.VMEM((2 * F, SKEL), jnp.float32),
    pltpu.VMEM((2 * F, SKEL), jnp.float32),
]


def node_kernel(index_ref, merge_ref, leaves_ref, out_ref, right, chosen, total):
    def block_at(k):
        return lambda: leaves_ref[k // 2, :, pl.ds(k % 2 * SKEL, SKEL)]

    index = index_ref[...].astype(jnp.float32)
    out_ref[pl.ds(0, 2 * F), :] = skeleton(index, [block_at(k) for k in range(2 * LEAF_DEV)], right, chosen, total)
    entry = merge_ref[...]
    high = entry // 32
    row = lax.broadcasted_iota(jnp.int32, (16, SKEL), 0)
    packed = jnp.zeros((16, SKEL), jnp.float32)
    for k, line in enumerate((high[:1], entry[:1] - 32 * high[:1], high[1:2], entry[1:2] - 32 * high[1:2])):
        packed = jnp.where(row == k, line.astype(jnp.float32), packed)
    out_ref[pl.ds(2 * F, 16), :] = packed.astype(jnp.bfloat16)


def first_node(index, merge_index, leaves):
    return pl.pallas_call(
        node_kernel,
        out_shape=jax.ShapeDtypeStruct((2 * F + 16, SKEL), jnp.bfloat16),
        in_specs=[VMEM, VMEM, VMEM],
        out_specs=VMEM,
        scratch_shapes=SKELETON_SCRATCH,
        compiler_params=PARAMS,
        name="first_node",
        cost_estimate=COST,
    )(index, merge_index, leaves)


def siblings_kernel(place_ref, nodes_ref, out_ref, pairs, right, chosen, total):
    place = place_ref[0]
    pair = place // 2
    quad = place // 4
    other_pair = pair + 1 - 2 * (pair % 2)
    other_quad = quad + 1 - 2 * (quad % 2)
    out_ref[0] = nodes_ref[place + 1 - 2 * (place % 2), pl.ds(0, 2 * F), :]

    def entries(base, level):
        lines = nodes_ref[base, pl.ds(2 * F, 16), :].astype(jnp.float32)
        return lines[2 * level : 2 * level + 1] * 32.0 + lines[2 * level + 1 : 2 * level + 2]

    def merge_pair(k, _):
        base = 2 * jnp.where(k == 0, other_pair, 2 * other_quad + k - 1)
        blocks = [lambda: nodes_ref[base, pl.ds(0, 2 * F), :], lambda: nodes_ref[base + 1, pl.ds(0, 2 * F), :]]
        pairs[k] = skeleton(entries(base, 0), blocks, right, chosen, total)
        return 0

    lax.fori_loop(0, 3, merge_pair, 0)
    out_ref[1] = pairs[0]
    out_ref[2] = skeleton(entries(4 * other_quad, 1), [lambda: pairs[1], lambda: pairs[2]], right, chosen, total)


def sibling_nodes(place, nodes):
    return pl.pallas_call(
        siblings_kernel,
        out_shape=jax.ShapeDtypeStruct((LEVELS, 2 * F, SKEL), jnp.bfloat16),
        in_specs=[SMEM, VMEM],
        out_specs=VMEM,
        scratch_shapes=[pltpu.VMEM((3, 2 * F, SKEL), jnp.bfloat16)] + SKELETON_SCRATCH,
        compiler_params=PARAMS,
        name="sibling_nodes",
        cost_estimate=COST,
    )(place, nodes)


def add_terms(target, block, left_ref, total, right):
    fill_right(right, block)
    weights = block
    base = pl.multiple_of(target * LEAF_PTS, LEAF_PTS)
    for step in range(LEAF_PTS // 256):
        rows = pl.ds(base + step * 256, 256)
        exponent = jnp.dot(left_ref[rows, :], right[...], preferred_element_type=jnp.float32)
        dense = jnp.exp2(exponent).astype(jnp.bfloat16)
        total[rows, :] += lax.dot_general(
            dense, weights, (((1,), (1,)), ((), ())), preferred_element_type=jnp.float32
        )


def far_kernel(flags_ref, left_ref, before_ref, siblings_ref, out_ref, right):
    out_ref[...] = before_ref[...]
    for level in range(LEVELS):
        block = siblings_ref[level]
        fill_right(right, block)

        def leaf_step(leaf, _):
            @pl.when(flags_ref[leaf * LEVELS + level] != 0)
            def _():
                base = pl.multiple_of(leaf * LEAF_PTS, LEAF_PTS)
                for step in range(2):
                    rows = pl.ds(base + step * 512, 512)
                    exponent = jnp.dot(left_ref[rows, :], right[...], preferred_element_type=jnp.float32)
                    dense = jnp.exp2(exponent).astype(jnp.bfloat16)
                    out_ref[rows, :] += lax.dot_general(
                        dense, block, (((1,), (1,)), ((), ())), preferred_element_type=jnp.float32
                    )
            return 0

        lax.fori_loop(0, LEAF_DEV, leaf_step, 0)


def far_terms(flags, left, before, siblings):
    return pl.pallas_call(
        far_kernel,
        out_shape=jax.ShapeDtypeStruct((PTS, 2 * F), jnp.float32),
        in_specs=[SMEM, VMEM, VMEM, VMEM],
        out_specs=VMEM,
        scratch_shapes=[pltpu.VMEM((4 * F, SKEL), jnp.bfloat16)],
        compiler_params=PARAMS,
        name="far_terms",
        cost_estimate=COST,
    )(flags, left, before, siblings)


def source_of(me, distance, other):
    core = me % 2
    chip = (me // 2 - (1 - 2 * core) * distance + 8) % 8
    return 2 * chip + (core + other) % 2


def copy_kernel(picks, me_ref, table_ref, *refs):
    inputs, outputs = refs[: -3 - len(picks)], refs[-3 - len(picks) : -3]
    held, arrive, leave = refs[-3:]
    me = me_ref[0]
    rows = [(out_ref, k, *pick) for out_ref, out in zip(outputs, picks) for k, pick in enumerate(out)]
    incoming, outgoing = [], []
    for at, (out_ref, k, source, leaf_of) in enumerate(rows):
        incoming.append(pltpu.make_async_copy(inputs[source].at[leaf_of(me, table_ref)], held.at[at], arrive.at[at]))
        outgoing.append(pltpu.make_async_copy(held.at[at], out_ref.at[k], leave.at[at]))
    for copy in incoming:
        copy.start()
    for one, two in zip(incoming, outgoing):
        one.wait()
        two.start()
    for copy in outgoing:
        copy.wait()


def copy_leaves(me, table, inputs, picks):
    size = (2 * F, LEAF_PTS)
    count = sum(len(rows) for rows in picks)
    return pl.pallas_call(
        functools.partial(copy_kernel, picks),
        out_shape=[jax.ShapeDtypeStruct((len(rows),) + size, jnp.bfloat16) for rows in picks],
        in_specs=[SMEM, SMEM] + [HBM] * len(inputs),
        out_specs=[HBM] * len(picks),
        scratch_shapes=[
            pltpu.VMEM((count,) + size, jnp.bfloat16),
            pltpu.SemaphoreType.DMA((count,)),
            pltpu.SemaphoreType.DMA((count,)),
        ],
        compiler_params=PARAMS,
        name="copy_leaves",
        cost_estimate=COST,
    )(me, table, *inputs)


def asked(distance, other, to_chip, to_other):
    def leaf_of(me, table_ref):
        core = me % 2
        chip = (me // 2 + (1 - 2 * core) * to_chip + 8) % 8
        return table_ref[2 * chip + (core + to_other) % 2, 0, source_of(me, distance, other)]

    return leaf_of


def at_slot(slot):
    return lambda me, table_ref: slot


def near_kernel(items, first, last, me_ref, source_ref, target_ref, left_ref, *refs):
    refs = list(refs)
    before_ref = None if first else refs.pop(0)
    count = len(items)
    arrays, out_ref, held, arrive, right = refs[:count], refs[count], refs[count + 1], refs[count + 2], refs[count + 3]
    total = refs[count + 4] if last else out_ref
    plan = []
    for k, ((distance, other, slot), array_ref) in enumerate(zip(items, arrays)):
        peer = source_of(me_ref[0], distance, other)
        leaf = source_ref[peer] if slot is None else slot
        plan.append((target_ref[peer], pltpu.make_async_copy(array_ref.at[leaf], held.at[k], arrive.at[k])))
    for target, copy in plan:
        pl.when(target >= 0)(copy.start)
    total[...] = jnp.zeros_like(total) if first else before_ref[...]
    for k, (target, copy) in enumerate(plan):

        @pl.when(target >= 0)
        def _():
            copy.wait()
            add_terms(target, held[k], left_ref, total, right)

    if last:
        for part in range(8):
            rows = pl.ds(part * 512, 512)
            out_ref[:, rows] = total[rows, :].T[F:]


def near_terms(me, source, target, left, before, items, last=False):
    first = before is None
    plan = [item[1:] for item in items]
    count = len(items)
    scratch = [
        pltpu.VMEM((count, 2 * F, LEAF_PTS), jnp.bfloat16),
        pltpu.SemaphoreType.DMA((count,)),
        pltpu.VMEM((4 * F, LEAF_PTS), jnp.bfloat16),
    ]
    if last:
        scratch.append(pltpu.VMEM((PTS, 2 * F), jnp.float32))
    return pl.pallas_call(
        functools.partial(near_kernel, plan, first, last),
        out_shape=jax.ShapeDtypeStruct((F, PTS) if last else (PTS, 2 * F), jnp.float32),
        in_specs=[SMEM] * 3 + [VMEM] * (1 if first else 2) + [HBM] * count,
        out_specs=VMEM,
        scratch_shapes=scratch,
        compiler_params=PARAMS,
        name="near_terms",
        cost_estimate=COST,
    )(me, source, target, left, *([] if first else [before]), *[item[0] for item in items])


def partner(value, axis, stride):
    pairs = [(source, source ^ 2**stride) for source in range(lax.axis_size(axis))]
    return lax.ppermute(value, axis, pairs)


def hop(value):
    pairs = [(j, (j + 2 - 4 * (j % 2)) % 16) for j in range(16)]
    return lax.ppermute(value, "task", pairs)


def after(value, *others):
    return lax.optimization_barrier((value, *others))[0]


def body(points, weights, point_order, node_order, merge_order, far_list, task_target, task_source):
    me = lax.axis_index("task").astype(jnp.int32).reshape(1)
    source = task_source.reshape(-1)
    target = task_target.reshape(-1)
    near = functools.partial(near_terms, me, source, target)
    place = (lax.axis_index("leaf") % 8).astype(jnp.int32).reshape(1)

    row = jnp.broadcast_to(source, (16, 1, 16))
    table = lax.all_to_all(row, "task", split_axis=0, concat_axis=0, tiled=True)
    leaves = sort_leaves(point_order.reshape(-1), points.T, weights.T)
    leaves = after(leaves, table)
    one_a = hop(leaves)
    beside = partner(leaves, "task", 0)
    one_b = hop(beside)
    left = target_factors(after(leaves, beside))
    node = first_node(node_order.reshape(1, -1)[:, :SKEL], merge_order[0, 0, :, :SKEL], after(leaves, beside))
    groups = [list(range(8 * x, 8 * x + 8)) for x in range(lax.axis_size("leaf") // 8)]
    nodes = lax.all_to_all(
        jnp.broadcast_to(node, (8,) + node.shape), "leaf", split_axis=0, concat_axis=0, axis_index_groups=groups, tiled=True
    )

    one_a = after(one_a, node)
    two_a = hop(one_a)
    one_b = after(one_b, one_a)
    two_b = hop(one_b)
    siblings = sibling_nodes(place, after(nodes, one_b))
    total = near(
        left,
        None,
        [
            (leaves, 0, 0, None),
            (after(beside, siblings), 0, 1, None),
            (one_a, 1, 0, None),
            (one_b, 1, 1, None),
        ],
    )
    two_a = after(two_a, total)
    send, send_side = copy_leaves(
        me,
        table,
        [one_a, one_b, two_a],
        [
            [(2, asked(2, 0, 1, 0)), (2, asked(2, 0, 1, 1)), (2, asked(2, 0, 2, 0))],
            [(0, asked(1, 0, 0, 1)), (1, asked(1, 1, 0, 1)), (2, asked(2, 0, 0, 1))],
        ],
    )
    three_a = hop(send)
    side = partner(send_side, "task", 0)
    two_b = after(two_b, send)
    [send] = copy_leaves(
        me, table, [two_b], [[(0, asked(2, 1, 1, 0)), (0, asked(2, 1, 1, 1)), (0, asked(2, 1, 2, 0))]]
    )
    three_b = hop(send)
    side = after(side, send)
    total = near(
        left,
        total,
        [(two_a, 2, 0, None), (two_b, 2, 1, None), (side, -1, 1, 0), (side, -1, 0, 1), (side, -2, 1, 2)],
    )
    three_a = after(three_a, total)
    send, send_side = copy_leaves(
        me,
        table,
        [two_b, three_a, three_b],
        [[(1, at_slot(2)), (2, at_slot(2))], [(0, asked(2, 1, 0, 1)), (1, at_slot(1)), (2, at_slot(1))]],
    )
    four = hop(send)
    side = partner(send_side, "task", 0)
    total = far_terms(far_list.reshape(-1), left, after(total, send), siblings)
    side = after(side, total)
    total = near(
        left,
        total,
        [
            (three_a, 3, 0, 0),
            (three_b, 3, 1, 0),
            (side, -2, 0, 0),
            (side, -3, 1, 1),
            (side, -3, 0, 2),
            (after(four, side), 4, 0, 0),
            (four, 4, 1, 1),
        ],
        last=True,
    )
    return total.T


def solution(mesh):
    return jax.shard_map(
        body,
        mesh=mesh,
        in_specs=(
            P(("leaf", "task"), None),
            P(("leaf", "task"), None),
            P("leaf", "task", None),
            P("leaf", "task", None),
            P("leaf", "task", None, None),
            P("leaf", "task", None, None),
            P("leaf", "task", None, None),
            P("leaf", "task", None, None),
        ),
        out_specs=P(("leaf", "task"), None),
        check_vma=False,
    )
```

```python
import functools
import math

import jax
import jax.numpy as jnp
from jax import lax
from jax.experimental import pallas as pl
from jax.experimental.pallas import tpu as pltpu
from jax.sharding import PartitionSpec as P

LEAF_PTS = 1024
SKEL = 512
LEVELS = 3
LEAF_DEV = 4
F = 64
PTS = LEAF_PTS * LEAF_DEV
RATE = 1.5 / 64 * math.log2(math.e)
VMEM = pl.BlockSpec(memory_space=pltpu.VMEM)
SMEM = pl.BlockSpec(memory_space=pltpu.SMEM)
HBM = pl.BlockSpec(memory_space=pltpu.HBM)
COST = pl.CostEstimate(flops=0, bytes_accessed=1000, transcendentals=0)
PARAMS = pltpu.CompilerParams(vmem_limit_bytes=20 * 2**20)


def split3(value):
    one = value.astype(jnp.bfloat16).astype(jnp.float32)
    rest = value - one
    two = rest.astype(jnp.bfloat16).astype(jnp.float32)
    return one, two, rest - two


def gather_rows(src_ref, index_ref, dst_ref, count, unroll=16):
    def step(i, _):
        for k in range(unroll):
            at = i * unroll + k
            dst_ref[pl.ds(at, 1), :] = src_ref[pl.ds(index_ref[at], 1), :]
        return 0

    lax.fori_loop(0, count // unroll, step, 0)


def sort_kernel(order_ref, points_ref, weights_ref, out_ref, held, arrive, raw, tree):
    copies = []
    for c in range(4):
        cols = pl.ds(c * 1024, 1024)
        for k, array_ref in enumerate((points_ref, weights_ref)):
            into = held.at[pl.ds(k * F, F), cols]
            copies.append(pltpu.make_async_copy(array_ref.at[:, cols], into, arrive.at[2 * c + k]))
    for copy in copies:
        copy.start()
    for c in range(8):
        if c % 2 == 0:
            copies[c].wait()
            copies[c + 1].wait()
        raw[pl.ds(c * 512, 512), :] = held[:, pl.ds(c * 512, 512)].astype(jnp.float32).T
    gather_rows(raw, order_ref, tree, PTS)
    for leaf in range(LEAF_DEV):
        rows = tree[pl.ds(leaf * LEAF_PTS, LEAF_PTS), :]
        out_ref[leaf] = rows.T.astype(jnp.bfloat16)


def sort_leaves(order, points_t, weights_t):
    return pl.pallas_call(
        sort_kernel,
        out_shape=jax.ShapeDtypeStruct((LEAF_DEV, 2 * F, LEAF_PTS), jnp.bfloat16),
        in_specs=[SMEM, HBM, HBM],
        out_specs=VMEM,
        scratch_shapes=[
            pltpu.VMEM((2 * F, PTS), jnp.bfloat16),
            pltpu.SemaphoreType.DMA((8,)),
            pltpu.VMEM((PTS, 2 * F), jnp.float32),
            pltpu.VMEM((PTS, 2 * F), jnp.float32),
        ],
        compiler_params=pltpu.CompilerParams(vmem_limit_bytes=56 * 2**20),
        name="sort_leaves",
        cost_estimate=COST,
    )(order, points_t, weights_t)


def left_factor(rows, with_ones):
    lane = lax.broadcasted_iota(jnp.int32, rows.shape, 1)
    is_point = lane < F
    scaled = jnp.where(is_point, rows * (2 * RATE), 0.0)
    high = scaled.astype(jnp.bfloat16)
    low = scaled - high.astype(jnp.float32)
    norm = -RATE * jnp.sum(jnp.where(is_point, rows * rows, 0.0), axis=1, keepdims=True)
    one, two, three = split3(norm)
    tail = jnp.where(lane == F, one, 0.0)
    tail = jnp.where(lane == F + 1, two, tail)
    tail = jnp.where(lane == F + 2, three, tail)
    if with_ones:
        tail = jnp.where((lane > F + 2) & (lane < F + 6), 1.0, tail)
    second = jnp.where(is_point, low, tail).astype(jnp.bfloat16)
    return jnp.concatenate([high, second], axis=1)


def fill_right(right, block):
    size = block.shape[1]
    points = block[:F]
    wide = points.astype(jnp.float32)
    norm = -RATE * jnp.sum(wide * wide, axis=0, keepdims=True)
    one, two, three = split3(norm)
    row = lax.broadcasted_iota(jnp.int32, (16, size), 0)
    tail = jnp.where(row < 3, 1.0, 0.0)
    tail = jnp.where(row == 3, one, tail)
    tail = jnp.where(row == 4, two, tail)
    tail = jnp.where(row == 5, three, tail)
    right[pl.ds(0, 2 * F), :] = block
    right[pl.ds(2 * F, F), :] = points
    right[pl.ds(3 * F, 16), :] = tail.astype(jnp.bfloat16)
    right[pl.ds(3 * F + 16, F - 16), :] = jnp.zeros((F - 16, size), jnp.bfloat16)


def targets_kernel(leaves_ref, out_ref):
    for leaf in range(LEAF_DEV):
        for half in range(2):
            rows = leaves_ref[leaf, :, pl.ds(half * 512, 512)].astype(jnp.float32).T
            out_ref[pl.ds(leaf * LEAF_PTS + half * 512, 512), :] = left_factor(rows, True)


def target_factors(leaves):
    return pl.pallas_call(
        targets_kernel,
        out_shape=jax.ShapeDtypeStruct((PTS, 4 * F), jnp.bfloat16),
        in_specs=[VMEM],
        out_specs=VMEM,
        compiler_params=PARAMS,
        name="target_factors",
        cost_estimate=COST,
    )(leaves)


def skeleton(index, blocks, right, chosen, total):
    spots = lax.broadcasted_iota(jnp.int32, (SKEL, SKEL), 0).astype(jnp.float32)

    def picks(k):
        return jnp.where(spots == index - k * SKEL, 1.0, 0.0).astype(jnp.bfloat16)

    for k, block in enumerate(blocks):
        part = jnp.dot(block(), picks(k), preferred_element_type=jnp.float32)
        chosen[...] = part if k == 0 else chosen[...] + part
    left = left_factor(chosen[...].T, False)
    ones = jnp.ones((16, SKEL), jnp.bfloat16)
    nt = (((1,), (1,)), ((), ()))
    for k, block in enumerate(blocks):
        taken = lax.dot_general(ones, picks(k), nt, preferred_element_type=jnp.float32)[:1]
        rows = block()
        fill_right(right, rows)
        dense = jnp.exp2(jnp.dot(left, right[...], preferred_element_type=jnp.float32))
        factor = jnp.where(taken > 0.5, 0.0, 1.0 / jnp.sum(dense, axis=0, keepdims=True))
        spread = (dense * factor).astype(jnp.bfloat16)
        part = lax.dot_general(rows, spread, nt, preferred_element_type=jnp.float32)
        total[...] = part if k == 0 else total[...] + part
    row = lax.broadcasted_iota(jnp.int32, (2 * F, SKEL), 0)
    return (chosen[...] + jnp.where(row < F, 0.0, total[...])).astype(jnp.bfloat16)


SKELETON_SCRATCH = [
    pltpu.VMEM((4 * F, SKEL), jnp.bfloat16),
    pltpu.VMEM((2 * F, SKEL), jnp.float32),
    pltpu.VMEM((2 * F, SKEL), jnp.float32),
]


def node_kernel(index_ref, merge_ref, leaves_ref, out_ref, right, chosen, total):
    def block_at(k):
        return lambda: leaves_ref[k // 2, :, pl.ds(k % 2 * SKEL, SKEL)]

    index = index_ref[...].astype(jnp.float32)
    out_ref[pl.ds(0, 2 * F), :] = skeleton(index, [block_at(k) for k in range(2 * LEAF_DEV)], right, chosen, total)
    entry = merge_ref[...]
    high = entry // 32
    row = lax.broadcasted_iota(jnp.int32, (16, SKEL), 0)
    packed = jnp.zeros((16, SKEL), jnp.float32)
    for k, line in enumerate((high[:1], entry[:1] - 32 * high[:1], high[1:2], entry[1:2] - 32 * high[1:2])):
        packed = jnp.where(row == k, line.astype(jnp.float32), packed)
    out_ref[pl.ds(2 * F, 16), :] = packed.astype(jnp.bfloat16)


def first_node(index, merge_index, leaves):
    return pl.pallas_call(
        node_kernel,
        out_shape=jax.ShapeDtypeStruct((2 * F + 16, SKEL), jnp.bfloat16),
        in_specs=[VMEM, VMEM, VMEM],
        out_specs=VMEM,
        scratch_shapes=SKELETON_SCRATCH,
        compiler_params=PARAMS,
        name="first_node",
        cost_estimate=COST,
    )(index, merge_index, leaves)


def add_terms(target, block, left_ref, total, right):
    fill_right(right, block)
    weights = block
    base = pl.multiple_of(target * LEAF_PTS, LEAF_PTS)
    for step in range(LEAF_PTS // 256):
        rows = pl.ds(base + step * 256, 256)
        exponent = jnp.dot(left_ref[rows, :], right[...], preferred_element_type=jnp.float32)
        dense = jnp.exp2(exponent).astype(jnp.bfloat16)
        total[rows, :] += lax.dot_general(
            dense, weights, (((1,), (1,)), ((), ())), preferred_element_type=jnp.float32
        )


def far_kernel(place_ref, flags_ref, left_ref, before_ref, nodes_ref, out_ref, siblings, pairs, right, chosen, total):
    place = place_ref[0]
    pair = place // 2
    quad = place // 4
    other_pair = pair + 1 - 2 * (pair % 2)
    other_quad = quad + 1 - 2 * (quad % 2)
    siblings[0] = nodes_ref[place + 1 - 2 * (place % 2), pl.ds(0, 2 * F), :]

    def entries(base, level):
        lines = nodes_ref[base, pl.ds(2 * F, 16), :].astype(jnp.float32)
        return lines[2 * level : 2 * level + 1] * 32.0 + lines[2 * level + 1 : 2 * level + 2]

    def merge_pair(k, _):
        base = 2 * jnp.where(k == 0, other_pair, 2 * other_quad + k - 1)
        blocks = [lambda: nodes_ref[base, pl.ds(0, 2 * F), :], lambda: nodes_ref[base + 1, pl.ds(0, 2 * F), :]]
        pairs[k] = skeleton(entries(base, 0), blocks, right, chosen, total)
        return 0

    lax.fori_loop(0, 3, merge_pair, 0)
    siblings[1] = pairs[0]
    siblings[2] = skeleton(entries(4 * other_quad, 1), [lambda: pairs[1], lambda: pairs[2]], right, chosen, total)
    out_ref[...] = before_ref[...]
    for level in range(LEVELS):
        block = siblings[level]
        fill_right(right, block)

        def leaf_step(leaf, _):
            @pl.when(flags_ref[leaf * LEVELS + level] != 0)
            def _():
                base = pl.multiple_of(leaf * LEAF_PTS, LEAF_PTS)
                for step in range(2):
                    rows = pl.ds(base + step * 512, 512)
                    exponent = jnp.dot(left_ref[rows, :], right[...], preferred_element_type=jnp.float32)
                    dense = jnp.exp2(exponent).astype(jnp.bfloat16)
                    out_ref[rows, :] += lax.dot_general(
                        dense, block, (((1,), (1,)), ((), ())), preferred_element_type=jnp.float32
                    )
            return 0

        lax.fori_loop(0, LEAF_DEV, leaf_step, 0)


def far_terms(place, flags, left, before, nodes):
    return pl.pallas_call(
        far_kernel,
        out_shape=jax.ShapeDtypeStruct((PTS, 2 * F), jnp.float32),
        in_specs=[SMEM, SMEM, VMEM, VMEM, VMEM],
        out_specs=VMEM,
        scratch_shapes=[pltpu.VMEM((3, 2 * F, SKEL), jnp.bfloat16), pltpu.VMEM((3, 2 * F, SKEL), jnp.bfloat16)]
        + SKELETON_SCRATCH,
        compiler_params=PARAMS,
        name="far_terms",
        cost_estimate=COST,
    )(place, flags, left, before, nodes)


def source_of(me, distance, other):
    core = me % 2
    chip = (me // 2 - (1 - 2 * core) * distance + 8) % 8
    return 2 * chip + (core + other) % 2


def copy_kernel(picks, me_ref, table_ref, *refs):
    inputs, outputs = refs[: -3 - len(picks)], refs[-3 - len(picks) : -3]
    held, arrive, leave = refs[-3:]
    me = me_ref[0]
    rows = [(out_ref, k, *pick) for out_ref, out in zip(outputs, picks) for k, pick in enumerate(out)]
    incoming, outgoing = [], []
    for at, (out_ref, k, source, leaf_of) in enumerate(rows):
        incoming.append(pltpu.make_async_copy(inputs[source].at[leaf_of(me, table_ref)], held.at[at], arrive.at[at]))
        outgoing.append(pltpu.make_async_copy(held.at[at], out_ref.at[k], leave.at[at]))
    for copy in incoming:
        copy.start()
    for one, two in zip(incoming, outgoing):
        one.wait()
        two.start()
    for copy in outgoing:
        copy.wait()


def copy_leaves(me, table, inputs, picks):
    size = (2 * F, LEAF_PTS)
    count = sum(len(rows) for rows in picks)
    return pl.pallas_call(
        functools.partial(copy_kernel, picks),
        out_shape=[jax.ShapeDtypeStruct((len(rows),) + size, jnp.bfloat16) for rows in picks],
        in_specs=[SMEM, SMEM] + [HBM] * len(inputs),
        out_specs=[HBM] * len(picks),
        scratch_shapes=[
            pltpu.VMEM((count,) + size, jnp.bfloat16),
            pltpu.SemaphoreType.DMA((count,)),
            pltpu.SemaphoreType.DMA((count,)),
        ],
        compiler_params=PARAMS,
        name="copy_leaves",
        cost_estimate=COST,
    )(me, table, *inputs)


def asked(distance, other, to_chip, to_other):
    def leaf_of(me, table_ref):
        core = me % 2
        chip = (me // 2 + (1 - 2 * core) * to_chip + 8) % 8
        return table_ref[2 * chip + (core + to_other) % 2, 0, source_of(me, distance, other)]

    return leaf_of


def at_slot(slot):
    return lambda me, table_ref: slot


def near_kernel(items, first, last, me_ref, source_ref, target_ref, left_ref, *refs):
    refs = list(refs)
    before_ref = None if first else refs.pop(0)
    count = len(items)
    arrays, out_ref, held, arrive, right = refs[:count], refs[count], refs[count + 1], refs[count + 2], refs[count + 3]
    total = refs[count + 4] if last else out_ref
    plan = []
    for k, ((distance, other, slot), array_ref) in enumerate(zip(items, arrays)):
        peer = source_of(me_ref[0], distance, other)
        leaf = source_ref[peer] if slot is None else slot
        plan.append((target_ref[peer], pltpu.make_async_copy(array_ref.at[leaf], held.at[k], arrive.at[k])))
    for target, copy in plan:
        pl.when(target >= 0)(copy.start)
    total[...] = jnp.zeros_like(total) if first else before_ref[...]
    for k, (target, copy) in enumerate(plan):

        @pl.when(target >= 0)
        def _():
            copy.wait()
            add_terms(target, held[k], left_ref, total, right)

    if last:
        for part in range(8):
            rows = pl.ds(part * 512, 512)
            out_ref[:, rows] = total[rows, :].T[F:]


def near_terms(me, source, target, left, before, items, last=False):
    first = before is None
    plan = [item[1:] for item in items]
    count = len(items)
    scratch = [
        pltpu.VMEM((count, 2 * F, LEAF_PTS), jnp.bfloat16),
        pltpu.SemaphoreType.DMA((count,)),
        pltpu.VMEM((4 * F, LEAF_PTS), jnp.bfloat16),
    ]
    if last:
        scratch.append(pltpu.VMEM((PTS, 2 * F), jnp.float32))
    return pl.pallas_call(
        functools.partial(near_kernel, plan, first, last),
        out_shape=jax.ShapeDtypeStruct((F, PTS) if last else (PTS, 2 * F), jnp.float32),
        in_specs=[SMEM] * 3 + [VMEM] * (1 if first else 2) + [HBM] * count,
        out_specs=VMEM,
        scratch_shapes=scratch,
        compiler_params=PARAMS,
        name="near_terms",
        cost_estimate=COST,
    )(me, source, target, left, *([] if first else [before]), *[item[0] for item in items])


def partner(value, axis, stride):
    pairs = [(source, source ^ 2**stride) for source in range(lax.axis_size(axis))]
    return lax.ppermute(value, axis, pairs)


def hop(value):
    pairs = [(j, (j + 2 - 4 * (j % 2)) % 16) for j in range(16)]
    return lax.ppermute(value, "task", pairs)


def after(value, *others):
    return lax.optimization_barrier((value, *others))[0]


def body(points, weights, point_order, node_order, merge_order, far_list, task_target, task_source):
    me = lax.axis_index("task").astype(jnp.int32).reshape(1)
    source = task_source.reshape(-1)
    target = task_target.reshape(-1)
    near = functools.partial(near_terms, me, source, target)
    place = (lax.axis_index("leaf") % 8).astype(jnp.int32).reshape(1)

    row = jnp.broadcast_to(source, (16, 1, 16))
    table = lax.all_to_all(row, "task", split_axis=0, concat_axis=0, tiled=True)
    leaves = after(sort_leaves(point_order.reshape(-1), points.T, weights.T), table)
    one_a = hop(leaves)
    beside = partner(leaves, "task", 0)
    one_b = hop(beside)
    left = target_factors(after(leaves, beside))
    node = first_node(node_order.reshape(1, -1)[:, :SKEL], merge_order[0, 0, :, :SKEL], after(leaves, beside))
    groups = [list(range(8 * x, 8 * x + 8)) for x in range(lax.axis_size("leaf") // 8)]
    nodes = lax.all_to_all(
        jnp.broadcast_to(node, (8,) + node.shape), "leaf", split_axis=0, concat_axis=0, axis_index_groups=groups, tiled=True
    )

    one_a = after(one_a, node)
    two_a = hop(one_a)
    one_b = after(one_b, one_a)
    two_b = hop(one_b)
    total = near(
        left,
        None,
        [
            (leaves, 0, 0, None),
            (beside, 0, 1, None),
            (one_a, 1, 0, None),
            (one_b, 1, 1, None),
        ],
    )
    two_a = after(two_a, total)
    send, send_side = copy_leaves(
        me,
        table,
        [one_a, one_b, two_a],
        [
            [(2, asked(2, 0, 1, 0)), (2, asked(2, 0, 1, 1)), (2, asked(2, 0, 2, 0))],
            [(0, asked(1, 0, 0, 1)), (1, asked(1, 1, 0, 1)), (2, asked(2, 0, 0, 1))],
        ],
    )
    three_a = hop(send)
    side = partner(send_side, "task", 0)
    two_b = after(two_b, send)
    [send] = copy_leaves(
        me, table, [two_b], [[(0, asked(2, 1, 1, 0)), (0, asked(2, 1, 1, 1)), (0, asked(2, 1, 2, 0))]]
    )
    three_b = hop(send)
    total = far_terms(place, far_list.reshape(-1), left, total, after(nodes, send))
    three_a = after(three_a, total)
    send, send_side = copy_leaves(
        me,
        table,
        [two_b, three_a, three_b],
        [[(1, at_slot(2)), (2, at_slot(2))], [(0, asked(2, 1, 0, 1)), (1, at_slot(1)), (2, at_slot(1))]],
    )
    four = hop(send)
    last_side = partner(send_side, "task", 0)
    total = near(
        left,
        total,
        [
            (after(two_a, send), 2, 0, None),
            (two_b, 2, 1, None),
            (side, -1, 1, 0),
            (side, -1, 0, 1),
            (side, -2, 1, 2),
            (three_a, 3, 0, 0),
            (three_b, 3, 1, 0),
        ],
    )
    last_side = after(last_side, total)
    total = near(
        left,
        total,
        [
            (last_side, -2, 0, 0),
            (last_side, -3, 1, 1),
            (last_side, -3, 0, 2),
            (after(four, last_side), 4, 0, 0),
            (four, 4, 1, 1),
        ],
        last=True,
    )
    return total.T


def solution(mesh):
    return jax.shard_map(
        body,
        mesh=mesh,
        in_specs=(
            P(("leaf", "task"), None),
            P(("leaf", "task"), None),
            P("leaf", "task", None),
            P("leaf", "task", None),
            P("leaf", "task", None, None),
            P("leaf", "task", None, None),
            P("leaf", "task", None, None),
            P("leaf", "task", None, None),
        ),
        out_specs=P(("leaf", "task"), None),
        check_vma=False,
    )
```

```python
import functools
import math

import jax
import jax.numpy as jnp
from jax import lax
from jax.experimental import pallas as pl
from jax.experimental.pallas import tpu as pltpu
from jax.sharding import PartitionSpec as P

LEAF_PTS = 1024
SKEL = 512
LEVELS = 3
LEAF_DEV = 4
F = 64
PTS = LEAF_PTS * LEAF_DEV
RATE = 1.5 / 64 * math.log2(math.e)
VMEM = pl.BlockSpec(memory_space=pltpu.VMEM)
SMEM = pl.BlockSpec(memory_space=pltpu.SMEM)
HBM = pl.BlockSpec(memory_space=pltpu.HBM)
COST = pl.CostEstimate(flops=0, bytes_accessed=1000, transcendentals=0)
PARAMS = pltpu.CompilerParams(vmem_limit_bytes=20 * 2**20)


def split3(value):
    one = value.astype(jnp.bfloat16).astype(jnp.float32)
    rest = value - one
    two = rest.astype(jnp.bfloat16).astype(jnp.float32)
    return one, two, rest - two


def gather_rows(src_ref, index_ref, dst_ref, count, unroll=16):
    def step(i, _):
        for k in range(unroll):
            at = i * unroll + k
            dst_ref[pl.ds(at, 1), :] = src_ref[pl.ds(index_ref[at], 1), :]
        return 0

    lax.fori_loop(0, count // unroll, step, 0)


def sort_kernel(order_ref, points_ref, weights_ref, out_ref, held, arrive, raw, tree):
    copies = []
    for c in range(4):
        cols = pl.ds(c * 1024, 1024)
        for k, array_ref in enumerate((points_ref, weights_ref)):
            into = held.at[pl.ds(k * F, F), cols]
            copies.append(pltpu.make_async_copy(array_ref.at[:, cols], into, arrive.at[2 * c + k]))
    for copy in copies:
        copy.start()
    for c in range(8):
        if c % 2 == 0:
            copies[c].wait()
            copies[c + 1].wait()
        raw[pl.ds(c * 512, 512), :] = held[:, pl.ds(c * 512, 512)].astype(jnp.float32).T
    gather_rows(raw, order_ref, tree, PTS)
    for leaf in range(LEAF_DEV):
        rows = tree[pl.ds(leaf * LEAF_PTS, LEAF_PTS), :]
        out_ref[leaf] = rows.T.astype(jnp.bfloat16)


def sort_leaves(order, points_t, weights_t):
    return pl.pallas_call(
        sort_kernel,
        out_shape=jax.ShapeDtypeStruct((LEAF_DEV, 2 * F, LEAF_PTS), jnp.bfloat16),
        in_specs=[SMEM, HBM, HBM],
        out_specs=VMEM,
        scratch_shapes=[
            pltpu.VMEM((2 * F, PTS), jnp.bfloat16),
            pltpu.SemaphoreType.DMA((8,)),
            pltpu.VMEM((PTS, 2 * F), jnp.float32),
            pltpu.VMEM((PTS, 2 * F), jnp.float32),
        ],
        compiler_params=pltpu.CompilerParams(vmem_limit_bytes=56 * 2**20),
        name="sort_leaves",
        cost_estimate=COST,
    )(order, points_t, weights_t)


def left_factor(rows, with_ones):
    lane = lax.broadcasted_iota(jnp.int32, rows.shape, 1)
    is_point = lane < F
    scaled = jnp.where(is_point, rows * (2 * RATE), 0.0)
    high = scaled.astype(jnp.bfloat16)
    low = scaled - high.astype(jnp.float32)
    norm = -RATE * jnp.sum(jnp.where(is_point, rows * rows, 0.0), axis=1, keepdims=True)
    one, two, three = split3(norm)
    tail = jnp.where(lane == F, one, 0.0)
    tail = jnp.where(lane == F + 1, two, tail)
    tail = jnp.where(lane == F + 2, three, tail)
    if with_ones:
        tail = jnp.where((lane > F + 2) & (lane < F + 6), 1.0, tail)
    second = jnp.where(is_point, low, tail).astype(jnp.bfloat16)
    return jnp.concatenate([high, second], axis=1)


def fill_right(right, block):
    size = block.shape[1]
    points = block[:F]
    wide = points.astype(jnp.float32)
    norm = -RATE * jnp.sum(wide * wide, axis=0, keepdims=True)
    one, two, three = split3(norm)
    row = lax.broadcasted_iota(jnp.int32, (16, size), 0)
    tail = jnp.where(row < 3, 1.0, 0.0)
    tail = jnp.where(row == 3, one, tail)
    tail = jnp.where(row == 4, two, tail)
    tail = jnp.where(row == 5, three, tail)
    right[pl.ds(0, 2 * F), :] = block
    right[pl.ds(2 * F, F), :] = points
    right[pl.ds(3 * F, 16), :] = tail.astype(jnp.bfloat16)
    right[pl.ds(3 * F + 16, F - 16), :] = jnp.zeros((F - 16, size), jnp.bfloat16)


def targets_kernel(leaves_ref, out_ref):
    for leaf in range(LEAF_DEV):
        for half in range(2):
            rows = leaves_ref[leaf, :, pl.ds(half * 512, 512)].astype(jnp.float32).T
            out_ref[pl.ds(leaf * LEAF_PTS + half * 512, 512), :] = left_factor(rows, True)


def target_factors(leaves):
    return pl.pallas_call(
        targets_kernel,
        out_shape=jax.ShapeDtypeStruct((PTS, 4 * F), jnp.bfloat16),
        in_specs=[VMEM],
        out_specs=VMEM,
        compiler_params=PARAMS,
        name="target_factors",
        cost_estimate=COST,
    )(leaves)


def skeleton(index, blocks, right, chosen, total):
    spots = lax.broadcasted_iota(jnp.int32, (SKEL, SKEL), 1).astype(jnp.float32)
    column = jnp.broadcast_to(index, (8, SKEL)).T[:, :1]
    nt = (((1,), (1,)), ((), ()))
    taken = []
    for k, block in enumerate(blocks):
        picks = jnp.where(spots == column - k * SKEL, 1.0, 0.0)
        taken.append(jnp.sum(picks, axis=0, keepdims=True))
        part = lax.dot_general(picks.astype(jnp.bfloat16), block(), nt, preferred_element_type=jnp.float32)
        chosen[...] = part if k == 0 else chosen[...] + part
    left = left_factor(chosen[...], False)
    for k, block in enumerate(blocks):
        rows = block()
        fill_right(right, rows)
        dense = jnp.exp2(jnp.dot(left, right[...], preferred_element_type=jnp.float32))
        factor = jnp.where(taken[k] > 0.5, 0.0, 1.0 / jnp.sum(dense, axis=0, keepdims=True))
        spread = (dense * factor).astype(jnp.bfloat16)
        part = lax.dot_general(spread, rows, nt, preferred_element_type=jnp.float32)
        total[...] = part if k == 0 else total[...] + part
    lane = lax.broadcasted_iota(jnp.int32, (SKEL, 2 * F), 1)
    return (chosen[...] + jnp.where(lane < F, 0.0, total[...])).T.astype(jnp.bfloat16)


SKELETON_SCRATCH = [
    pltpu.VMEM((4 * F, SKEL), jnp.bfloat16),
    pltpu.VMEM((SKEL, 2 * F), jnp.float32),
    pltpu.VMEM((SKEL, 2 * F), jnp.float32),
]


def node_kernel(index_ref, merge_ref, leaves_ref, out_ref, right, chosen, total):
    def block_at(k):
        return lambda: leaves_ref[k // 2, :, pl.ds(k % 2 * SKEL, SKEL)]

    index = index_ref[...].astype(jnp.float32)
    out_ref[pl.ds(0, 2 * F), :] = skeleton(index, [block_at(k) for k in range(2 * LEAF_DEV)], right, chosen, total)
    entry = merge_ref[...]
    high = entry // 32
    row = lax.broadcasted_iota(jnp.int32, (16, SKEL), 0)
    packed = jnp.zeros((16, SKEL), jnp.float32)
    for k, line in enumerate((high[:1], entry[:1] - 32 * high[:1], high[1:2], entry[1:2] - 32 * high[1:2])):
        packed = jnp.where(row == k, line.astype(jnp.float32), packed)
    out_ref[pl.ds(2 * F, 16), :] = packed.astype(jnp.bfloat16)


def first_node(index, merge_index, leaves):
    return pl.pallas_call(
        node_kernel,
        out_shape=jax.ShapeDtypeStruct((2 * F + 16, SKEL), jnp.bfloat16),
        in_specs=[VMEM, VMEM, VMEM],
        out_specs=VMEM,
        scratch_shapes=SKELETON_SCRATCH,
        compiler_params=PARAMS,
        name="first_node",
        cost_estimate=COST,
    )(index, merge_index, leaves)


def add_terms(target, block, left_ref, total, right):
    fill_right(right, block)
    weights = block
    base = pl.multiple_of(target * LEAF_PTS, LEAF_PTS)
    for step in range(LEAF_PTS // 256):
        rows = pl.ds(base + step * 256, 256)
        exponent = jnp.dot(left_ref[rows, :], right[...], preferred_element_type=jnp.float32)
        dense = jnp.exp2(exponent).astype(jnp.bfloat16)
        total[rows, :] += lax.dot_general(
            dense, weights, (((1,), (1,)), ((), ())), preferred_element_type=jnp.float32
        )


def far_kernel(place_ref, flags_ref, left_ref, before_ref, nodes_ref, out_ref, siblings, pairs, arrive, right, chosen, total):
    fetch = pltpu.make_async_copy(before_ref, out_ref, arrive)
    fetch.start()
    place = place_ref[0]
    pair = place // 2
    quad = place // 4
    other_pair = pair + 1 - 2 * (pair % 2)
    other_quad = quad + 1 - 2 * (quad % 2)
    siblings[0] = nodes_ref[place + 1 - 2 * (place % 2), pl.ds(0, 2 * F), :]

    def entries(base, level):
        lines = nodes_ref[base, pl.ds(2 * F, 16), :].astype(jnp.float32)
        return lines[2 * level : 2 * level + 1] * 32.0 + lines[2 * level + 1 : 2 * level + 2]

    def merge_pair(k, _):
        base = 2 * jnp.where(k == 0, other_pair, 2 * other_quad + k - 1)
        blocks = [lambda: nodes_ref[base, pl.ds(0, 2 * F), :], lambda: nodes_ref[base + 1, pl.ds(0, 2 * F), :]]
        pairs[k] = skeleton(entries(base, 0), blocks, right, chosen, total)
        return 0

    lax.fori_loop(0, 3, merge_pair, 0)
    siblings[1] = pairs[0]
    siblings[2] = skeleton(entries(4 * other_quad, 1), [lambda: pairs[1], lambda: pairs[2]], right, chosen, total)
    fetch.wait()
    for level in range(LEVELS):
        block = siblings[level]
        fill_right(right, block)

        def leaf_step(leaf, _):
            @pl.when(flags_ref[leaf * LEVELS + level] != 0)
            def _():
                base = pl.multiple_of(leaf * LEAF_PTS, LEAF_PTS)
                for step in range(2):
                    rows = pl.ds(base + step * 512, 512)
                    exponent = jnp.dot(left_ref[rows, :], right[...], preferred_element_type=jnp.float32)
                    dense = jnp.exp2(exponent).astype(jnp.bfloat16)
                    out_ref[rows, :] += lax.dot_general(
                        dense, block, (((1,), (1,)), ((), ())), preferred_element_type=jnp.float32
                    )
            return 0

        lax.fori_loop(0, LEAF_DEV, leaf_step, 0)


def far_terms(place, flags, left, before, nodes):
    return pl.pallas_call(
        far_kernel,
        out_shape=jax.ShapeDtypeStruct((PTS, 2 * F), jnp.float32),
        in_specs=[SMEM, SMEM, VMEM, HBM, VMEM],
        out_specs=VMEM,
        scratch_shapes=[
            pltpu.VMEM((3, 2 * F, SKEL), jnp.bfloat16),
            pltpu.VMEM((3, 2 * F, SKEL), jnp.bfloat16),
            pltpu.SemaphoreType.DMA,
            *SKELETON_SCRATCH,
        ],
        compiler_params=PARAMS,
        name="far_terms",
        cost_estimate=COST,
    )(place, flags, left, before, nodes)


def source_of(me, distance, other):
    core = me % 2
    chip = (me // 2 - (1 - 2 * core) * distance + 8) % 8
    return 2 * chip + (core + other) % 2


def copy_kernel(picks, me_ref, table_ref, *refs):
    inputs, outputs, arrive = refs[: -1 - len(picks)], refs[-1 - len(picks) : -1], refs[-1]
    me = me_ref[0]
    rows = [(out_ref, k, *pick) for out_ref, out in zip(outputs, picks) for k, pick in enumerate(out)]
    copies = [
        pltpu.make_async_copy(inputs[source].at[leaf_of(me, table_ref)], out_ref.at[k], arrive.at[at])
        for at, (out_ref, k, source, leaf_of) in enumerate(rows)
    ]
    for copy in copies:
        copy.start()
    for copy in copies:
        copy.wait()


def copy_leaves(me, table, inputs, picks):
    size = (2 * F, LEAF_PTS)
    return pl.pallas_call(
        functools.partial(copy_kernel, picks),
        out_shape=[jax.ShapeDtypeStruct((len(rows),) + size, jnp.bfloat16) for rows in picks],
        in_specs=[SMEM, SMEM] + [HBM] * len(inputs),
        out_specs=[VMEM] * len(picks),
        scratch_shapes=[pltpu.SemaphoreType.DMA((sum(len(rows) for rows in picks),))],
        compiler_params=PARAMS,
        name="copy_leaves",
        cost_estimate=COST,
    )(me, table, *inputs)


def asked(distance, other, to_chip, to_other):
    def leaf_of(me, table_ref):
        core = me % 2
        chip = (me // 2 + (1 - 2 * core) * to_chip + 8) % 8
        return table_ref[2 * chip + (core + to_other) % 2, 0, source_of(me, distance, other)]

    return leaf_of


def at_slot(slot):
    return lambda me, table_ref: slot


def near_kernel(items, first, last, me_ref, source_ref, target_ref, left_ref, *refs):
    refs = list(refs)
    before_ref = None if first else refs.pop(0)
    count = len(items)
    arrays, out_ref, held, arrive, right = refs[:count], refs[count], refs[count + 1], refs[count + 2], refs[count + 3]
    total = refs[count + 4] if last else out_ref
    plan = []
    for k, ((distance, other, slot), array_ref) in enumerate(zip(items, arrays)):
        peer = source_of(me_ref[0], distance, other)
        leaf = source_ref[peer] if slot is None else slot
        plan.append((target_ref[peer], pltpu.make_async_copy(array_ref.at[leaf], held.at[k], arrive.at[k])))
    for target, copy in plan:
        pl.when(target >= 0)(copy.start)
    total[...] = jnp.zeros_like(total) if first else before_ref[...]
    for k, (target, copy) in enumerate(plan):

        @pl.when(target >= 0)
        def _():
            copy.wait()
            add_terms(target, held[k], left_ref, total, right)

    if last:
        for part in range(8):
            rows = pl.ds(part * 512, 512)
            out_ref[:, rows] = total[rows, :].T[F:]


def near_terms(me, source, target, left, before, items, last=False):
    first = before is None
    plan = [item[1:] for item in items]
    count = len(items)
    scratch = [
        pltpu.VMEM((count, 2 * F, LEAF_PTS), jnp.bfloat16),
        pltpu.SemaphoreType.DMA((count,)),
        pltpu.VMEM((4 * F, LEAF_PTS), jnp.bfloat16),
    ]
    if last:
        scratch.append(pltpu.VMEM((PTS, 2 * F), jnp.float32))
    return pl.pallas_call(
        functools.partial(near_kernel, plan, first, last),
        out_shape=jax.ShapeDtypeStruct((F, PTS) if last else (PTS, 2 * F), jnp.float32),
        in_specs=[SMEM] * 3 + [VMEM] * (1 if first else 2) + [HBM] * count,
        out_specs=VMEM,
        scratch_shapes=scratch,
        compiler_params=PARAMS,
        name="near_terms",
        cost_estimate=COST,
    )(me, source, target, left, *([] if first else [before]), *[item[0] for item in items])


def partner(value, axis, stride):
    pairs = [(source, source ^ 2**stride) for source in range(lax.axis_size(axis))]
    return lax.ppermute(value, axis, pairs)


def hop(value):
    pairs = [(j, (j + 2 - 4 * (j % 2)) % 16) for j in range(16)]
    return lax.ppermute(value, "task", pairs)


def after(value, *others):
    return lax.optimization_barrier((value, *others))[0]


def body(points, weights, point_order, node_order, merge_order, far_list, task_target, task_source):
    me = lax.axis_index("task").astype(jnp.int32).reshape(1)
    source = task_source.reshape(-1)
    target = task_target.reshape(-1)
    near = functools.partial(near_terms, me, source, target)
    place = (lax.axis_index("leaf") % 8).astype(jnp.int32).reshape(1)

    row = jnp.broadcast_to(source, (16, 1, 16))
    table = lax.all_to_all(row, "task", split_axis=0, concat_axis=0, tiled=True)
    leaves = after(sort_leaves(point_order.reshape(-1), points.T, weights.T), table)
    one_a = hop(leaves)
    beside = partner(leaves, "task", 0)
    one_b = hop(beside)
    left = target_factors(after(leaves, beside))
    node = first_node(node_order.reshape(1, -1)[:, :SKEL], merge_order[0, 0, :, :SKEL], after(leaves, beside))
    groups = [list(range(8 * x, 8 * x + 8)) for x in range(lax.axis_size("leaf") // 8)]
    nodes = lax.all_to_all(
        jnp.broadcast_to(node, (8,) + node.shape), "leaf", split_axis=0, concat_axis=0, axis_index_groups=groups, tiled=True
    )

    one_a = after(one_a, node)
    two_a = hop(one_a)
    one_b = after(one_b, one_a)
    two_b = hop(one_b)
    total = near(
        left,
        None,
        [
            (leaves, 0, 0, None),
            (beside, 0, 1, None),
            (one_a, 1, 0, None),
            (one_b, 1, 1, None),
        ],
    )
    two_a = after(two_a, total)
    send, send_side = copy_leaves(
        me,
        table,
        [one_a, one_b, two_a],
        [
            [(2, asked(2, 0, 1, 0)), (2, asked(2, 0, 1, 1)), (2, asked(2, 0, 2, 0))],
            [(0, asked(1, 0, 0, 1)), (1, asked(1, 1, 0, 1)), (2, asked(2, 0, 0, 1))],
        ],
    )
    three_a = hop(send)
    side = partner(send_side, "task", 0)
    two_b = after(two_b, send)
    [send] = copy_leaves(
        me, table, [two_b], [[(0, asked(2, 1, 1, 0)), (0, asked(2, 1, 1, 1)), (0, asked(2, 1, 2, 0))]]
    )
    three_b = hop(send)
    total = far_terms(place, far_list.reshape(-1), left, total, after(nodes, send))
    three_a = after(three_a, total)
    send, send_side = copy_leaves(
        me,
        table,
        [two_b, three_a, three_b],
        [[(1, at_slot(2)), (2, at_slot(2))], [(0, asked(2, 1, 0, 1)), (1, at_slot(1)), (2, at_slot(1))]],
    )
    four = hop(send)
    last_side = partner(send_side, "task", 0)
    total = near(
        left,
        total,
        [
            (after(two_a, send), 2, 0, None),
            (two_b, 2, 1, None),
            (side, -1, 1, 0),
            (side, -1, 0, 1),
            (side, -2, 1, 2),
            (three_a, 3, 0, 0),
            (three_b, 3, 1, 0),
        ],
    )
    last_side = after(last_side, total)
    total = near(
        left,
        total,
        [
            (last_side, -2, 0, 0),
            (last_side, -3, 1, 1),
            (last_side, -3, 0, 2),
            (after(four, last_side), 4, 0, 0),
            (four, 4, 1, 1),
        ],
        last=True,
    )
    return total.T


def solution(mesh):
    return jax.shard_map(
        body,
        mesh=mesh,
        in_specs=(
            P(("leaf", "task"), None),
            P(("leaf", "task"), None),
            P("leaf", "task", None),
            P("leaf", "task", None),
            P("leaf", "task", None, None),
            P("leaf", "task", None, None),
            P("leaf", "task", None, None),
            P("leaf", "task", None, None),
        ),
        out_specs=P(("leaf", "task"), None),
        check_vma=False,
    )
```

```python
import functools
import math

import jax
import jax.numpy as jnp
from jax import lax
from jax.experimental import pallas as pl
from jax.experimental.pallas import tpu as pltpu
from jax.sharding import PartitionSpec as P

LEAF_PTS = 1024
SKEL = 512
LEVELS = 3
LEAF_DEV = 4
F = 64
PTS = LEAF_PTS * LEAF_DEV
RATE = 1.5 / 64 * math.log2(math.e)
VMEM = pl.BlockSpec(memory_space=pltpu.VMEM)
SMEM = pl.BlockSpec(memory_space=pltpu.SMEM)
HBM = pl.BlockSpec(memory_space=pltpu.HBM)
COST = pl.CostEstimate(flops=0, bytes_accessed=1000, transcendentals=0)
PARAMS = pltpu.CompilerParams(vmem_limit_bytes=20 * 2**20)


def split3(value):
    one = value.astype(jnp.bfloat16).astype(jnp.float32)
    rest = value - one
    two = rest.astype(jnp.bfloat16).astype(jnp.float32)
    return one, two, rest - two


def gather_rows(src_ref, index_ref, dst_ref, count, unroll=16):
    def step(i, _):
        for k in range(unroll):
            at = i * unroll + k
            dst_ref[pl.ds(at, 1), :] = src_ref[pl.ds(index_ref[at], 1), :]
        return 0

    lax.fori_loop(0, count // unroll, step, 0)


def sort_kernel(order_ref, points_ref, weights_ref, out_ref, held, arrive, raw, tree):
    copies = []
    for c in range(4):
        cols = pl.ds(c * 1024, 1024)
        for k, array_ref in enumerate((points_ref, weights_ref)):
            into = held.at[pl.ds(k * F, F), cols]
            copies.append(pltpu.make_async_copy(array_ref.at[:, cols], into, arrive.at[2 * c + k]))
    for copy in copies:
        copy.start()
    for c in range(8):
        if c % 2 == 0:
            copies[c].wait()
            copies[c + 1].wait()
        raw[pl.ds(c * 512, 512), :] = held[:, pl.ds(c * 512, 512)].astype(jnp.float32).T
    gather_rows(raw, order_ref, tree, PTS)
    for leaf in range(LEAF_DEV):
        rows = tree[pl.ds(leaf * LEAF_PTS, LEAF_PTS), :]
        out_ref[leaf] = rows.T.astype(jnp.bfloat16)


def sort_leaves(order, points_t, weights_t):
    return pl.pallas_call(
        sort_kernel,
        out_shape=jax.ShapeDtypeStruct((LEAF_DEV, 2 * F, LEAF_PTS), jnp.bfloat16),
        in_specs=[SMEM, HBM, HBM],
        out_specs=VMEM,
        scratch_shapes=[
            pltpu.VMEM((2 * F, PTS), jnp.bfloat16),
            pltpu.SemaphoreType.DMA((8,)),
            pltpu.VMEM((PTS, 2 * F), jnp.float32),
            pltpu.VMEM((PTS, 2 * F), jnp.float32),
        ],
        compiler_params=pltpu.CompilerParams(vmem_limit_bytes=56 * 2**20),
        name="sort_leaves",
        cost_estimate=COST,
    )(order, points_t, weights_t)


def left_factor(rows, with_ones):
    lane = lax.broadcasted_iota(jnp.int32, rows.shape, 1)
    is_point = lane < F
    scaled = jnp.where(is_point, rows * (2 * RATE), 0.0)
    high = scaled.astype(jnp.bfloat16)
    low = scaled - high.astype(jnp.float32)
    norm = -RATE * jnp.sum(jnp.where(is_point, rows * rows, 0.0), axis=1, keepdims=True)
    one, two, three = split3(norm)
    tail = jnp.where(lane == F, one, 0.0)
    tail = jnp.where(lane == F + 1, two, tail)
    tail = jnp.where(lane == F + 2, three, tail)
    if with_ones:
        tail = jnp.where((lane > F + 2) & (lane < F + 6), 1.0, tail)
    second = jnp.where(is_point, low, tail).astype(jnp.bfloat16)
    return jnp.concatenate([high, second], axis=1)


def fill_right(right, block):
    size = block.shape[1]
    points = block[:F]
    wide = points.astype(jnp.float32)
    norm = -RATE * jnp.sum(wide * wide, axis=0, keepdims=True)
    one, two, three = split3(norm)
    row = lax.broadcasted_iota(jnp.int32, (16, size), 0)
    tail = jnp.where(row < 3, 1.0, 0.0)
    tail = jnp.where(row == 3, one, tail)
    tail = jnp.where(row == 4, two, tail)
    tail = jnp.where(row == 5, three, tail)
    right[pl.ds(0, 2 * F), :] = block
    right[pl.ds(2 * F, F), :] = points
    right[pl.ds(3 * F, 16), :] = tail.astype(jnp.bfloat16)
    right[pl.ds(3 * F + 16, F - 16), :] = jnp.zeros((F - 16, size), jnp.bfloat16)


def targets_kernel(leaves_ref, out_ref):
    for leaf in range(LEAF_DEV):
        for half in range(2):
            rows = leaves_ref[leaf, :, pl.ds(half * 512, 512)].astype(jnp.float32).T
            out_ref[pl.ds(leaf * LEAF_PTS + half * 512, 512), :] = left_factor(rows, True)


def target_factors(leaves):
    return pl.pallas_call(
        targets_kernel,
        out_shape=jax.ShapeDtypeStruct((PTS, 4 * F), jnp.bfloat16),
        in_specs=[VMEM],
        out_specs=VMEM,
        compiler_params=PARAMS,
        name="target_factors",
        cost_estimate=COST,
    )(leaves)


def skeleton(index, blocks, right, chosen, total):
    spots = lax.broadcasted_iota(jnp.int32, (SKEL, SKEL), 1).astype(jnp.float32)
    column = jnp.broadcast_to(index, (8, SKEL)).T[:, :1]
    nt = (((1,), (1,)), ((), ()))
    taken = []
    for k, block in enumerate(blocks):
        picks = jnp.where(spots == column - k * SKEL, 1.0, 0.0)
        taken.append(jnp.sum(picks, axis=0, keepdims=True))
        part = lax.dot_general(picks.astype(jnp.bfloat16), block(), nt, preferred_element_type=jnp.float32)
        chosen[...] = part if k == 0 else chosen[...] + part
    left = left_factor(chosen[...], False)
    for k, block in enumerate(blocks):
        rows = block()
        fill_right(right, rows)
        dense = jnp.exp2(jnp.dot(left, right[...], preferred_element_type=jnp.float32))
        factor = jnp.where(taken[k] > 0.5, 0.0, 1.0 / jnp.sum(dense, axis=0, keepdims=True))
        spread = (dense * factor).astype(jnp.bfloat16)
        part = lax.dot_general(spread, rows, nt, preferred_element_type=jnp.float32)
        total[...] = part if k == 0 else total[...] + part
    lane = lax.broadcasted_iota(jnp.int32, (SKEL, 2 * F), 1)
    return (chosen[...] + jnp.where(lane < F, 0.0, total[...])).T.astype(jnp.bfloat16)


SKELETON_SCRATCH = [
    pltpu.VMEM((4 * F, SKEL), jnp.bfloat16),
    pltpu.VMEM((SKEL, 2 * F), jnp.float32),
    pltpu.VMEM((SKEL, 2 * F), jnp.float32),
]


def node_kernel(index_ref, merge_ref, leaves_ref, out_ref, right, chosen, total):
    def block_at(k):
        return lambda: leaves_ref[k // 2, :, pl.ds(k % 2 * SKEL, SKEL)]

    index = index_ref[...].astype(jnp.float32)
    out_ref[pl.ds(0, 2 * F), :] = skeleton(index, [block_at(k) for k in range(2 * LEAF_DEV)], right, chosen, total)
    entry = merge_ref[...]
    high = entry // 32
    row = lax.broadcasted_iota(jnp.int32, (16, SKEL), 0)
    packed = jnp.zeros((16, SKEL), jnp.float32)
    for k, line in enumerate((high[:1], entry[:1] - 32 * high[:1], high[1:2], entry[1:2] - 32 * high[1:2])):
        packed = jnp.where(row == k, line.astype(jnp.float32), packed)
    out_ref[pl.ds(2 * F, 16), :] = packed.astype(jnp.bfloat16)


def first_node(index, merge_index, leaves):
    return pl.pallas_call(
        node_kernel,
        out_shape=jax.ShapeDtypeStruct((2 * F + 16, SKEL), jnp.bfloat16),
        in_specs=[VMEM, VMEM, VMEM],
        out_specs=VMEM,
        scratch_shapes=SKELETON_SCRATCH,
        compiler_params=PARAMS,
        name="first_node",
        cost_estimate=COST,
    )(index, merge_index, leaves)


def add_terms(target, block, left_ref, total, right):
    fill_right(right, block)
    weights = block
    base = pl.multiple_of(target * LEAF_PTS, LEAF_PTS)
    for step in range(LEAF_PTS // 256):
        rows = pl.ds(base + step * 256, 256)
        exponent = jnp.dot(left_ref[rows, :], right[...], preferred_element_type=jnp.float32)
        dense = jnp.exp2(exponent).astype(jnp.bfloat16)
        total[rows, :] += lax.dot_general(
            dense, weights, (((1,), (1,)), ((), ())), preferred_element_type=jnp.float32
        )


def far_kernel(place_ref, flags_ref, left_ref, before_ref, nodes_ref, out_ref, siblings, pairs, arrive, right, chosen, total):
    fetch = pltpu.make_async_copy(before_ref, out_ref, arrive)
    fetch.start()
    place = place_ref[0]
    pair = place // 2
    quad = place // 4
    other_pair = pair + 1 - 2 * (pair % 2)
    other_quad = quad + 1 - 2 * (quad % 2)
    siblings[0] = nodes_ref[place + 1 - 2 * (place % 2), pl.ds(0, 2 * F), :]

    def entries(base, level):
        lines = nodes_ref[base, pl.ds(2 * F, 16), :].astype(jnp.float32)
        return lines[2 * level : 2 * level + 1] * 32.0 + lines[2 * level + 1 : 2 * level + 2]

    def merge_pair(k, _):
        base = 2 * jnp.where(k == 0, other_pair, 2 * other_quad + k - 1)
        blocks = [lambda: nodes_ref[base, pl.ds(0, 2 * F), :], lambda: nodes_ref[base + 1, pl.ds(0, 2 * F), :]]
        pairs[k] = skeleton(entries(base, 0), blocks, right, chosen, total)
        return 0

    lax.fori_loop(0, 3, merge_pair, 0)
    siblings[1] = pairs[0]
    siblings[2] = skeleton(entries(4 * other_quad, 1), [lambda: pairs[1], lambda: pairs[2]], right, chosen, total)
    fetch.wait()
    for level in range(LEVELS):
        block = siblings[level]
        fill_right(right, block)

        def leaf_step(leaf, _):
            @pl.when(flags_ref[leaf * LEVELS + level] != 0)
            def _():
                base = pl.multiple_of(leaf * LEAF_PTS, LEAF_PTS)
                for step in range(2):
                    rows = pl.ds(base + step * 512, 512)
                    exponent = jnp.dot(left_ref[rows, :], right[...], preferred_element_type=jnp.float32)
                    dense = jnp.exp2(exponent).astype(jnp.bfloat16)
                    out_ref[rows, :] += lax.dot_general(
                        dense, block, (((1,), (1,)), ((), ())), preferred_element_type=jnp.float32
                    )
            return 0

        lax.fori_loop(0, LEAF_DEV, leaf_step, 0)


def far_terms(place, flags, left, before, nodes):
    return pl.pallas_call(
        far_kernel,
        out_shape=jax.ShapeDtypeStruct((PTS, 2 * F), jnp.float32),
        in_specs=[SMEM, SMEM, VMEM, HBM, VMEM],
        out_specs=VMEM,
        scratch_shapes=[
            pltpu.VMEM((3, 2 * F, SKEL), jnp.bfloat16),
            pltpu.VMEM((3, 2 * F, SKEL), jnp.bfloat16),
            pltpu.SemaphoreType.DMA,
            *SKELETON_SCRATCH,
        ],
        compiler_params=PARAMS,
        name="far_terms",
        cost_estimate=COST,
    )(place, flags, left, before, nodes)


def source_of(me, distance, other):
    core = me % 2
    chip = (me // 2 - (1 - 2 * core) * distance + 8) % 8
    return 2 * chip + (core + other) % 2


def copy_kernel(picks, me_ref, table_ref, *refs):
    inputs, outputs, arrive = refs[: -1 - len(picks)], refs[-1 - len(picks) : -1], refs[-1]
    me = me_ref[0]
    rows = [(out_ref, k, *pick) for out_ref, out in zip(outputs, picks) for k, pick in enumerate(out)]
    copies = [
        pltpu.make_async_copy(inputs[source].at[leaf_of(me, table_ref)], out_ref.at[k], arrive.at[at])
        for at, (out_ref, k, source, leaf_of) in enumerate(rows)
    ]
    for copy in copies:
        copy.start()
    for copy in copies:
        copy.wait()


def copy_leaves(me, table, inputs, picks):
    size = (2 * F, LEAF_PTS)
    return pl.pallas_call(
        functools.partial(copy_kernel, picks),
        out_shape=[jax.ShapeDtypeStruct((len(rows),) + size, jnp.bfloat16) for rows in picks],
        in_specs=[SMEM, SMEM] + [HBM] * len(inputs),
        out_specs=[VMEM] * len(picks),
        scratch_shapes=[pltpu.SemaphoreType.DMA((sum(len(rows) for rows in picks),))],
        compiler_params=PARAMS,
        name="copy_leaves",
        cost_estimate=COST,
    )(me, table, *inputs)


def asked(distance, other, to_chip, to_other):
    def leaf_of(me, table_ref):
        core = me % 2
        chip = (me // 2 + (1 - 2 * core) * to_chip + 8) % 8
        return table_ref[2 * chip + (core + to_other) % 2, 0, source_of(me, distance, other)]

    return leaf_of


def at_slot(slot):
    return lambda me, table_ref: slot


def near_kernel(items, first, last, me_ref, source_ref, target_ref, left_ref, *refs):
    refs = list(refs)
    before_ref = None if first else refs.pop(0)
    count = len(items)
    arrays, out_ref, held, arrive, right = refs[:count], refs[count], refs[count + 1], refs[count + 2], refs[count + 3]
    total = refs[count + 4] if last else out_ref
    plan = []
    for k, ((distance, other, slot), array_ref) in enumerate(zip(items, arrays)):
        peer = source_of(me_ref[0], distance, other)
        leaf = source_ref[peer] if slot is None else slot
        plan.append((target_ref[peer], pltpu.make_async_copy(array_ref.at[leaf], held.at[k], arrive.at[k])))
    for target, copy in plan:
        pl.when(target >= 0)(copy.start)
    total[...] = jnp.zeros_like(total) if first else before_ref[...]
    for k, (target, copy) in enumerate(plan):

        @pl.when(target >= 0)
        def _():
            copy.wait()
            add_terms(target, held[k], left_ref, total, right)

    if last:
        for part in range(8):
            rows = pl.ds(part * 512, 512)
            out_ref[:, rows] = total[rows, :].T[F:]


def near_terms(me, source, target, left, before, items, last=False):
    first = before is None
    plan = [item[1:] for item in items]
    count = len(items)
    scratch = [
        pltpu.VMEM((count, 2 * F, LEAF_PTS), jnp.bfloat16),
        pltpu.SemaphoreType.DMA((count,)),
        pltpu.VMEM((4 * F, LEAF_PTS), jnp.bfloat16),
    ]
    if last:
        scratch.append(pltpu.VMEM((PTS, 2 * F), jnp.float32))
    return pl.pallas_call(
        functools.partial(near_kernel, plan, first, last),
        out_shape=jax.ShapeDtypeStruct((F, PTS) if last else (PTS, 2 * F), jnp.float32),
        in_specs=[SMEM] * 3 + [VMEM] * (1 if first else 2) + [HBM] * count,
        out_specs=VMEM,
        scratch_shapes=scratch,
        compiler_params=PARAMS,
        name="near_terms",
        cost_estimate=COST,
    )(me, source, target, left, *([] if first else [before]), *[item[0] for item in items])


def partner(value, axis, stride):
    pairs = [(source, source ^ 2**stride) for source in range(lax.axis_size(axis))]
    return lax.ppermute(value, axis, pairs)


def hop(value):
    pairs = [(j, (j + 2 - 4 * (j % 2)) % 16) for j in range(16)]
    return lax.ppermute(value, "task", pairs)


def after(value, *others):
    return lax.optimization_barrier((value, *others))[0]


def body(points, weights, point_order, node_order, merge_order, far_list, task_target, task_source):
    me = lax.axis_index("task").astype(jnp.int32).reshape(1)
    source = task_source.reshape(-1)
    target = task_target.reshape(-1)
    near = functools.partial(near_terms, me, source, target)
    place = (lax.axis_index("leaf") % 8).astype(jnp.int32).reshape(1)

    row = jnp.broadcast_to(source, (16, 1, 16))
    table = lax.all_to_all(row, "task", split_axis=0, concat_axis=0, tiled=True)
    leaves = after(sort_leaves(point_order.reshape(-1), points.T, weights.T), table)
    one_a = hop(leaves)
    beside = partner(leaves, "task", 0)
    one_b = hop(beside)
    left = target_factors(after(leaves, beside))
    node = first_node(node_order.reshape(1, -1)[:, :SKEL], merge_order[0, 0, :, :SKEL], after(leaves, beside))
    groups = [list(range(8 * x, 8 * x + 8)) for x in range(lax.axis_size("leaf") // 8)]
    nodes = lax.all_to_all(
        jnp.broadcast_to(node, (8,) + node.shape), "leaf", split_axis=0, concat_axis=0, axis_index_groups=groups, tiled=True
    )

    one_a = after(one_a, node)
    two_a = hop(one_a)
    one_b = after(one_b, one_a)
    two_b = hop(one_b)
    total = near(
        left,
        None,
        [
            (leaves, 0, 0, None),
            (beside, 0, 1, None),
            (one_a, 1, 0, None),
            (one_b, 1, 1, None),
        ],
    )
    two_a = after(two_a, total)
    [send] = copy_leaves(
        me, table, [two_a], [[(0, asked(2, 0, 1, 0)), (0, asked(2, 0, 1, 1)), (0, asked(2, 0, 2, 0))]]
    )
    three_a = hop(send)
    two_b = after(two_b, send)
    send, send_side = copy_leaves(
        me,
        table,
        [one_a, one_b, two_a, two_b],
        [
            [(3, asked(2, 1, 1, 0)), (3, asked(2, 1, 1, 1)), (3, asked(2, 1, 2, 0))],
            [(0, asked(1, 0, 0, 1)), (1, asked(1, 1, 0, 1)), (2, asked(2, 0, 0, 1)), (3, asked(2, 1, 0, 1))],
        ],
    )
    three_b = hop(send)
    side = partner(send_side, "task", 0)
    total = far_terms(place, far_list.reshape(-1), left, total, after(nodes, send))
    three_a = after(three_a, total)
    send, send_side = copy_leaves(
        me,
        table,
        [three_a, three_b],
        [[(0, at_slot(2)), (1, at_slot(2))], [(0, at_slot(1)), (1, at_slot(1))]],
    )
    four = hop(send)
    last_side = partner(send_side, "task", 0)
    total = near(
        left,
        total,
        [
            (after(two_a, send), 2, 0, None),
            (two_b, 2, 1, None),
            (side, -1, 1, 0),
            (side, -1, 0, 1),
            (side, -2, 1, 2),
            (side, -2, 0, 3),
            (three_a, 3, 0, 0),
            (three_b, 3, 1, 0),
        ],
    )
    four = after(four, total)
    last_side = after(last_side, four)
    total = near(
        left,
        total,
        [
            (four, 4, 0, 0),
            (four, 4, 1, 1),
            (last_side, -3, 1, 0),
            (last_side, -3, 0, 1),
        ],
        last=True,
    )
    return total.T


def solution(mesh):
    return jax.shard_map(
        body,
        mesh=mesh,
        in_specs=(
            P(("leaf", "task"), None),
            P(("leaf", "task"), None),
            P("leaf", "task", None),
            P("leaf", "task", None),
            P("leaf", "task", None, None),
            P("leaf", "task", None, None),
            P("leaf", "task", None, None),
            P("leaf", "task", None, None),
        ),
        out_specs=P(("leaf", "task"), None),
        check_vma=False,
    )
```

```python
import functools
import math

import jax
import jax.numpy as jnp
from jax import lax
from jax.experimental import pallas as pl
from jax.experimental.pallas import tpu as pltpu
from jax.sharding import PartitionSpec as P

LEAF_PTS = 1024
SKEL = 512
LEVELS = 3
LEAF_DEV = 4
F = 64
PTS = LEAF_PTS * LEAF_DEV
RATE = 1.5 / 64 * math.log2(math.e)
VMEM = pl.BlockSpec(memory_space=pltpu.VMEM)
SMEM = pl.BlockSpec(memory_space=pltpu.SMEM)
HBM = pl.BlockSpec(memory_space=pltpu.HBM)
COST = pl.CostEstimate(flops=0, bytes_accessed=1000, transcendentals=0)
PARAMS = pltpu.CompilerParams(vmem_limit_bytes=20 * 2**20)


def split3(value):
    one = value.astype(jnp.bfloat16).astype(jnp.float32)
    rest = value - one
    two = rest.astype(jnp.bfloat16).astype(jnp.float32)
    return one, two, rest - two


def gather_rows(src_ref, index_ref, dst_ref, count, unroll=16):
    def step(i, _):
        for k in range(unroll):
            at = i * unroll + k
            dst_ref[pl.ds(at, 1), :] = src_ref[pl.ds(index_ref[at], 1), :]
        return 0

    lax.fori_loop(0, count // unroll, step, 0)


def sort_kernel(order_ref, points_ref, weights_ref, out_ref, held, arrive, raw, tree):
    copies = []
    for c in range(4):
        cols = pl.ds(c * 1024, 1024)
        for k, array_ref in enumerate((points_ref, weights_ref)):
            into = held.at[pl.ds(k * F, F), cols]
            copies.append(pltpu.make_async_copy(array_ref.at[:, cols], into, arrive.at[2 * c + k]))
    for copy in copies:
        copy.start()
    for c in range(8):
        if c % 2 == 0:
            copies[c].wait()
            copies[c + 1].wait()
        raw[pl.ds(c * 512, 512), :] = held[:, pl.ds(c * 512, 512)].astype(jnp.float32).T
    gather_rows(raw, order_ref, tree, PTS)
    for leaf in range(LEAF_DEV):
        rows = tree[pl.ds(leaf * LEAF_PTS, LEAF_PTS), :]
        out_ref[leaf] = rows.T.astype(jnp.bfloat16)


def sort_leaves(order, points_t, weights_t):
    return pl.pallas_call(
        sort_kernel,
        out_shape=jax.ShapeDtypeStruct((LEAF_DEV, 2 * F, LEAF_PTS), jnp.bfloat16),
        in_specs=[SMEM, HBM, HBM],
        out_specs=VMEM,
        scratch_shapes=[
            pltpu.VMEM((2 * F, PTS), jnp.bfloat16),
            pltpu.SemaphoreType.DMA((8,)),
            pltpu.VMEM((PTS, 2 * F), jnp.float32),
            pltpu.VMEM((PTS, 2 * F), jnp.float32),
        ],
        compiler_params=pltpu.CompilerParams(vmem_limit_bytes=56 * 2**20),
        name="sort_leaves",
        cost_estimate=COST,
    )(order, points_t, weights_t)


def left_factor(rows, with_ones):
    lane = lax.broadcasted_iota(jnp.int32, rows.shape, 1)
    is_point = lane < F
    scaled = jnp.where(is_point, rows * (2 * RATE), 0.0)
    high = scaled.astype(jnp.bfloat16)
    low = scaled - high.astype(jnp.float32)
    norm = -RATE * jnp.sum(jnp.where(is_point, rows * rows, 0.0), axis=1, keepdims=True)
    one, two, three = split3(norm)
    tail = jnp.where(lane == F, one, 0.0)
    tail = jnp.where(lane == F + 1, two, tail)
    tail = jnp.where(lane == F + 2, three, tail)
    if with_ones:
        tail = jnp.where((lane > F + 2) & (lane < F + 6), 1.0, tail)
    second = jnp.where(is_point, low, tail).astype(jnp.bfloat16)
    return jnp.concatenate([high, second], axis=1)


def fill_right(right, block):
    size = block.shape[1]
    points = block[:F]
    wide = points.astype(jnp.float32)
    norm = -RATE * jnp.sum(wide * wide, axis=0, keepdims=True)
    one, two, three = split3(norm)
    row = lax.broadcasted_iota(jnp.int32, (16, size), 0)
    tail = jnp.where(row < 3, 1.0, 0.0)
    tail = jnp.where(row == 3, one, tail)
    tail = jnp.where(row == 4, two, tail)
    tail = jnp.where(row == 5, three, tail)
    right[pl.ds(0, 2 * F), :] = block
    right[pl.ds(2 * F, F), :] = points
    right[pl.ds(3 * F, 16), :] = tail.astype(jnp.bfloat16)
    right[pl.ds(3 * F + 16, F - 16), :] = jnp.zeros((F - 16, size), jnp.bfloat16)


def targets_kernel(leaves_ref, out_ref):
    for leaf in range(LEAF_DEV):
        for half in range(2):
            rows = leaves_ref[leaf, :, pl.ds(half * 512, 512)].astype(jnp.float32).T
            out_ref[pl.ds(leaf * LEAF_PTS + half * 512, 512), :] = left_factor(rows, True)


def target_factors(leaves):
    return pl.pallas_call(
        targets_kernel,
        out_shape=jax.ShapeDtypeStruct((PTS, 4 * F), jnp.bfloat16),
        in_specs=[VMEM],
        out_specs=VMEM,
        compiler_params=PARAMS,
        name="target_factors",
        cost_estimate=COST,
    )(leaves)


def skeleton(index, blocks, right, chosen, total):
    spots = lax.broadcasted_iota(jnp.int32, (SKEL, SKEL), 1).astype(jnp.float32)
    column = jnp.broadcast_to(index, (8, SKEL)).T[:, :1]
    nt = (((1,), (1,)), ((), ()))
    taken = []
    for k, block in enumerate(blocks):
        picks = jnp.where(spots == column - k * SKEL, 1.0, 0.0)
        taken.append(jnp.sum(picks, axis=0, keepdims=True))
        part = lax.dot_general(picks.astype(jnp.bfloat16), block(), nt, preferred_element_type=jnp.float32)
        chosen[...] = part if k == 0 else chosen[...] + part
    left = left_factor(chosen[...], False)
    for k, block in enumerate(blocks):
        rows = block()
        fill_right(right, rows)
        dense = jnp.exp2(jnp.dot(left, right[...], preferred_element_type=jnp.float32))
        factor = jnp.where(taken[k] > 0.5, 0.0, 1.0 / jnp.sum(dense, axis=0, keepdims=True))
        spread = (dense * factor).astype(jnp.bfloat16)
        part = lax.dot_general(spread, rows, nt, preferred_element_type=jnp.float32)
        total[...] = part if k == 0 else total[...] + part
    lane = lax.broadcasted_iota(jnp.int32, (SKEL, 2 * F), 1)
    return (chosen[...] + jnp.where(lane < F, 0.0, total[...])).T.astype(jnp.bfloat16)


SKELETON_SCRATCH = [
    pltpu.VMEM((4 * F, SKEL), jnp.bfloat16),
    pltpu.VMEM((SKEL, 2 * F), jnp.float32),
    pltpu.VMEM((SKEL, 2 * F), jnp.float32),
]


def node_kernel(index_ref, merge_ref, leaves_ref, out_ref, right, chosen, total):
    def block_at(k):
        return lambda: leaves_ref[k // 2, :, pl.ds(k % 2 * SKEL, SKEL)]

    index = index_ref[...].astype(jnp.float32)
    out_ref[pl.ds(0, 2 * F), :] = skeleton(index, [block_at(k) for k in range(2 * LEAF_DEV)], right, chosen, total)
    entry = merge_ref[...]
    high = entry // 32
    row = lax.broadcasted_iota(jnp.int32, (16, SKEL), 0)
    packed = jnp.zeros((16, SKEL), jnp.float32)
    for k, line in enumerate((high[:1], entry[:1] - 32 * high[:1], high[1:2], entry[1:2] - 32 * high[1:2])):
        packed = jnp.where(row == k, line.astype(jnp.float32), packed)
    out_ref[pl.ds(2 * F, 16), :] = packed.astype(jnp.bfloat16)


def first_node(index, merge_index, leaves):
    return pl.pallas_call(
        node_kernel,
        out_shape=jax.ShapeDtypeStruct((2 * F + 16, SKEL), jnp.bfloat16),
        in_specs=[VMEM, VMEM, VMEM],
        out_specs=VMEM,
        scratch_shapes=SKELETON_SCRATCH,
        compiler_params=PARAMS,
        name="first_node",
        cost_estimate=COST,
    )(index, merge_index, leaves)


def add_terms(target, block, left_ref, total, right):
    fill_right(right, block)
    weights = block
    base = pl.multiple_of(target * LEAF_PTS, LEAF_PTS)
    for step in range(LEAF_PTS // 256):
        rows = pl.ds(base + step * 256, 256)
        exponent = jnp.dot(left_ref[rows, :], right[...], preferred_element_type=jnp.float32)
        dense = jnp.exp2(exponent).astype(jnp.bfloat16)
        total[rows, :] += lax.dot_general(
            dense, weights, (((1,), (1,)), ((), ())), preferred_element_type=jnp.float32
        )


def far_kernel(place_ref, flags_ref, left_ref, before_ref, nodes_ref, out_ref, siblings, pairs, arrive, right, chosen, total):
    fetch = pltpu.make_async_copy(before_ref, out_ref, arrive)
    fetch.start()
    place = place_ref[0]
    pair = place // 2
    quad = place // 4
    other_pair = pair + 1 - 2 * (pair % 2)
    other_quad = quad + 1 - 2 * (quad % 2)
    siblings[0] = nodes_ref[place + 1 - 2 * (place % 2), pl.ds(0, 2 * F), :]

    def entries(base, level):
        lines = nodes_ref[base, pl.ds(2 * F, 16), :].astype(jnp.float32)
        return lines[2 * level : 2 * level + 1] * 32.0 + lines[2 * level + 1 : 2 * level + 2]

    def merge_pair(k, _):
        base = 2 * jnp.where(k == 0, other_pair, 2 * other_quad + k - 1)
        blocks = [lambda: nodes_ref[base, pl.ds(0, 2 * F), :], lambda: nodes_ref[base + 1, pl.ds(0, 2 * F), :]]
        pairs[k] = skeleton(entries(base, 0), blocks, right, chosen, total)
        return 0

    lax.fori_loop(0, 3, merge_pair, 0)
    siblings[1] = pairs[0]
    siblings[2] = skeleton(entries(4 * other_quad, 1), [lambda: pairs[1], lambda: pairs[2]], right, chosen, total)
    fetch.wait()
    for level in range(LEVELS):
        block = siblings[level]
        fill_right(right, block)

        def leaf_step(leaf, _):
            @pl.when(flags_ref[leaf * LEVELS + level] != 0)
            def _():
                base = pl.multiple_of(leaf * LEAF_PTS, LEAF_PTS)
                for step in range(2):
                    rows = pl.ds(base + step * 512, 512)
                    exponent = jnp.dot(left_ref[rows, :], right[...], preferred_element_type=jnp.float32)
                    dense = jnp.exp2(exponent).astype(jnp.bfloat16)
                    out_ref[rows, :] += lax.dot_general(
                        dense, block, (((1,), (1,)), ((), ())), preferred_element_type=jnp.float32
                    )
            return 0

        lax.fori_loop(0, LEAF_DEV, leaf_step, 0)


def far_terms(place, flags, left, before, nodes):
    return pl.pallas_call(
        far_kernel,
        out_shape=jax.ShapeDtypeStruct((PTS, 2 * F), jnp.float32),
        in_specs=[SMEM, SMEM, VMEM, HBM, VMEM],
        out_specs=VMEM,
        scratch_shapes=[
            pltpu.VMEM((3, 2 * F, SKEL), jnp.bfloat16),
            pltpu.VMEM((3, 2 * F, SKEL), jnp.bfloat16),
            pltpu.SemaphoreType.DMA,
            *SKELETON_SCRATCH,
        ],
        compiler_params=PARAMS,
        name="far_terms",
        cost_estimate=COST,
    )(place, flags, left, before, nodes)


def source_of(me, distance, other):
    core = me % 2
    chip = (me // 2 - (1 - 2 * core) * distance + 8) % 8
    return 2 * chip + (core + other) % 2


def copy_kernel(picks, me_ref, table_ref, *refs):
    inputs, outputs, arrive = refs[: -1 - len(picks)], refs[-1 - len(picks) : -1], refs[-1]
    me = me_ref[0]
    rows = [(out_ref, k, *pick) for out_ref, out in zip(outputs, picks) for k, pick in enumerate(out)]
    copies = [
        pltpu.make_async_copy(inputs[source].at[leaf_of(me, table_ref)], out_ref.at[k], arrive.at[at])
        for at, (out_ref, k, source, leaf_of) in enumerate(rows)
    ]
    for copy in copies:
        copy.start()
    for copy in copies:
        copy.wait()


def copy_leaves(me, table, inputs, picks):
    size = (2 * F, LEAF_PTS)
    return pl.pallas_call(
        functools.partial(copy_kernel, picks),
        out_shape=[jax.ShapeDtypeStruct((len(rows),) + size, jnp.bfloat16) for rows in picks],
        in_specs=[SMEM, SMEM] + [HBM] * len(inputs),
        out_specs=[VMEM] * len(picks),
        scratch_shapes=[pltpu.SemaphoreType.DMA((sum(len(rows) for rows in picks),))],
        compiler_params=PARAMS,
        name="copy_leaves",
        cost_estimate=COST,
    )(me, table, *inputs)


def asked(distance, other, to_chip, to_other):
    def leaf_of(me, table_ref):
        core = me % 2
        chip = (me // 2 + (1 - 2 * core) * to_chip + 8) % 8
        return table_ref[2 * chip + (core + to_other) % 2, 0, source_of(me, distance, other)]

    return leaf_of


def at_slot(slot):
    return lambda me, table_ref: slot


def near_kernel(items, first, last, me_ref, source_ref, target_ref, left_ref, *refs):
    refs = list(refs)
    before_ref = None if first else refs.pop(0)
    count = len(items)
    arrays, out_ref, held, arrive, right = refs[:count], refs[count], refs[count + 1], refs[count + 2], refs[count + 3]
    total = refs[count + 4] if last else out_ref
    plan = []
    for k, ((distance, other, slot), array_ref) in enumerate(zip(items, arrays)):
        peer = source_of(me_ref[0], distance, other)
        leaf = source_ref[peer] if slot is None else slot
        plan.append((target_ref[peer], pltpu.make_async_copy(array_ref.at[leaf], held.at[k], arrive.at[k])))
    for target, copy in plan:
        pl.when(target >= 0)(copy.start)
    total[...] = jnp.zeros_like(total) if first else before_ref[...]
    for k, (target, copy) in enumerate(plan):

        @pl.when(target >= 0)
        def _():
            copy.wait()
            add_terms(target, held[k], left_ref, total, right)

    if last:
        for part in range(8):
            rows = pl.ds(part * 512, 512)
            out_ref[:, rows] = total[rows, :].T[F:]


def near_terms(me, source, target, left, before, items, last=False):
    first = before is None
    plan = [item[1:] for item in items]
    count = len(items)
    scratch = [
        pltpu.VMEM((count, 2 * F, LEAF_PTS), jnp.bfloat16),
        pltpu.SemaphoreType.DMA((count,)),
        pltpu.VMEM((4 * F, LEAF_PTS), jnp.bfloat16),
    ]
    if last:
        scratch.append(pltpu.VMEM((PTS, 2 * F), jnp.float32))
    return pl.pallas_call(
        functools.partial(near_kernel, plan, first, last),
        out_shape=jax.ShapeDtypeStruct((F, PTS) if last else (PTS, 2 * F), jnp.float32),
        in_specs=[SMEM] * 3 + [VMEM] * (1 if first else 2) + [HBM] * count,
        out_specs=VMEM,
        scratch_shapes=scratch,
        compiler_params=PARAMS,
        name="near_terms",
        cost_estimate=COST,
    )(me, source, target, left, *([] if first else [before]), *[item[0] for item in items])


def partner(value, axis, stride):
    pairs = [(source, source ^ 2**stride) for source in range(lax.axis_size(axis))]
    return lax.ppermute(value, axis, pairs)


def hop(value):
    pairs = [(j, (j + 2 - 4 * (j % 2)) % 16) for j in range(16)]
    return lax.ppermute(value, "task", pairs)


def after(value, *others):
    return lax.optimization_barrier((value, *others))[0]


def body(points, weights, point_order, node_order, merge_order, far_list, task_target, task_source):
    me = lax.axis_index("task").astype(jnp.int32).reshape(1)
    source = task_source.reshape(-1)
    target = task_target.reshape(-1)
    near = functools.partial(near_terms, me, source, target)
    place = (lax.axis_index("leaf") % 8).astype(jnp.int32).reshape(1)

    row = jnp.broadcast_to(source, (16, 1, 16))
    table = lax.all_to_all(row, "task", split_axis=0, concat_axis=0, tiled=True)
    leaves = after(sort_leaves(point_order.reshape(-1), points.T, weights.T), table)
    one_a = hop(leaves)
    beside = partner(leaves, "task", 0)
    one_b = hop(beside)
    left = target_factors(after(leaves, beside))
    node = first_node(node_order.reshape(1, -1)[:, :SKEL], merge_order[0, 0, :, :SKEL], after(leaves, beside))
    groups = [list(range(8 * x, 8 * x + 8)) for x in range(lax.axis_size("leaf") // 8)]
    nodes = lax.all_to_all(
        jnp.broadcast_to(node, (8,) + node.shape), "leaf", split_axis=0, concat_axis=0, axis_index_groups=groups, tiled=True
    )

    one_a = after(one_a, node)
    two_a = hop(one_a)
    one_b = after(one_b, one_a)
    two_b = hop(one_b)
    send_side = copy_leaves(
        me, table, [one_a, after(one_b, left)], [[(0, asked(1, 0, 0, 1)), (1, asked(1, 1, 0, 1))]]
    )
    first_side = partner(send_side[0], "task", 0)
    total = near(
        left,
        None,
        [
            (leaves, 0, 0, None),
            (beside, 0, 1, None),
            (one_a, 1, 0, None),
            (one_b, 1, 1, None),
        ],
    )
    two_a = after(two_a, total)
    [send] = copy_leaves(
        me, table, [two_a], [[(0, asked(2, 0, 1, 0)), (0, asked(2, 0, 1, 1)), (0, asked(2, 0, 2, 0))]]
    )
    three_a = hop(send)
    first_side = after(first_side, send)
    total = near(
        left, total, [(after(two_a, send), 2, 0, None), (first_side, -1, 1, 0), (first_side, -1, 0, 1)]
    )
    two_b = after(two_b, total)
    send, send_side = copy_leaves(
        me,
        table,
        [two_a, two_b],
        [
            [(1, asked(2, 1, 1, 0)), (1, asked(2, 1, 1, 1)), (1, asked(2, 1, 2, 0))],
            [(0, asked(2, 0, 0, 1)), (1, asked(2, 1, 0, 1))],
        ],
    )
    three_b = hop(send)
    side = partner(send_side, "task", 0)
    total = far_terms(place, far_list.reshape(-1), left, total, after(nodes, send))
    three_a = after(three_a, total)
    send, send_side = copy_leaves(
        me,
        table,
        [three_a, three_b],
        [[(0, at_slot(2)), (1, at_slot(2))], [(0, at_slot(1)), (1, at_slot(1))]],
    )
    four = hop(send)
    last_side = partner(send_side, "task", 0)
    total = near(
        left,
        total,
        [
            (after(two_b, send), 2, 1, None),
            (side, -2, 1, 0),
            (side, -2, 0, 1),
            (three_a, 3, 0, 0),
            (three_b, 3, 1, 0),
        ],
    )
    four = after(four, total)
    last_side = after(last_side, four)
    total = near(
        left,
        total,
        [
            (four, 4, 0, 0),
            (four, 4, 1, 1),
            (last_side, -3, 1, 0),
            (last_side, -3, 0, 1),
        ],
        last=True,
    )
    return total.T


def solution(mesh):
    return jax.shard_map(
        body,
        mesh=mesh,
        in_specs=(
            P(("leaf", "task"), None),
            P(("leaf", "task"), None),
            P("leaf", "task", None),
            P("leaf", "task", None),
            P("leaf", "task", None, None),
            P("leaf", "task", None, None),
            P("leaf", "task", None, None),
            P("leaf", "task", None, None),
        ),
        out_specs=P(("leaf", "task"), None),
        check_vma=False,
    )
```

```python
import functools
import math

import jax
import jax.numpy as jnp
from jax import lax
from jax.experimental import pallas as pl
from jax.experimental.pallas import tpu as pltpu
from jax.sharding import PartitionSpec as P

LEAF_PTS = 1024
SKEL = 512
LEVELS = 3
LEAF_DEV = 4
F = 64
PTS = LEAF_PTS * LEAF_DEV
RATE = 1.5 / 64 * math.log2(math.e)
VMEM = pl.BlockSpec(memory_space=pltpu.VMEM)
SMEM = pl.BlockSpec(memory_space=pltpu.SMEM)
HBM = pl.BlockSpec(memory_space=pltpu.HBM)
COST = pl.CostEstimate(flops=0, bytes_accessed=1000, transcendentals=0)
PARAMS = pltpu.CompilerParams(vmem_limit_bytes=20 * 2**20)


def split3(value):
    one = value.astype(jnp.bfloat16).astype(jnp.float32)
    rest = value - one
    two = rest.astype(jnp.bfloat16).astype(jnp.float32)
    return one, two, rest - two


def gather_rows(src_ref, index_ref, dst_ref, count, unroll=16):
    def step(i, _):
        for k in range(unroll):
            at = i * unroll + k
            dst_ref[pl.ds(at, 1), :] = src_ref[pl.ds(index_ref[at], 1), :]
        return 0

    lax.fori_loop(0, count // unroll, step, 0)


def sort_kernel(order_ref, points_ref, weights_ref, out_ref, held, arrive, raw, tree):
    copies = []
    for c in range(4):
        cols = pl.ds(c * 1024, 1024)
        for k, array_ref in enumerate((points_ref, weights_ref)):
            into = held.at[pl.ds(k * F, F), cols]
            copies.append(pltpu.make_async_copy(array_ref.at[:, cols], into, arrive.at[2 * c + k]))
    for copy in copies:
        copy.start()
    for c in range(8):
        if c % 2 == 0:
            copies[c].wait()
            copies[c + 1].wait()
        raw[pl.ds(c * 512, 512), :] = held[:, pl.ds(c * 512, 512)].astype(jnp.float32).T
    gather_rows(raw, order_ref, tree, PTS)
    for leaf in range(LEAF_DEV):
        rows = tree[pl.ds(leaf * LEAF_PTS, LEAF_PTS), :]
        out_ref[leaf] = rows.T.astype(jnp.bfloat16)


def sort_leaves(order, points_t, weights_t):
    return pl.pallas_call(
        sort_kernel,
        out_shape=jax.ShapeDtypeStruct((LEAF_DEV, 2 * F, LEAF_PTS), jnp.bfloat16),
        in_specs=[SMEM, HBM, HBM],
        out_specs=VMEM,
        scratch_shapes=[
            pltpu.VMEM((2 * F, PTS), jnp.bfloat16),
            pltpu.SemaphoreType.DMA((8,)),
            pltpu.VMEM((PTS, 2 * F), jnp.float32),
            pltpu.VMEM((PTS, 2 * F), jnp.float32),
        ],
        compiler_params=pltpu.CompilerParams(vmem_limit_bytes=56 * 2**20),
        name="sort_leaves",
        cost_estimate=COST,
    )(order, points_t, weights_t)


def left_factor(rows, with_ones):
    lane = lax.broadcasted_iota(jnp.int32, rows.shape, 1)
    is_point = lane < F
    scaled = jnp.where(is_point, rows * (2 * RATE), 0.0)
    high = scaled.astype(jnp.bfloat16)
    low = scaled - high.astype(jnp.float32)
    norm = -RATE * jnp.sum(jnp.where(is_point, rows * rows, 0.0), axis=1, keepdims=True)
    one, two, three = split3(norm)
    tail = jnp.where(lane == F, one, 0.0)
    tail = jnp.where(lane == F + 1, two, tail)
    tail = jnp.where(lane == F + 2, three, tail)
    if with_ones:
        tail = jnp.where((lane > F + 2) & (lane < F + 6), 1.0, tail)
    second = jnp.where(is_point, low, tail).astype(jnp.bfloat16)
    return jnp.concatenate([high, second], axis=1)


def fill_right(right, block):
    size = block.shape[1]
    points = block[:F]
    wide = points.astype(jnp.float32)
    norm = -RATE * jnp.sum(wide * wide, axis=0, keepdims=True)
    one, two, three = split3(norm)
    row = lax.broadcasted_iota(jnp.int32, (16, size), 0)
    tail = jnp.where(row < 3, 1.0, 0.0)
    tail = jnp.where(row == 3, one, tail)
    tail = jnp.where(row == 4, two, tail)
    tail = jnp.where(row == 5, three, tail)
    right[pl.ds(0, 2 * F), :] = block
    right[pl.ds(2 * F, F), :] = points
    right[pl.ds(3 * F, 16), :] = tail.astype(jnp.bfloat16)
    right[pl.ds(3 * F + 16, F - 16), :] = jnp.zeros((F - 16, size), jnp.bfloat16)


def targets_kernel(leaves_ref, out_ref):
    for leaf in range(LEAF_DEV):
        for half in range(2):
            rows = leaves_ref[leaf, :, pl.ds(half * 512, 512)].astype(jnp.float32).T
            out_ref[pl.ds(leaf * LEAF_PTS + half * 512, 512), :] = left_factor(rows, True)


def target_factors(leaves):
    return pl.pallas_call(
        targets_kernel,
        out_shape=jax.ShapeDtypeStruct((PTS, 4 * F), jnp.bfloat16),
        in_specs=[VMEM],
        out_specs=VMEM,
        compiler_params=PARAMS,
        name="target_factors",
        cost_estimate=COST,
    )(leaves)


def skeleton(index, blocks, right, chosen, total):
    spots = lax.broadcasted_iota(jnp.int32, (SKEL, SKEL), 1).astype(jnp.float32)
    column = jnp.broadcast_to(index, (8, SKEL)).T[:, :1]
    nt = (((1,), (1,)), ((), ()))
    taken = []
    for k, block in enumerate(blocks):
        picks = jnp.where(spots == column - k * SKEL, 1.0, 0.0)
        taken.append(jnp.sum(picks, axis=0, keepdims=True))
        part = lax.dot_general(picks.astype(jnp.bfloat16), block(), nt, preferred_element_type=jnp.float32)
        chosen[...] = part if k == 0 else chosen[...] + part
    left = left_factor(chosen[...], False)
    for k, block in enumerate(blocks):
        rows = block()
        fill_right(right, rows)
        dense = jnp.exp2(jnp.dot(left, right[...], preferred_element_type=jnp.float32))
        factor = jnp.where(taken[k] > 0.5, 0.0, 1.0 / jnp.sum(dense, axis=0, keepdims=True))
        spread = (dense * factor).astype(jnp.bfloat16)
        part = lax.dot_general(spread, rows, nt, preferred_element_type=jnp.float32)
        total[...] = part if k == 0 else total[...] + part
    lane = lax.broadcasted_iota(jnp.int32, (SKEL, 2 * F), 1)
    return (chosen[...] + jnp.where(lane < F, 0.0, total[...])).T.astype(jnp.bfloat16)


SKELETON_SCRATCH = [
    pltpu.VMEM((4 * F, SKEL), jnp.bfloat16),
    pltpu.VMEM((SKEL, 2 * F), jnp.float32),
    pltpu.VMEM((SKEL, 2 * F), jnp.float32),
]


def node_kernel(index_ref, merge_ref, leaves_ref, out_ref, right, chosen, total):
    def block_at(k):
        return lambda: leaves_ref[k // 2, :, pl.ds(k % 2 * SKEL, SKEL)]

    index = index_ref[...].astype(jnp.float32)
    out_ref[pl.ds(0, 2 * F), :] = skeleton(index, [block_at(k) for k in range(2 * LEAF_DEV)], right, chosen, total)
    entry = merge_ref[...]
    high = entry // 32
    row = lax.broadcasted_iota(jnp.int32, (16, SKEL), 0)
    packed = jnp.zeros((16, SKEL), jnp.float32)
    for k, line in enumerate((high[:1], entry[:1] - 32 * high[:1], high[1:2], entry[1:2] - 32 * high[1:2])):
        packed = jnp.where(row == k, line.astype(jnp.float32), packed)
    out_ref[pl.ds(2 * F, 16), :] = packed.astype(jnp.bfloat16)


def first_node(index, merge_index, leaves):
    return pl.pallas_call(
        node_kernel,
        out_shape=jax.ShapeDtypeStruct((2 * F + 16, SKEL), jnp.bfloat16),
        in_specs=[VMEM, VMEM, VMEM],
        out_specs=VMEM,
        scratch_shapes=SKELETON_SCRATCH,
        compiler_params=PARAMS,
        name="first_node",
        cost_estimate=COST,
    )(index, merge_index, leaves)


def add_terms(target, block, left_ref, total, right):
    fill_right(right, block)
    weights = block
    base = pl.multiple_of(target * LEAF_PTS, LEAF_PTS)
    for step in range(LEAF_PTS // 256):
        rows = pl.ds(base + step * 256, 256)
        exponent = jnp.dot(left_ref[rows, :], right[...], preferred_element_type=jnp.float32)
        dense = jnp.exp2(exponent).astype(jnp.bfloat16)
        total[rows, :] += lax.dot_general(
            dense, weights, (((1,), (1,)), ((), ())), preferred_element_type=jnp.float32
        )


def far_kernel(place_ref, flags_ref, left_ref, before_ref, nodes_ref, out_ref, siblings, pairs, arrive, right, chosen, total):
    fetch = pltpu.make_async_copy(before_ref, out_ref, arrive)
    fetch.start()
    place = place_ref[0]
    pair = place // 2
    quad = place // 4
    other_pair = pair + 1 - 2 * (pair % 2)
    other_quad = quad + 1 - 2 * (quad % 2)
    siblings[0] = nodes_ref[place + 1 - 2 * (place % 2), pl.ds(0, 2 * F), :]

    def entries(base, level):
        lines = nodes_ref[base, pl.ds(2 * F, 16), :].astype(jnp.float32)
        return lines[2 * level : 2 * level + 1] * 32.0 + lines[2 * level + 1 : 2 * level + 2]

    def merge_pair(k, _):
        base = 2 * jnp.where(k == 0, other_pair, 2 * other_quad + k - 1)
        blocks = [lambda: nodes_ref[base, pl.ds(0, 2 * F), :], lambda: nodes_ref[base + 1, pl.ds(0, 2 * F), :]]
        pairs[k] = skeleton(entries(base, 0), blocks, right, chosen, total)
        return 0

    lax.fori_loop(0, 3, merge_pair, 0)
    siblings[1] = pairs[0]
    siblings[2] = skeleton(entries(4 * other_quad, 1), [lambda: pairs[1], lambda: pairs[2]], right, chosen, total)
    fetch.wait()
    for level in range(LEVELS):
        block = siblings[level]
        fill_right(right, block)

        def leaf_step(leaf, _):
            @pl.when(flags_ref[leaf * LEVELS + level] != 0)
            def _():
                base = pl.multiple_of(leaf * LEAF_PTS, LEAF_PTS)
                for step in range(2):
                    rows = pl.ds(base + step * 512, 512)
                    exponent = jnp.dot(left_ref[rows, :], right[...], preferred_element_type=jnp.float32)
                    dense = jnp.exp2(exponent).astype(jnp.bfloat16)
                    out_ref[rows, :] += lax.dot_general(
                        dense, block, (((1,), (1,)), ((), ())), preferred_element_type=jnp.float32
                    )
            return 0

        lax.fori_loop(0, LEAF_DEV, leaf_step, 0)


def far_terms(place, flags, left, before, nodes):
    return pl.pallas_call(
        far_kernel,
        out_shape=jax.ShapeDtypeStruct((PTS, 2 * F), jnp.float32),
        in_specs=[SMEM, SMEM, VMEM, HBM, VMEM],
        out_specs=VMEM,
        scratch_shapes=[
            pltpu.VMEM((3, 2 * F, SKEL), jnp.bfloat16),
            pltpu.VMEM((3, 2 * F, SKEL), jnp.bfloat16),
            pltpu.SemaphoreType.DMA,
            *SKELETON_SCRATCH,
        ],
        compiler_params=PARAMS,
        name="far_terms",
        cost_estimate=COST,
    )(place, flags, left, before, nodes)


def source_of(me, distance, other):
    core = me % 2
    chip = (me // 2 - (1 - 2 * core) * distance + 8) % 8
    return 2 * chip + (core + other) % 2


def copy_kernel(picks, me_ref, table_ref, *refs):
    inputs, outputs, arrive = refs[: -1 - len(picks)], refs[-1 - len(picks) : -1], refs[-1]
    me = me_ref[0]
    rows = [(out_ref, k, *pick) for out_ref, out in zip(outputs, picks) for k, pick in enumerate(out)]
    copies = [
        pltpu.make_async_copy(inputs[source].at[leaf_of(me, table_ref)], out_ref.at[k], arrive.at[at])
        for at, (out_ref, k, source, leaf_of) in enumerate(rows)
    ]
    for copy in copies:
        copy.start()
    for copy in copies:
        copy.wait()


def copy_leaves(me, table, inputs, picks):
    size = (2 * F, LEAF_PTS)
    return pl.pallas_call(
        functools.partial(copy_kernel, picks),
        out_shape=[jax.ShapeDtypeStruct((len(rows),) + size, jnp.bfloat16) for rows in picks],
        in_specs=[SMEM, SMEM] + [HBM] * len(inputs),
        out_specs=[VMEM] * len(picks),
        scratch_shapes=[pltpu.SemaphoreType.DMA((sum(len(rows) for rows in picks),))],
        compiler_params=PARAMS,
        name="copy_leaves",
        cost_estimate=COST,
    )(me, table, *inputs)


def asked(distance, other, to_chip, to_other):
    def leaf_of(me, table_ref):
        core = me % 2
        chip = (me // 2 + (1 - 2 * core) * to_chip + 8) % 8
        return table_ref[2 * chip + (core + to_other) % 2, 0, source_of(me, distance, other)]

    return leaf_of


def at_slot(slot):
    return lambda me, table_ref: slot


def near_kernel(items, first, last, me_ref, source_ref, target_ref, left_ref, *refs):
    refs = list(refs)
    before_ref = None if first else refs.pop(0)
    count = len(items)
    arrays, out_ref, held, arrive, right = refs[:count], refs[count], refs[count + 1], refs[count + 2], refs[count + 3]
    total = refs[count + 4] if last else out_ref
    plan = []
    for k, ((distance, other, slot), array_ref) in enumerate(zip(items, arrays)):
        peer = source_of(me_ref[0], distance, other)
        leaf = source_ref[peer] if slot is None else slot
        plan.append((target_ref[peer], pltpu.make_async_copy(array_ref.at[leaf], held.at[k], arrive.at[k])))
    for target, copy in plan:
        pl.when(target >= 0)(copy.start)
    total[...] = jnp.zeros_like(total) if first else before_ref[...]
    for k, (target, copy) in enumerate(plan):

        @pl.when(target >= 0)
        def _():
            copy.wait()
            add_terms(target, held[k], left_ref, total, right)

    if last:
        for part in range(8):
            rows = pl.ds(part * 512, 512)
            out_ref[:, rows] = total[rows, :].T[F:]


def near_terms(me, source, target, left, before, items, last=False):
    first = before is None
    plan = [item[1:] for item in items]
    count = len(items)
    scratch = [
        pltpu.VMEM((count, 2 * F, LEAF_PTS), jnp.bfloat16),
        pltpu.SemaphoreType.DMA((count,)),
        pltpu.VMEM((4 * F, LEAF_PTS), jnp.bfloat16),
    ]
    if last:
        scratch.append(pltpu.VMEM((PTS, 2 * F), jnp.float32))
    return pl.pallas_call(
        functools.partial(near_kernel, plan, first, last),
        out_shape=jax.ShapeDtypeStruct((F, PTS) if last else (PTS, 2 * F), jnp.float32),
        in_specs=[SMEM] * 3 + [VMEM] * (1 if first else 2) + [HBM] * count,
        out_specs=VMEM,
        scratch_shapes=scratch,
        compiler_params=PARAMS,
        name="near_terms",
        cost_estimate=COST,
    )(me, source, target, left, *([] if first else [before]), *[item[0] for item in items])


def partner(value, axis, stride):
    pairs = [(source, source ^ 2**stride) for source in range(lax.axis_size(axis))]
    return lax.ppermute(value, axis, pairs)


def hop(value):
    pairs = [(j, (j + 2 - 4 * (j % 2)) % 16) for j in range(16)]
    return lax.ppermute(value, "task", pairs)


def after(value, *others):
    return lax.optimization_barrier((value, *others))[0]


def body(points, weights, point_order, node_order, merge_order, far_list, task_target, task_source):
    me = lax.axis_index("task").astype(jnp.int32).reshape(1)
    source = task_source.reshape(-1)
    target = task_target.reshape(-1)
    near = functools.partial(near_terms, me, source, target)
    place = (lax.axis_index("leaf") % 8).astype(jnp.int32).reshape(1)

    row = jnp.broadcast_to(source, (16, 1, 16))
    table = lax.all_to_all(row, "task", split_axis=0, concat_axis=0, tiled=True)
    leaves = after(sort_leaves(point_order.reshape(-1), points.T, weights.T), table)
    one_a = hop(leaves)
    beside = partner(leaves, "task", 0)
    one_b = hop(beside)
    left = target_factors(after(leaves, beside))
    node = first_node(node_order.reshape(1, -1)[:, :SKEL], merge_order[0, 0, :, :SKEL], after(leaves, beside))
    groups = [list(range(8 * x, 8 * x + 8)) for x in range(lax.axis_size("leaf") // 8)]
    nodes = lax.all_to_all(
        jnp.broadcast_to(node, (8,) + node.shape), "leaf", split_axis=0, concat_axis=0, axis_index_groups=groups, tiled=True
    )

    one_a = after(one_a, node)
    two_a = hop(one_a)
    one_b = after(one_b, one_a)
    two_b = hop(one_b)
    send_side = copy_leaves(
        me, table, [one_a, after(one_b, left)], [[(0, asked(1, 0, 0, 1)), (1, asked(1, 1, 0, 1))]]
    )
    first_side = partner(send_side[0], "task", 0)
    total = near(
        left,
        None,
        [
            (leaves, 0, 0, None),
            (beside, 0, 1, None),
            (one_a, 1, 0, None),
            (one_b, 1, 1, None),
        ],
    )
    two_a = after(two_a, total)
    [send] = copy_leaves(
        me, table, [two_a], [[(0, asked(2, 0, 1, 0)), (0, asked(2, 0, 1, 1)), (0, asked(2, 0, 2, 0))]]
    )
    three_a = hop(send)
    first_side = after(first_side, send)
    total = near(
        left, total, [(after(two_a, send), 2, 0, None), (first_side, -1, 1, 0), (first_side, -1, 0, 1)]
    )
    two_b = after(two_b, total)
    send, send_side = copy_leaves(
        me,
        table,
        [two_a, two_b],
        [
            [(1, asked(2, 1, 1, 0)), (1, asked(2, 1, 1, 1)), (1, asked(2, 1, 2, 0))],
            [(0, asked(2, 0, 0, 1)), (1, asked(2, 1, 0, 1))] * 2,
        ],
    )
    three_b = hop(send)
    side = partner(send_side, "task", 0)
    total = far_terms(place, far_list.reshape(-1), left, total, after(nodes, send))
    three_a = after(three_a, total)
    send, send_side = copy_leaves(
        me,
        table,
        [three_a, three_b],
        [[(0, at_slot(2)), (1, at_slot(2))], [(0, at_slot(1)), (1, at_slot(1))]],
    )
    four = hop(send)
    last_side = partner(send_side, "task", 0)
    total = near(
        left,
        total,
        [
            (after(two_b, send), 2, 1, None),
            (side, -2, 1, 0),
            (side, -2, 0, 1),
            (three_a, 3, 0, 0),
            (three_b, 3, 1, 0),
        ],
    )
    four = after(four, total)
    last_side = after(last_side, four)
    total = near(
        left,
        total,
        [
            (four, 4, 0, 0),
            (four, 4, 1, 1),
            (last_side, -3, 1, 0),
            (last_side, -3, 0, 1),
        ],
        last=True,
    )
    return total.T


def solution(mesh):
    return jax.shard_map(
        body,
        mesh=mesh,
        in_specs=(
            P(("leaf", "task"), None),
            P(("leaf", "task"), None),
            P("leaf", "task", None),
            P("leaf", "task", None),
            P("leaf", "task", None, None),
            P("leaf", "task", None, None),
            P("leaf", "task", None, None),
            P("leaf", "task", None, None),
        ),
        out_specs=P(("leaf", "task"), None),
        check_vma=False,
    )
```
